128 devices in a mesh: lat: 16 (over z_hi, y, core), lon: 8 (over x, z_lo).
Axes of the slice: x: 4, y: 4, z: 4 (z_hi: 2, z_lo: 2; z = z_hi * 2 + z_lo), core: 2. Of those that a mesh axis runs over, the one named last changes fastest.
Arguments:
- inputs: bfloat16 [96, 384, 384], P('lat', 'lon'), may hold values from -16 to 16
- cotangent: bfloat16 [96, 384, 384], P('lat', 'lon'), may hold values from -6 to 6
- norm_gains: float32 [2, 2, 192], replicated, may hold values from 0.25 to 1.75
- qkv_weight: bfloat16 [2, 192, 576], replicated, may hold values from -0.4375 to 0.4375
- out_weight: bfloat16 [2, 192, 192], replicated, may hold values from -0.4375 to 0.4375
- up_weight: bfloat16 [2, 192, 768], replicated, may hold values from -0.4375 to 0.4375
- down_weight: bfloat16 [2, 768, 192], replicated, may hold values from -0.21875 to 0.21875
- bias_table: float32 [2, 16, 6, 3312], P(None, 'lat'), may hold values from -3 to 3
Outputs:
- output: bfloat16 [96, 384, 384], P('lat', 'lon')
- grad_inputs: bfloat16 [96, 384, 384], P('lat', 'lon')
- grad_gains: float32 [2, 2, 192], replicated
- grad_qkv: float32 [2, 192, 576], replicated
- grad_out: float32 [2, 192, 192], replicated
- grad_up: float32 [2, 192, 768], replicated
- grad_down: float32 [2, 768, 192], replicated
- grad_table: float32 [2, 16, 6, 3312], P(None, 'lat')
The draws below stay inside these ranges and needn't reach their ends.
All inputs are finite; a program needn't handle non-finite values.
Results may differ from the reference program's by a relative error of at most 0.033.
Values may be sent and summed in bfloat16 or wider, within the bound.
No kernel may reach another device: no remote copies, remote signals or barrier semaphores. Data moves between devices by JAX's collectives and lax.ppermute only.
A program may use at most 128 MiB of HBM per device.

```python
import math
import jax
import jax.numpy as jnp
import numpy as np
from jax import lax

DIM = 192
HEADS = 6
MLP_UNITS = 768
LEVELS = 2
WIN_LAT = 6
WIN_LON = 12
SHIFT_LAT = 3
SHIFT_LON = 6
BLOCKS = 2
WIN_TOK = 144
TYPES = 16
NLAT = 96
NLON = 384
TABLE = 3312


def draw_inputs(key, part):
    key = jax.random.fold_in(key, 7)
    key_base, key_rows, key_cols = jax.random.split(key, 3)
    log_low = math.log(0.3)
    log_high = math.log(3.0)
    row_scale = jnp.exp(jax.random.uniform(key_rows, (NLAT, NLON, 1), jnp.float32, log_low, log_high))
    col_scale = jnp.exp(jax.random.uniform(key_cols, (1, 1, LEVELS * DIM), jnp.float32, log_low, log_high))
    values = jax.random.normal(key_base, (NLAT, NLON, LEVELS * DIM), jnp.float32) * col_scale * row_scale
    return jnp.clip(values, -16.0, 16.0).astype(jnp.bfloat16)


def block_levels(rng, shape, shards, low, high):
    gain, own = 1.0, jax.random.fold_in(rng, 6)
    for position, blocks in shards:
        steps = jnp.exp(jax.random.uniform(jax.random.fold_in(own, position), (blocks,), jnp.float32, low / len(shards), high / len(shards)))
        gain = gain * jnp.repeat(steps, shape[position] // blocks).reshape([-1 if axis == position else 1 for axis in range(len(shape))])
    return gain


def gaussian(stream_key, dims, width, most, cuts=(), dtype=jnp.bfloat16):
    loudness = block_levels(stream_key, dims, cuts, -0.22, 0.18) if cuts else 1.0
    entries = jax.random.normal(stream_key, dims, jnp.float32) * width * loudness
    return jnp.minimum(jnp.maximum(entries, -most), most).astype(dtype)


def setup_inputs(seed: int = 0) -> dict:
    streams_of = jax.random.split(jax.random.key(seed), 9)
    inputs = draw_inputs(jax.random.fold_in(streams_of[8], 71), 0)
    cotangent = gaussian(streams_of[1], (NLAT, NLON, LEVELS * DIM), 1.0, 6.0, ((0, 16), (1, 8)))
    norm_gains = jnp.clip(1.0 + 0.15 * jax.random.normal(streams_of[2], (BLOCKS, 2, DIM), jnp.float32), 0.25, 1.75)
    qkv_weight = gaussian(streams_of[3], (BLOCKS, DIM, 3 * DIM), DIM ** -0.5, 0.4375)
    out_weight = gaussian(streams_of[4], (BLOCKS, DIM, DIM), DIM ** -0.5, 0.4375)
    up_weight = gaussian(streams_of[5], (BLOCKS, DIM, MLP_UNITS), DIM ** -0.5, 0.4375)
    down_weight = gaussian(streams_of[6], (BLOCKS, MLP_UNITS, DIM), MLP_UNITS ** -0.5, 0.21875)
    bias_table = gaussian(streams_of[7], (BLOCKS, TYPES, HEADS, TABLE), 1.0, 3.0, ((1, 16),), jnp.float32)
    return {"inputs": inputs, "cotangent": cotangent, "norm_gains": norm_gains, "qkv_weight": qkv_weight, "out_weight": out_weight, "up_weight": up_weight, "down_weight": down_weight, "bias_table": bias_table}


MASK_VALUE = -100.0
NORM_EPS = 1e-05

def rel_positions():
    token_ids = np.arange(WIN_TOK)
    level_grid = token_ids // (WIN_LAT * WIN_LON)
    row_grid = token_ids // WIN_LON % WIN_LAT
    col_grid = token_ids % WIN_LON
    col_span = 2 * WIN_LON - 1
    table_pos = (level_grid[:, None] + level_grid[None, :] * LEVELS) * (WIN_LAT * WIN_LAT * col_span)
    table_pos = table_pos + (row_grid[:, None] + row_grid[None, :] * WIN_LAT) * col_span
    table_pos = table_pos + col_grid[:, None] - col_grid[None, :] + WIN_LON - 1
    return table_pos.astype(np.int32)

def group_mask():
    upper_rows = np.arange(WIN_TOK) // WIN_LON % WIN_LAT >= WIN_LAT - SHIFT_LAT
    return np.where(upper_rows[:, None] != upper_rows[None, :], MASK_VALUE, 0.0).astype(np.float32)

def keep_rounded(values):
    return lax.optimization_barrier(values)

def to_windows(tokens):
    row_count, col_count = (tokens.shape[0], tokens.shape[1])
    shaped = tokens.reshape(row_count // WIN_LAT, WIN_LAT, col_count // WIN_LON, WIN_LON, LEVELS, DIM)
    shaped = shaped.transpose(0, 2, 4, 1, 3, 5)
    return shaped.reshape(row_count // WIN_LAT, col_count // WIN_LON, WIN_TOK, DIM)

def from_windows(windows):
    lat_wins, lon_wins = (windows.shape[0], windows.shape[1])
    shaped = windows.reshape(lat_wins, lon_wins, LEVELS, WIN_LAT, WIN_LON, DIM)
    shaped = shaped.transpose(0, 3, 1, 4, 2, 5)
    return shaped.reshape(lat_wins * WIN_LAT, lon_wins * WIN_LON, LEVELS * DIM)

def layer_norm(widened, gain_row):
    shaped = widened.reshape(widened.shape[0], widened.shape[1], LEVELS, DIM)
    centre = lax.optimization_barrier(jnp.mean(shaped, axis=-1, keepdims=True))
    spread = lax.optimization_barrier(jnp.mean(jnp.square(shaped - centre), axis=-1, keepdims=True))
    normed = (shaped - centre) * lax.rsqrt(spread + NORM_EPS) * gain_row
    return normed.reshape(widened.shape).astype(jnp.bfloat16)

def prepare_mlp(widened, branch, gain_row):
    hidden_state = widened + branch.astype(jnp.float32)
    return (layer_norm(hidden_state, gain_row), hidden_state)

def activate(pre_act):
    return jax.nn.gelu(pre_act, approximate=False).astype(jnp.bfloat16)

def matmul(left_side, right_side):
    return jnp.dot(left_side, right_side, preferred_element_type=jnp.float32)

def outer_sum(left_side, right_side):
    return lax.dot_general(left_side, right_side, (((0,), (0,)), ((), ())), preferred_element_type=jnp.float32)

def times_transposed(left_side, right_side):
    return lax.dot_general(left_side, right_side, (((1,), (1,)), ((), ())), preferred_element_type=jnp.float32)

def split_heads(projections):
    head_dim = DIM // HEADS
    shaped = keep_rounded(projections).astype(jnp.float32)
    shaped = shaped.reshape(projections.shape[:3] + (3, HEADS, head_dim))
    return (shaped[:, :, :, 0], shaped[:, :, :, 1], shaped[:, :, :, 2])

def attend_forward(projections, bias_full):
    score_scale = 1.0 / math.sqrt(DIM // HEADS)
    queries, key_heads, values = split_heads(projections)
    scores = jnp.einsum('abqhd,abkhd->abhqk', queries, key_heads) * score_scale
    scores = scores + bias_full[:, None]
    weights = jnp.exp(scores)
    soft_weights = weights / lax.optimization_barrier(jnp.sum(weights, axis=-1, keepdims=True))
    rounded = keep_rounded(soft_weights.astype(jnp.bfloat16)).astype(jnp.float32)
    context = jnp.einsum('abhqk,abkhd->abqhd', rounded, values)
    return (context.astype(jnp.bfloat16).reshape(projections.shape[:3] + (DIM,)), soft_weights)

def attend_backward(projections, soft_weights, grad_context):
    head_dim = DIM // HEADS
    score_scale = 1.0 / math.sqrt(head_dim)
    queries, key_heads, values = split_heads(projections)
    grad_heads = keep_rounded(grad_context).astype(jnp.float32).reshape(grad_context.shape[:3] + (HEADS, head_dim))
    rounded = keep_rounded(soft_weights.astype(jnp.bfloat16)).astype(jnp.float32)
    grad_values = jnp.einsum('abhqk,abqhd->abkhd', rounded, grad_heads).astype(jnp.bfloat16)
    grad_probs = jnp.einsum('abqhd,abkhd->abhqk', grad_heads, values)
    grad_scores = soft_weights * (grad_probs - lax.optimization_barrier(jnp.sum(grad_probs * soft_weights, axis=-1, keepdims=True)))
    grad_bias = lax.optimization_barrier(jnp.sum(grad_scores, axis=1))
    scaled = keep_rounded(grad_scores.astype(jnp.bfloat16)).astype(jnp.float32)
    grad_queries = (jnp.einsum('abhqk,abkhd->abqhd', scaled, key_heads) * score_scale).astype(jnp.bfloat16)
    grad_keys = (jnp.einsum('abhqk,abqhd->abkhd', scaled, queries) * score_scale).astype(jnp.bfloat16)
    grad_mixed = jnp.stack([grad_queries, grad_keys, grad_values], axis=3).reshape(projections.shape)
    return (grad_mixed, grad_bias)

def attend_types(projections, bias_full):

    def one_type(triple):
        context, soft_weights = attend_forward(triple[0][None], triple[1][None])
        return context[0]
    return lax.map(one_type, (projections, bias_full))

def attend_types_back(projections, bias_full, grad_context):

    def one_type(triple):
        context, soft_weights = attend_forward(triple[0][None], triple[1][None])
        grad_mixed, grad_bias = attend_backward(triple[0][None], soft_weights, triple[2][None])
        return (grad_mixed[0], grad_bias[0])
    return lax.map(one_type, (projections, bias_full, grad_context))

def table_sum(grad_bias, rel_table):
    lat_wins = grad_bias.shape[0]
    columns = grad_bias.reshape(lat_wins * HEADS, WIN_TOK * WIN_TOK).T
    summed = jax.ops.segment_sum(columns, jnp.asarray(rel_table.reshape(-1)), num_segments=TABLE)
    return summed.T.reshape(lat_wins, HEADS, TABLE)

def block_forward(inputs, gains, qkv_weight, out_weight, up_weight, down_weight, bias_table, shifted):
    rel_table = rel_positions()
    widened = inputs.astype(jnp.float32)
    normed, norm_back = jax.vjp(layer_norm, widened, gains[0])
    if shifted:
        normed = jnp.roll(normed, (-SHIFT_LAT, -SHIFT_LON), (0, 1))
    windows = to_windows(normed)
    flat_in = windows.reshape(-1, DIM)
    projections = matmul(flat_in, qkv_weight).astype(jnp.bfloat16).reshape(windows.shape[:3] + (3 * DIM,))
    mask_flags = (jnp.arange(TYPES) == TYPES - 1).astype(jnp.float32) * (1.0 if shifted else 0.0)
    bias_full = jnp.take(bias_table, rel_table, axis=2) + mask_flags[:, None, None, None] * group_mask()
    context = attend_types(projections, bias_full)
    flat_ctx = context.reshape(-1, DIM)
    branch = from_windows(matmul(flat_ctx, out_weight).astype(jnp.bfloat16).reshape(windows.shape))
    if shifted:
        branch = jnp.roll(branch, (SHIFT_LAT, SHIFT_LON), (0, 1))
    (normed_mlp, hidden_state), mlp_back = jax.vjp(prepare_mlp, widened, branch, gains[1])
    flat_mlp = normed_mlp.reshape(-1, DIM)
    pre_act = matmul(flat_mlp, up_weight)
    expanded, gelu_back = jax.vjp(activate, pre_act)
    output = (hidden_state + matmul(expanded, down_weight).reshape(hidden_state.shape)).astype(jnp.bfloat16)

    def backward(grad_output):
        flat_grad = grad_output.reshape(-1, DIM)
        grad_down = outer_sum(expanded, flat_grad)
        grad_pre = gelu_back(times_transposed(flat_grad, down_weight).astype(jnp.bfloat16))[0].astype(jnp.bfloat16)
        grad_up = outer_sum(flat_mlp, grad_pre)
        grad_normed = times_transposed(grad_pre, up_weight).astype(jnp.bfloat16).reshape(normed_mlp.shape)
        grad_wide, grad_branch, grad_gain_mlp = mlp_back((grad_normed, grad_output.astype(jnp.float32)))
        if shifted:
            grad_branch = jnp.roll(grad_branch, (-SHIFT_LAT, -SHIFT_LON), (0, 1))
        grad_proj_in = to_windows(grad_branch).reshape(-1, DIM)
        grad_out = outer_sum(flat_ctx, grad_proj_in)
        grad_context = times_transposed(grad_proj_in, out_weight).astype(jnp.bfloat16).reshape(context.shape)
        grad_mixed, grad_bias = attend_types_back(projections, bias_full, grad_context)
        grad_table = table_sum(grad_bias, rel_table)
        flat_gm = grad_mixed.reshape(-1, 3 * DIM)
        grad_qkv = outer_sum(flat_in, flat_gm)
        grad_windows = times_transposed(flat_gm, qkv_weight).astype(jnp.bfloat16).reshape(windows.shape)
        grad_attn_in = from_windows(grad_windows)
        if shifted:
            grad_attn_in = jnp.roll(grad_attn_in, (SHIFT_LAT, SHIFT_LON), (0, 1))
        grad_first, grad_gain_attn = norm_back(grad_attn_in)
        grad_inputs = (grad_first + grad_wide).astype(jnp.bfloat16)
        stacked_gains = jnp.stack([grad_gain_attn, grad_gain_mlp])
        return (grad_inputs, (stacked_gains, grad_qkv, grad_out, grad_up, grad_down, grad_table))
    return (output, backward)

def reference(inputs, cotangent, norm_gains, qkv_weight, out_weight, up_weight, down_weight, bias_table):
    first_out, first_back = block_forward(inputs, norm_gains[0], qkv_weight[0], out_weight[0], up_weight[0], down_weight[0], bias_table[0], False)
    output, last_back = block_forward(first_out, norm_gains[1], qkv_weight[1], out_weight[1], up_weight[1], down_weight[1], bias_table[1], True)
    grad_middle, last_grads = last_back(cotangent)
    grad_inputs, first_grads = first_back(grad_middle)
    stacked = [jnp.stack([first_part, last_part]) for first_part, last_part in zip(first_grads, last_grads)]
    return (output, grad_inputs, stacked[0], stacked[1], stacked[2], stacked[3], stacked[4], stacked[5])
```

```python
import math

import jax
import jax.numpy as jnp
import numpy as np
from jax import lax
from jax.experimental import pallas as pl
from jax.experimental.pallas import tpu as pltpu
from jax.sharding import PartitionSpec as P

DIM = 192
HEADS = 6
HEAD_DIM = 32
UNITS = 768
ROWS = 6
COLS = 48
WIN_COLS = 12
WINDOWS = 4
WIN_TOK = 144
TOKENS = 576
GRID = ROWS * COLS
GROUP = 12
SPAN = 23
WIDE = SPAN * GROUP
QLANES = HEADS * WIN_TOK
STRIP = 32
SOURCE = 288 + 2 * STRIP
NORM_EPS = 1e-05
MASK_VALUE = -100.0
LOG2E = math.log2(math.e)
SCALE = 1.0 / math.sqrt(HEAD_DIM)
WBLOCK = 18 * DIM

F32 = jnp.float32
BF16 = jnp.bfloat16


def token_places():
    t = np.arange(TOKENS)
    w, rest = t // WIN_TOK, t % WIN_TOK
    c, l, r = rest // GROUP, rest % GROUP // ROWS, rest % ROWS
    return r, w * WIN_COLS + c, l


def one_hot(places, size):
    return (places[:, None] == np.arange(size)[None, :]).astype(np.float32)


def grid_picker():
    r, j, _ = token_places()
    return one_hot(r * COLS + j, GRID)


def shifted_picker():
    r, j, _ = token_places()
    half = np.where(r < 3, r, r - 3)
    inner = np.where(r < 3, 0, 144) + half * COLS + j + 6
    edge = np.where(r < 3, 288, 288 + STRIP) + half * 6 + j - 42
    return one_hot(np.where(j < 42, inner, edge), SOURCE)


def returned_picker():
    r, j, _ = token_places()
    half = np.where(r >= 3, r - 3, r)
    inner = np.where(r >= 3, 0, 144) + half * COLS + j
    edge = np.where(r >= 3, 288, 288 + STRIP) + half * 6 + j
    return one_hot(np.where(j >= 6, inner, edge), SOURCE)


def strip_picker():
    picked = np.zeros((2 * STRIP, GRID), np.float32)
    for i in range(3):
        for j in range(6):
            picked[i * 6 + j, (i + 3) * COLS + j] = 1
            picked[STRIP + i * 6 + j, i * COLS + j] = 1
    return picked


def table_rows():
    picked = np.zeros((2, HEADS * 16, HEADS * 24), np.float32)
    for h in range(HEADS):
        for lq in range(2):
            for lp in range(2):
                for rq in range(6):
                    picked[lp, h * 16 + lq * 6 + rq, ((h * 2 + lq) * 2 + lp) * 6 + rq] = 1
    return picked


def table_cols():
    picked = np.zeros((2, 6 * SPAN, WIDE), np.float32)
    for lp in range(2):
        for rp in range(6):
            for d in range(SPAN):
                picked[lp, rp * SPAN + d, d * GROUP + lp * 6 + rp] = 1
    return picked


def nn(a, b):
    return jnp.dot(a, b, preferred_element_type=F32)


def nt(a, b):
    return lax.dot_general(a, b, (((1,), (1,)), ((), ())), preferred_element_type=F32)


def tn(a, b):
    return lax.dot_general(a, b, (((0,), (0,)), ((), ())), preferred_element_type=F32)


def level_mask():
    t = lax.broadcasted_iota(jnp.int32, (TOKENS, DIM), 0)
    return (lax.div(t, 6) & 1) == 1


def gather_tokens(picker, source):
    both = nn(picker, source)
    return jnp.where(level_mask(), both[:, DIM:], both[:, :DIM])


def scatter_tokens(picker, tokens):
    upper = level_mask()
    zero = jnp.zeros_like(tokens)
    both = jnp.concatenate([jnp.where(upper, zero, tokens), jnp.where(upper, tokens, zero)], axis=1)
    return tn(picker, both.astype(BF16))


def normalize(x):
    centre = jnp.mean(x, axis=-1, keepdims=True)
    off = x - centre
    spread = jnp.mean(off * off, axis=-1, keepdims=True)
    inv = lax.rsqrt(spread + NORM_EPS)
    return off * inv, inv


def norm_backward(grad, gain, hat, inv):
    scaled = grad * gain
    mean_one = jnp.mean(scaled, axis=-1, keepdims=True)
    mean_two = jnp.mean(scaled * hat, axis=-1, keepdims=True)
    return inv * (scaled - mean_one - hat * mean_two)


def gelu_parts(x):
    bell = jnp.exp2(x * x * (-0.5 * LOG2E))
    t = 1.0 / (1.0 + (0.3275911 * math.sqrt(0.5)) * jnp.abs(x))
    poly = t * (0.254829592 + t * (-0.284496736 + t * (1.421413741 + t * (-1.453152027 + t * 1.061405429))))
    tail = 0.5 * poly * bell
    below = jnp.where(x >= 0, 1.0 - tail, tail)
    return below, bell * (1.0 / math.sqrt(2.0 * math.pi))


def head_rows():
    lane = lax.div(lax.broadcasted_iota(jnp.int32, (1, DIM), 1), HEAD_DIM)
    return [(lane == h) for h in range(HEADS)]


def stack_heads(x, masks):
    return jnp.concatenate([jnp.where(m, x, jnp.zeros_like(x)) for m in masks], axis=0)


def fold_heads(x, masks):
    folded = x[:WIN_TOK]
    for h in range(1, HEADS):
        folded = jnp.where(masks[h], x[h * WIN_TOK : (h + 1) * WIN_TOK], folded)
    return folded


def expand_table(table_ref, trows_ref, tcols_ref, bias_ref):
    table = table_ref[...] * LOG2E
    high = table.astype(BF16)
    low = (table - high.astype(F32)).astype(BF16)
    wide = jnp.zeros((HEADS * 16, WIDE), F32)
    for lp in range(2):
        for part in (high, low):
            wide += nn(nn(trows_ref[lp], part).astype(BF16), tcols_ref[lp])
    for cq in range(WIN_COLS):
        start = GROUP * (WIN_COLS - 1 - cq)
        row = jnp.concatenate(
            [wide[h * 16 : h * 16 + GROUP, start : start + WIN_TOK] for h in range(HEADS)], axis=1
        )
        bias_ref[cq * GROUP : (cq + 1) * GROUP, :] = row


def add_mask(bias_ref, flag):
    key = lax.broadcasted_iota(jnp.int32, (WIN_TOK, 1), 0)
    query = lax.broadcasted_iota(jnp.int32, (1, QLANES), 1)
    key_up = (lax.div(key, 3) & 1).astype(F32)
    query_up = (lax.div(query, 3) & 1).astype(F32)
    apart = jnp.abs(key_up - query_up)
    bias_ref[...] += apart * (flag * (MASK_VALUE * LOG2E))


def collapse_table(grad_ref, trows_ref, tcols_ref):
    parts = []
    for h in range(HEADS):
        total = None
        for cq in range(WIN_COLS):
            start = GROUP * (WIN_COLS - 1 - cq)
            piece = grad_ref[cq * GROUP : (cq + 1) * GROUP, h * WIN_TOK : (h + 1) * WIN_TOK]
            pads = [jnp.zeros((GROUP, start), F32)] if start else []
            tail = WIDE - start - WIN_TOK
            pads_after = [jnp.zeros((GROUP, tail), F32)] if tail else []
            piece = jnp.concatenate(pads + [piece] + pads_after, axis=1)
            total = piece if total is None else total + piece
        parts.append(jnp.concatenate([total, jnp.zeros((16 - GROUP, WIDE), F32)], axis=0))
    wide = jnp.concatenate(parts, axis=0).astype(BF16)
    result = jnp.zeros((HEADS * 24, 6 * SPAN), F32)
    for lp in range(2):
        narrow = nt(wide, tcols_ref[lp]).astype(BF16)
        result += tn(trows_ref[lp], narrow)
    return result


def attention(q_ref, k_ref, v_ref, bias_ref, probs_ref, ctx_ref, masks):
    for w in range(WINDOWS):
        rows = pl.ds(w * WIN_TOK, WIN_TOK)
        stacked = stack_heads(q_ref[rows, :], masks)
        scores = nt(k_ref[rows, :], stacked) * (SCALE * LOG2E) + bias_ref[...]
        weights = jnp.exp2(scores)
        inverse = 1.0 / jnp.sum(weights, axis=0, keepdims=True)
        probs = (weights * inverse).astype(BF16)
        probs_ref[w] = probs
        ctx_ref[rows, :] = fold_heads(tn(probs, v_ref[rows, :]), masks).astype(BF16)


def attention_back(q_ref, k_ref, v_ref, probs_ref, gctx_ref, dq_ref, dk_ref, dv_ref, grad_ref, masks):
    for w in range(WINDOWS):
        rows = pl.ds(w * WIN_TOK, WIN_TOK)
        stacked_g = stack_heads(gctx_ref[rows, :], masks)
        stacked_q = stack_heads(q_ref[rows, :], masks)
        probs_half = probs_ref[w]
        probs = probs_half.astype(F32)
        grad_probs = nt(v_ref[rows, :], stacked_g)
        inner = jnp.sum(grad_probs * probs, axis=0, keepdims=True)
        grad_scores = probs * (grad_probs - inner)
        if w == 0:
            grad_ref[...] = grad_scores
        else:
            grad_ref[...] += grad_scores
        half = grad_scores.astype(BF16)
        dv_ref[rows, :] = nn(probs_half, stacked_g).astype(BF16)
        dk_ref[rows, :] = (nn(half, stacked_q) * SCALE).astype(BF16)
        dq_ref[rows, :] = (fold_heads(tn(half, k_ref[rows, :]), masks) * SCALE).astype(BF16)


def project(normed, qkv_ref, q_ref, k_ref, v_ref):
    for i, ref in enumerate((q_ref, k_ref, v_ref)):
        ref[...] = nn(normed, qkv_ref[:, i * DIM : (i + 1) * DIM]).astype(BF16)


def put_weights(wbuf_ref, offset, value):
    tiles = value.shape[1] // 128
    for j in range(tiles):
        wbuf_ref[(offset + j) * DIM : (offset + j + 1) * DIM, :] = value[:, j * 128 : (j + 1) * 128].astype(BF16)


def weight_grads(wbuf_ref, normed, dq, dk, dv, ctx, gbranch, normed_mlp, gpre_ref, expanded_ref, g):
    for j in range(3):
        cols = slice(j * 256, (j + 1) * 256)
        put_weights(wbuf_ref, 2 * j, tn(normed_mlp, gpre_ref[:, cols]))
        put_weights(wbuf_ref, 6 + 2 * j, tn(g, expanded_ref[:, cols]))
    put_weights(wbuf_ref, 12, tn(normed, jnp.concatenate([dq, dk], axis=1)))
    put_weights(wbuf_ref, 15, jnp.concatenate([tn(normed, dv), tn(ctx, gbranch)], axis=1))


def attention_backward_part(
    x, gain, qkv_ref, out_ref, ghid, q_ref, k_ref, v_ref, probs_ref, ctx_ref, gctx_ref, dq_ref, dk_ref, dv_ref, grad_ref, masks
):
    gbranch = ghid.astype(BF16)
    gctx_ref[...] = nt(gbranch, out_ref[...]).astype(BF16)
    attention_back(q_ref, k_ref, v_ref, probs_ref, gctx_ref, dq_ref, dk_ref, dv_ref, grad_ref, masks)
    gnormed = nt(dq_ref[...], qkv_ref[:, :DIM])
    gnormed += nt(dk_ref[...], qkv_ref[:, DIM : 2 * DIM])
    gnormed += nt(dv_ref[...], qkv_ref[:, 2 * DIM :])
    gnormed = gnormed.astype(BF16).astype(F32)
    hat, inv = normalize(x)
    gain_grad = jnp.sum(gnormed * hat, axis=0, keepdims=True)
    gblock = norm_backward(gnormed, gain, hat, inv) + ghid
    normed = (hat * gain).astype(BF16)
    return gblock, normed, gbranch, gain_grad


def first_forward(
    x_ref, cot_ref, gains_ref, qkv_ref, out_ref, up_ref, down_ref, table_ref, trows_ref, tcols_ref, pick_ref, strips_ref,
    xw_ref, q_ref, k_ref, v_ref, probs_ref, ctx_ref, hidden_ref, expanded_ref, slope_ref, grid_ref, edges_ref, cot_edges_ref,
    bias_ref,
):
    masks = head_rows()
    cot_edges_ref[...] = nn(strips_ref[...], cot_ref[...]).astype(BF16)
    x = gather_tokens(pick_ref[...], x_ref[...])
    xw_ref[...] = x.astype(BF16)
    hat, _ = normalize(x)
    normed = (hat * gains_ref[0:1, :]).astype(BF16)
    project(normed, qkv_ref, q_ref, k_ref, v_ref)
    expand_table(table_ref, trows_ref, tcols_ref, bias_ref)
    attention(q_ref, k_ref, v_ref, bias_ref, probs_ref, ctx_ref, masks)
    branch = nn(ctx_ref[...], out_ref[...]).astype(BF16)
    hidden = xw_ref[...].astype(F32) + branch.astype(F32)
    hidden_ref[...] = hidden
    hat, _ = normalize(hidden)
    normed_mlp = (hat * gains_ref[1:2, :]).astype(BF16)
    total = hidden
    for j in range(3):
        cols = slice(j * 256, (j + 1) * 256)
        pre = nn(normed_mlp, up_ref[:, cols])
        below, density = gelu_parts(pre)
        expanded = (pre * below).astype(BF16)
        expanded_ref[:, cols] = expanded
        slope_ref[:, cols] = (below + pre * density).astype(BF16)
        total = total + nn(expanded, down_ref[cols, :])
    grid = scatter_tokens(pick_ref[...], total.astype(BF16)).astype(BF16)
    grid_ref[...] = grid
    edges_ref[...] = nn(strips_ref[...], grid).astype(BF16)


def second_both(
    flag_ref, grid_ref, above_ref, edges_ref, cot_ref, cot_above_ref, cot_edges_ref,
    gains_ref, qkv_ref, out_ref, up_ref, down_ref, table_ref, trows_ref, tcols_ref, pick_ref,
    y_ref, back_ref, wbuf_ref, gain_grad_ref, table_grad_ref,
    source_ref, x_ref, q_ref, k_ref, v_ref, probs_ref, ctx_ref, bias_ref, gctx_ref, dq_ref, dk_ref, dv_ref, gpre_ref, expanded_ref,
):
    masks = head_rows()

    def assemble(grid, above, edges):
        source_ref[0:144, :] = grid[144:288, :]
        source_ref[144:288, :] = above[...]
        source_ref[288:SOURCE, :] = edges[...]
        return gather_tokens(pick_ref[...], source_ref[...])

    x_ref[...] = assemble(grid_ref, above_ref, edges_ref)
    hat, _ = normalize(x_ref[...])
    normed = (hat * gains_ref[0:1, :]).astype(BF16)
    project(normed, qkv_ref, q_ref, k_ref, v_ref)
    expand_table(table_ref, trows_ref, tcols_ref, bias_ref)
    add_mask(bias_ref, flag_ref[0])
    attention(q_ref, k_ref, v_ref, bias_ref, probs_ref, ctx_ref, masks)
    branch = nn(ctx_ref[...], out_ref[...]).astype(BF16)
    hidden = x_ref[...] + branch.astype(F32)
    hat_mlp, inv_mlp = normalize(hidden)
    normed_mlp = (hat_mlp * gains_ref[1:2, :]).astype(BF16)
    g32 = assemble(cot_ref, cot_above_ref, cot_edges_ref)
    g = g32.astype(BF16)
    total = hidden
    gnormed = jnp.zeros((TOKENS, DIM), F32)
    for j in range(3):
        cols = slice(j * 256, (j + 1) * 256)
        pre = nn(normed_mlp, up_ref[:, cols])
        below, density = gelu_parts(pre)
        expanded = (pre * below).astype(BF16)
        expanded_ref[:, cols] = expanded
        total = total + nn(expanded, down_ref[cols, :])
        gact = nt(g, down_ref[cols, :]).astype(BF16).astype(F32)
        gpre = ((below + pre * density) * gact).astype(BF16)
        gpre_ref[:, cols] = gpre
        gnormed = gnormed + nt(gpre, up_ref[:, cols])
    y_ref[...] = scatter_tokens(pick_ref[...], total.astype(BF16)).astype(BF16)
    gnormed = gnormed.astype(BF16).astype(F32)
    gain_grad_ref[1:2, :] = jnp.sum(gnormed * hat_mlp, axis=0, keepdims=True)
    ghid = g32 + norm_backward(gnormed, gains_ref[1:2, :], hat_mlp, inv_mlp)
    gblock, normed, gbranch, gain_grad = attention_backward_part(
        x_ref[...], gains_ref[0:1, :], qkv_ref, out_ref, ghid,
        q_ref, k_ref, v_ref, probs_ref, ctx_ref, gctx_ref, dq_ref, dk_ref, dv_ref, bias_ref, masks,
    )
    gain_grad_ref[0:1, :] = gain_grad
    back_ref[...] = scatter_tokens(pick_ref[...], gblock.astype(BF16)).astype(BF16)
    weight_grads(
        wbuf_ref, normed, dq_ref[...], dk_ref[...], dv_ref[...], ctx_ref[...], gbranch, normed_mlp, gpre_ref, expanded_ref, g
    )
    table_grad_ref[...] = collapse_table(bias_ref, trows_ref, tcols_ref).astype(BF16)


def first_backward(
    back_ref, above_ref, edges_ref, xw_ref, q_ref, k_ref, v_ref, probs_ref, ctx_ref, hidden_ref, expanded_ref, slope_ref,
    gains_ref, qkv_ref, out_ref, up_ref, down_ref, trows_ref, tcols_ref, pick_ref, returned_ref,
    gin_ref, wbuf_ref, gain_grad_ref, table_grad_ref,
    source_ref, gctx_ref, dq_ref, dk_ref, dv_ref, gpre_ref, grad_ref,
):
    masks = head_rows()
    source_ref[0:144, :] = back_ref[0:144, :]
    source_ref[144:288, :] = above_ref[...]
    source_ref[288:SOURCE, :] = edges_ref[...]
    g32 = gather_tokens(returned_ref[...], source_ref[...])
    g = g32.astype(BF16)
    hat_mlp, inv_mlp = normalize(hidden_ref[...])
    normed_mlp = (hat_mlp * gains_ref[1:2, :]).astype(BF16)
    gnormed = jnp.zeros((TOKENS, DIM), F32)
    for j in range(3):
        cols = slice(j * 256, (j + 1) * 256)
        gact = nt(g, down_ref[cols, :]).astype(BF16).astype(F32)
        gpre = (slope_ref[:, cols].astype(F32) * gact).astype(BF16)
        gpre_ref[:, cols] = gpre
        gnormed = gnormed + nt(gpre, up_ref[:, cols])
    gnormed = gnormed.astype(BF16).astype(F32)
    gain_grad_ref[1:2, :] = jnp.sum(gnormed * hat_mlp, axis=0, keepdims=True)
    ghid = g32 + norm_backward(gnormed, gains_ref[1:2, :], hat_mlp, inv_mlp)
    gblock, normed, gbranch, gain_grad = attention_backward_part(
        xw_ref[...].astype(F32), gains_ref[0:1, :], qkv_ref, out_ref, ghid,
        q_ref, k_ref, v_ref, probs_ref, ctx_ref, gctx_ref, dq_ref, dk_ref, dv_ref, grad_ref, masks,
    )
    gain_grad_ref[0:1, :] = gain_grad
    gin_ref[...] = scatter_tokens(pick_ref[...], gblock.astype(BF16)).astype(BF16)
    weight_grads(
        wbuf_ref, normed, dq_ref[...], dk_ref[...], dv_ref[...], ctx_ref[...], gbranch, normed_mlp, gpre_ref, expanded_ref, g
    )
    table_grad_ref[...] = collapse_table(grad_ref, trows_ref, tcols_ref).astype(BF16)


def whole(array):
    return pl.BlockSpec(array.shape, lambda i: (0,) * array.ndim)


def picked(array, index):
    rest = array.shape[1:]
    return pl.BlockSpec((None,) + rest, lambda i: (index,) + (0,) * len(rest))


def call(kernel, operands, specs, outs, scratch):
    shapes = [jax.ShapeDtypeStruct(shape, dtype) for shape, dtype in outs]
    return pl.pallas_call(
        kernel,
        grid=(1,),
        out_shape=shapes,
        in_specs=specs,
        out_specs=[whole(s) for s in shapes],
        scratch_shapes=[pltpu.VMEM(shape, dtype) for shape, dtype in scratch],
        compiler_params=pltpu.CompilerParams(vmem_limit_bytes=56 * 1024 * 1024),
    )(*operands)


def neighbour(axes, sizes, steps):
    pairs = []
    for a in range(sizes[0]):
        for b in range(sizes[1]):
            source = ((a + steps[0]) % sizes[0]) * sizes[1] + (b + steps[1]) % sizes[1]
            pairs.append((source, a * sizes[1] + b))
    return pairs


def exchange(rows, edges, sizes, step):
    both = ("lat", "lon")
    above = lax.ppermute(rows, both, neighbour(both, sizes, (step, 0)))
    side = lax.ppermute(edges[:STRIP], both, neighbour(both, sizes, (0, step)))
    corner = lax.ppermute(edges[STRIP:], both, neighbour(both, sizes, (step, step)))
    return above, jnp.concatenate([side, corner], axis=0)


def total_sum(wbuf_first, wbuf_last, gains_first, gains_last):
    gains = jnp.concatenate([gains_first, gains_last]).reshape(-1).astype(BF16)
    flat = jnp.concatenate([wbuf_first, wbuf_last, jnp.pad(gains, (0, 256 * 128 - 768)).reshape(256, 128)])
    parts = lax.all_to_all(flat.reshape(128, 56, 128), ("lat", "lon"), 0, 0, tiled=False)
    mine = jnp.sum(parts.astype(F32), axis=0).astype(BF16)
    spread = jnp.broadcast_to(mine[None], (128, 56, 128))
    full = lax.all_to_all(spread, ("lat", "lon"), 0, 0, tiled=False)
    return full.reshape(128 * 56, 128)


def on_device(sizes, inputs, cotangent, norm_gains, qkv_weight, out_weight, up_weight, down_weight, bias_table):
    x = inputs.reshape(GRID, 2 * DIM)
    cot = cotangent.reshape(GRID, 2 * DIM)
    tables = bias_table.reshape(2, HEADS * 24, 6 * SPAN)
    trows, tcols = jnp.asarray(table_rows(), BF16), jnp.asarray(table_cols(), BF16)
    pick_grid, pick_shift, pick_back = (
        jnp.asarray(m, BF16) for m in (grid_picker(), shifted_picker(), returned_picker())
    )
    strips = jnp.asarray(strip_picker(), BF16)
    last = (lax.axis_index("lat") == sizes[0] - 1).astype(F32).reshape(1)
    weights = (norm_gains, qkv_weight, out_weight, up_weight, down_weight)
    tok = (TOKENS, DIM)

    operands = [x, cot, *weights, tables, trows, tcols, pick_grid, strips]
    specs = [whole(x), whole(cot)] + [picked(a, 0) for a in (*weights, tables)]
    specs += [whole(a) for a in (trows, tcols, pick_grid, strips)]
    outs = [(tok, BF16), (tok, BF16), (tok, BF16), (tok, BF16), ((WINDOWS, WIN_TOK, QLANES), BF16), (tok, BF16), (tok, F32)]
    outs += [((TOKENS, UNITS), BF16), ((TOKENS, UNITS), BF16), ((GRID, 2 * DIM), BF16), ((2 * STRIP, 2 * DIM), BF16)]
    outs += [((2 * STRIP, 2 * DIM), BF16)]
    results = call(first_forward, operands, specs, outs, [((WIN_TOK, QLANES), F32)])
    saved, grid, edges, cot_edges = results[:9], results[9], results[10], results[11]

    above, edges = exchange(grid[:144], edges, sizes, 1)
    cot_above, cot_edges = exchange(cot[:144], cot_edges, sizes, 1)

    operands = [last, grid, above, edges, cot, cot_above, cot_edges, *weights, tables, trows, tcols, pick_shift]
    specs = [pl.BlockSpec(memory_space=pltpu.SMEM)]
    specs += [whole(a) for a in (grid, above, edges, cot, cot_above, cot_edges)]
    specs += [picked(a, 1) for a in (*weights, tables)] + [whole(a) for a in (trows, tcols, pick_shift)]
    src = (SOURCE, 2 * DIM)
    outs = [(src, BF16), (src, BF16), ((WBLOCK, 128), BF16), ((2, DIM), F32), ((HEADS * 24, 6 * SPAN), BF16)]
    scratch = [(src, BF16), (tok, F32), (tok, BF16), (tok, BF16), (tok, BF16), ((WINDOWS, WIN_TOK, QLANES), BF16), (tok, BF16)]
    scratch += [((WIN_TOK, QLANES), F32)] + [(tok, BF16)] * 4 + [((TOKENS, UNITS), BF16)] * 2
    y_src, back, wbuf_last, gains_last, table_last = call(second_both, operands, specs, outs, scratch)

    back_above, back_edges = exchange(back[144:288], back[288:], sizes, -1)
    operands = [back, back_above, back_edges, *saved, *weights, trows, tcols, pick_grid, pick_back]
    specs = [whole(a) for a in (back, back_above, back_edges, *saved)] + [picked(a, 0) for a in weights]
    specs += [whole(a) for a in (trows, tcols, pick_grid, pick_back)]
    outs = [((GRID, 2 * DIM), BF16), ((WBLOCK, 128), BF16), ((2, DIM), F32), ((HEADS * 24, 6 * SPAN), BF16)]
    scratch = [(src, BF16)] + [(tok, BF16)] * 4 + [((TOKENS, UNITS), BF16), ((WIN_TOK, QLANES), F32)]
    grad_inputs, wbuf_first, gains_first, table_first = call(first_backward, operands, specs, outs, scratch)

    y_above, y_edges = exchange(y_src[144:288], y_src[288:], sizes, -1)
    rows = jnp.concatenate([y_above, y_src[:144]]).reshape(ROWS, COLS, 2 * DIM)
    corner = y_edges[STRIP : STRIP + 18].reshape(3, 6, 2 * DIM)
    side = y_edges[:18].reshape(3, 6, 2 * DIM)
    output = jnp.concatenate([jnp.concatenate([corner, side]), rows[:, 6:]], axis=1)

    full = total_sum(wbuf_first, wbuf_last, gains_first, gains_last)
    weight_part = full[: 2 * WBLOCK].reshape(2, 18, DIM, 128).transpose(0, 2, 1, 3).reshape(2, DIM, 18 * 128).astype(F32)
    grad_up = weight_part[:, :, :UNITS]
    grad_down = weight_part[:, :, UNITS : 2 * UNITS].transpose(0, 2, 1)
    grad_qkv = weight_part[:, :, 2 * UNITS : 2 * UNITS + 3 * DIM]
    grad_out = weight_part[:, :, 2 * UNITS + 3 * DIM :]
    grad_gains = full[2 * WBLOCK : 2 * WBLOCK + 6].reshape(2, 2, DIM).astype(F32)
    table_terms = jnp.stack([table_first, table_last]).reshape(2, 1, HEADS, 24 * 6 * SPAN)
    grad_table = lax.psum(table_terms, "lon").astype(F32)
    return (output, grad_inputs.reshape(ROWS, COLS, 2 * DIM), grad_gains, grad_qkv, grad_out, grad_up, grad_down, grad_table)


def solution(mesh):
    sizes = (mesh.shape["lat"], mesh.shape["lon"])

    def program(*arguments):
        return on_device(sizes, *arguments)

    fields, tables = P("lat", "lon", None), P(None, "lat", None, None)
    return jax.shard_map(
        program,
        mesh=mesh,
        in_specs=(fields, fields, P(), P(), P(), P(), P(), tables),
        out_specs=(fields, fields, P(), P(), P(), P(), P(), tables),
        check_vma=False,
    )
```

```python
import math

import jax
import jax.numpy as jnp
import numpy as np
from jax import lax
from jax.experimental import pallas as pl
from jax.experimental.pallas import tpu as pltpu
from jax.sharding import PartitionSpec as P

DIM = 192
HEADS = 6
HEAD_DIM = 32
UNITS = 768
ROWS = 6
COLS = 48
WIN_COLS = 12
WINDOWS = 4
WIN_TOK = 144
TOKENS = 576
GRID = ROWS * COLS
GROUP = 12
SPAN = 23
WIDE = SPAN * GROUP
CELL = 6 * SPAN
TABLE = 24 * CELL
QLANES = HEADS * WIN_TOK
STRIP = 32
SOURCE = 288 + 2 * STRIP
NORM_EPS = 1e-05
MASK_VALUE = -100.0
LOG2E = math.log2(math.e)
SCALE = 1.0 / math.sqrt(HEAD_DIM)
WBLOCK = 18 * DIM
CHUNK = 448
HALF = 8 * CHUNK
TCHUNK = 64
TROWS = 208

F32 = jnp.float32
BF16 = jnp.bfloat16


def token_places():
    t = np.arange(TOKENS)
    w, rest = t // WIN_TOK, t % WIN_TOK
    c, l, r = rest // GROUP, rest % GROUP // ROWS, rest % ROWS
    return r, w * WIN_COLS + c, l


def one_hot(places, size):
    return (places[:, None] == np.arange(size)[None, :]).astype(np.float32)


def grid_picker():
    r, j, _ = token_places()
    return one_hot(r * COLS + j, GRID)


def shifted_picker():
    r, j, _ = token_places()
    half = np.where(r < 3, r, r - 3)
    inner = np.where(r < 3, 0, 144) + half * COLS + j + 6
    edge = np.where(r < 3, 288, 288 + STRIP) + half * 6 + j - 42
    return one_hot(np.where(j < 42, inner, edge), SOURCE)


def returned_picker():
    r, j, _ = token_places()
    half = np.where(r >= 3, r - 3, r)
    inner = np.where(r >= 3, 0, 144) + half * COLS + j
    edge = np.where(r >= 3, 288, 288 + STRIP) + half * 6 + j
    return one_hot(np.where(j >= 6, inner, edge), SOURCE)


def strip_picker():
    picked = np.zeros((2 * STRIP, GRID), np.float32)
    for i in range(3):
        for j in range(6):
            picked[i * 6 + j, (i + 3) * COLS + j] = 1
            picked[STRIP + i * 6 + j, i * COLS + j] = 1
    return picked


def table_rows():
    picked = np.zeros((2, HEADS * 16, 24 * 8), np.float32)
    for h in range(HEADS):
        for lq in range(2):
            for lp in range(2):
                for rq in range(6):
                    picked[lp, h * 16 + lq * 6 + rq, (lq * 12 + lp * 6 + rq) * 8 + h] = 1
    return picked


def table_cols():
    picked = np.zeros((2, 6 * SPAN, WIDE), np.float32)
    for lp in range(2):
        for rp in range(6):
            for d in range(SPAN):
                picked[lp, rp * SPAN + d, d * GROUP + lp * 6 + rp] = 1
    return picked


def nn(a, b):
    return jnp.dot(a, b, preferred_element_type=F32)


def nt(a, b):
    return lax.dot_general(a, b, (((1,), (1,)), ((), ())), preferred_element_type=F32)


def tn(a, b):
    return lax.dot_general(a, b, (((0,), (0,)), ((), ())), preferred_element_type=F32)


def level_mask():
    t = lax.broadcasted_iota(jnp.int32, (TOKENS, DIM), 0)
    return (lax.div(t, 6) & 1) == 1


def gather_tokens(picker, source):
    both = nn(picker, source)
    return jnp.where(level_mask(), both[:, DIM:], both[:, :DIM])


def scatter_tokens(picker, tokens):
    upper = level_mask()
    zero = jnp.zeros_like(tokens)
    both = jnp.concatenate([jnp.where(upper, zero, tokens), jnp.where(upper, tokens, zero)], axis=1)
    return tn(picker, both.astype(BF16))


def normalize(x):
    centre = jnp.mean(x, axis=-1, keepdims=True)
    off = x - centre
    spread = jnp.mean(off * off, axis=-1, keepdims=True)
    inv = lax.rsqrt(spread + NORM_EPS)
    return off * inv, inv


def norm_backward(grad, gain, hat, inv):
    scaled = grad * gain
    mean_one = jnp.mean(scaled, axis=-1, keepdims=True)
    mean_two = jnp.mean(scaled * hat, axis=-1, keepdims=True)
    return inv * (scaled - mean_one - hat * mean_two)


def gelu_parts(x):
    bell = jnp.exp2(x * x * (-0.5 * LOG2E))
    t = 1.0 / (1.0 + (0.3275911 * math.sqrt(0.5)) * jnp.abs(x))
    poly = t * (0.254829592 + t * (-0.284496736 + t * (1.421413741 + t * (-1.453152027 + t * 1.061405429))))
    tail = 0.5 * poly * bell
    below = jnp.where(x >= 0, 1.0 - tail, tail)
    return below, bell * (1.0 / math.sqrt(2.0 * math.pi))


def head_rows():
    lane = lax.div(lax.broadcasted_iota(jnp.int32, (1, DIM), 1), HEAD_DIM)
    return [(lane == h) for h in range(HEADS)]


def stack_heads(x, masks):
    return jnp.concatenate([jnp.where(m, x, jnp.zeros_like(x)) for m in masks], axis=0)


def fold_heads(x, masks):
    folded = x[:WIN_TOK]
    for h in range(1, HEADS):
        folded = jnp.where(masks[h], x[h * WIN_TOK : (h + 1) * WIN_TOK], folded)
    return folded


def expand_table(table_ref, trows_ref, tcols_ref, bias_ref):
    table = jnp.concatenate([table_ref[...] * LOG2E, jnp.zeros((2, TABLE), F32)], axis=0)
    table = jnp.concatenate([table[:, k * CELL : (k + 1) * CELL] for k in range(24)], axis=0)
    high = table.astype(BF16)
    low = (table - high.astype(F32)).astype(BF16)
    wide = jnp.zeros((HEADS * 16, WIDE), F32)
    for lp in range(2):
        for part in (high, low):
            wide += nn(nn(trows_ref[lp], part).astype(BF16), tcols_ref[lp])
    for cq in range(WIN_COLS):
        start = GROUP * (WIN_COLS - 1 - cq)
        row = jnp.concatenate(
            [wide[h * 16 : h * 16 + GROUP, start : start + WIN_TOK] for h in range(HEADS)], axis=1
        )
        bias_ref[cq * GROUP : (cq + 1) * GROUP, :] = row


def add_mask(bias_ref, flag):
    key = lax.broadcasted_iota(jnp.int32, (WIN_TOK, 1), 0)
    query = lax.broadcasted_iota(jnp.int32, (1, QLANES), 1)
    key_up = (lax.div(key, 3) & 1).astype(F32)
    query_up = (lax.div(query, 3) & 1).astype(F32)
    apart = jnp.abs(key_up - query_up)
    bias_ref[...] += apart * (flag * (MASK_VALUE * LOG2E))


def collapse_table(grad_ref, trows_ref, tcols_ref):
    parts = []
    for h in range(HEADS):
        total = None
        for cq in range(WIN_COLS):
            start = GROUP * (WIN_COLS - 1 - cq)
            piece = grad_ref[cq * GROUP : (cq + 1) * GROUP, h * WIN_TOK : (h + 1) * WIN_TOK]
            pads = [jnp.zeros((GROUP, start), F32)] if start else []
            tail = WIDE - start - WIN_TOK
            pads_after = [jnp.zeros((GROUP, tail), F32)] if tail else []
            piece = jnp.concatenate(pads + [piece] + pads_after, axis=1)
            total = piece if total is None else total + piece
        parts.append(jnp.concatenate([total, jnp.zeros((16 - GROUP, WIDE), F32)], axis=0))
    wide = jnp.concatenate(parts, axis=0).astype(BF16)
    result = jnp.zeros((24 * 8, CELL), F32)
    for lp in range(2):
        narrow = nt(wide, tcols_ref[lp]).astype(BF16)
        result += tn(trows_ref[lp], narrow)
    cells = [result[k * 8 : (k + 1) * 8] for k in range(24)] + [jnp.zeros((8, 26 * 128 - TABLE), F32)]
    flat = jnp.concatenate(cells, axis=1)
    return jnp.concatenate([flat[:, j * 128 : (j + 1) * 128] for j in range(26)], axis=0).astype(BF16)


def attention(q_ref, k_ref, v_ref, bias_ref, probs_ref, ctx_ref, masks):
    for w in range(WINDOWS):
        rows = pl.ds(w * WIN_TOK, WIN_TOK)
        stacked = stack_heads(q_ref[rows, :], masks)
        scores = nt(k_ref[rows, :], stacked) * (SCALE * LOG2E) + bias_ref[...]
        weights = jnp.exp2(scores)
        inverse = 1.0 / jnp.sum(weights, axis=0, keepdims=True)
        probs = (weights * inverse).astype(BF16)
        probs_ref[w] = probs
        ctx_ref[rows, :] = fold_heads(tn(probs, v_ref[rows, :]), masks).astype(BF16)


def attention_back(q_ref, k_ref, v_ref, probs_ref, gctx_ref, dq_ref, dk_ref, dv_ref, grad_ref, masks):
    for w in range(WINDOWS):
        rows = pl.ds(w * WIN_TOK, WIN_TOK)
        stacked_g = stack_heads(gctx_ref[rows, :], masks)
        stacked_q = stack_heads(q_ref[rows, :], masks)
        probs_half = probs_ref[w]
        probs = probs_half.astype(F32)
        grad_probs = nt(v_ref[rows, :], stacked_g)
        inner = jnp.sum(grad_probs * probs, axis=0, keepdims=True)
        grad_scores = probs * (grad_probs - inner)
        if w == 0:
            grad_ref[...] = grad_scores
        else:
            grad_ref[...] += grad_scores
        half = grad_scores.astype(BF16)
        dv_ref[rows, :] = nn(probs_half, stacked_g).astype(BF16)
        dk_ref[rows, :] = (nn(half, stacked_q) * SCALE).astype(BF16)
        dq_ref[rows, :] = (fold_heads(tn(half, k_ref[rows, :]), masks) * SCALE).astype(BF16)


def project(normed, qkv_ref, q_ref, k_ref, v_ref):
    for i, ref in enumerate((q_ref, k_ref, v_ref)):
        ref[...] = nn(normed, qkv_ref[:, i * DIM : (i + 1) * DIM]).astype(BF16)


def put_weights(wbuf_ref, offset, value):
    tiles = value.shape[1] // 128
    for j in range(tiles):
        wbuf_ref[(offset + j) * DIM : (offset + j + 1) * DIM, :] = value[:, j * 128 : (j + 1) * 128].astype(BF16)


def weight_grads(wbuf_ref, normed, dq, dk, dv, ctx, gbranch, normed_mlp, gpre_ref, expanded_ref, g):
    for j in range(3):
        cols = slice(j * 256, (j + 1) * 256)
        put_weights(wbuf_ref, 2 * j, tn(normed_mlp, gpre_ref[:, cols]))
        put_weights(wbuf_ref, 6 + 2 * j, tn(g, expanded_ref[:, cols]))
    put_weights(wbuf_ref, 12, tn(normed, jnp.concatenate([dq, dk], axis=1)))
    put_weights(wbuf_ref, 15, jnp.concatenate([tn(normed, dv), tn(ctx, gbranch)], axis=1))


def attention_backward_part(
    x, gain, qkv_ref, out_ref, ghid, q_ref, k_ref, v_ref, probs_ref, ctx_ref, gctx_ref, dq_ref, dk_ref, dv_ref, grad_ref, masks
):
    gbranch = ghid.astype(BF16)
    gctx_ref[...] = nt(gbranch, out_ref[...]).astype(BF16)
    attention_back(q_ref, k_ref, v_ref, probs_ref, gctx_ref, dq_ref, dk_ref, dv_ref, grad_ref, masks)
    gnormed = nt(dq_ref[...], qkv_ref[:, :DIM])
    gnormed += nt(dk_ref[...], qkv_ref[:, DIM : 2 * DIM])
    gnormed += nt(dv_ref[...], qkv_ref[:, 2 * DIM :])
    gnormed = gnormed.astype(BF16).astype(F32)
    hat, inv = normalize(x)
    gain_grad = jnp.sum(gnormed * hat, axis=0, keepdims=True)
    gblock = norm_backward(gnormed, gain, hat, inv) + ghid
    normed = (hat * gain).astype(BF16)
    return gblock, normed, gbranch, gain_grad


def first_forward(
    x_ref, gains_ref, qkv_ref, out_ref, up_ref, down_ref, table_ref, trows_ref, tcols_ref, pick_ref, strips_ref,
    xw_ref, q_ref, k_ref, v_ref, probs_ref, ctx_ref, hidden_ref, expanded_ref, slope_ref, top_ref, bottom_ref, side_ref, corner_ref,
    bias_ref,
):
    masks = head_rows()
    x = gather_tokens(pick_ref[...], x_ref[...])
    xw_ref[...] = x.astype(BF16)
    hat, _ = normalize(x)
    normed = (hat * gains_ref[0:1, :]).astype(BF16)
    project(normed, qkv_ref, q_ref, k_ref, v_ref)
    expand_table(table_ref, trows_ref, tcols_ref, bias_ref)
    attention(q_ref, k_ref, v_ref, bias_ref, probs_ref, ctx_ref, masks)
    branch = nn(ctx_ref[...], out_ref[...]).astype(BF16)
    hidden = xw_ref[...].astype(F32) + branch.astype(F32)
    hidden_ref[...] = hidden
    hat, _ = normalize(hidden)
    normed_mlp = (hat * gains_ref[1:2, :]).astype(BF16)
    total = hidden
    for j in range(3):
        cols = slice(j * 256, (j + 1) * 256)
        pre = nn(normed_mlp, up_ref[:, cols])
        below, density = gelu_parts(pre)
        expanded = (pre * below).astype(BF16)
        expanded_ref[:, cols] = expanded
        slope_ref[:, cols] = (below + pre * density).astype(BF16)
        total = total + nt(expanded, down_ref[:, cols])
    grid = scatter_tokens(pick_ref[...], total.astype(BF16)).astype(BF16)
    top_ref[...] = grid[:144]
    bottom_ref[...] = grid[144:]
    edges = nn(strips_ref[...], grid).astype(BF16)
    side_ref[...] = edges[:STRIP]
    corner_ref[...] = edges[STRIP:]


def fill_source(source_ref, own, above_ref, side_ref, corner_ref):
    source_ref[0:144, :] = own
    source_ref[144:288, :] = above_ref[...]
    source_ref[288:SOURCE, :] = jnp.zeros((2 * STRIP, 2 * DIM), BF16)
    source_ref[288 : 288 + side_ref.shape[0], :] = side_ref[...]
    source_ref[288 + STRIP : 288 + STRIP + corner_ref.shape[0], :] = corner_ref[...]


def put_source(own_ref, row_ref, side_ref, corner_ref, value):
    own_ref[...] = value[0:144]
    row_ref[...] = value[144:288]
    side_ref[...] = value[288 : 288 + STRIP]
    corner_ref[...] = value[288 + STRIP :]


def second_both(
    own_ref, above_ref, side_ref, corner_ref, cot_ref, cot_above_ref, cot_side_ref, cot_corner_ref,
    gains_ref, qkv_ref, out_ref, up_ref, down_ref, table_ref, trows_ref, tcols_ref, pick_ref,
    y_own_ref, y_row_ref, y_side_ref, y_corner_ref, back_own_ref, back_row_ref, back_side_ref, back_corner_ref,
    wbuf_ref, gain_grad_ref, table_grad_ref,
    source_ref, x_ref, q_ref, k_ref, v_ref, probs_ref, ctx_ref, bias_ref, gctx_ref, dq_ref, dk_ref, dv_ref, gpre_ref, expanded_ref,
):
    masks = head_rows()

    fill_source(source_ref, own_ref[...], above_ref, side_ref, corner_ref)
    x_ref[...] = gather_tokens(pick_ref[...], source_ref[...])
    hat, _ = normalize(x_ref[...])
    normed = (hat * gains_ref[0:1, :]).astype(BF16)
    project(normed, qkv_ref, q_ref, k_ref, v_ref)
    expand_table(table_ref, trows_ref, tcols_ref, bias_ref)
    add_mask(bias_ref, (lax.axis_index("lat") == lax.axis_size("lat") - 1).astype(F32))
    attention(q_ref, k_ref, v_ref, bias_ref, probs_ref, ctx_ref, masks)
    branch = nn(ctx_ref[...], out_ref[...]).astype(BF16)
    hidden = x_ref[...] + branch.astype(F32)
    hat_mlp, inv_mlp = normalize(hidden)
    normed_mlp = (hat_mlp * gains_ref[1:2, :]).astype(BF16)
    fill_source(source_ref, cot_ref[144:288, :], cot_above_ref, cot_side_ref, cot_corner_ref)
    g32 = gather_tokens(pick_ref[...], source_ref[...])
    g = g32.astype(BF16)
    total = hidden
    gnormed = jnp.zeros((TOKENS, DIM), F32)
    for j in range(3):
        cols = slice(j * 256, (j + 1) * 256)
        pre = nn(normed_mlp, up_ref[:, cols])
        below, density = gelu_parts(pre)
        expanded = (pre * below).astype(BF16)
        expanded_ref[:, cols] = expanded
        total = total + nt(expanded, down_ref[:, cols])
        gact = nn(g, down_ref[:, cols]).astype(BF16).astype(F32)
        gpre = ((below + pre * density) * gact).astype(BF16)
        gpre_ref[:, cols] = gpre
        gnormed = gnormed + nt(gpre, up_ref[:, cols])
    y = scatter_tokens(pick_ref[...], total.astype(BF16)).astype(BF16)
    put_source(y_own_ref, y_row_ref, y_side_ref, y_corner_ref, y)
    gnormed = gnormed.astype(BF16).astype(F32)
    gain_grad_ref[1:2, :] = jnp.sum(gnormed * hat_mlp, axis=0, keepdims=True)
    ghid = g32 + norm_backward(gnormed, gains_ref[1:2, :], hat_mlp, inv_mlp)
    gblock, normed, gbranch, gain_grad = attention_backward_part(
        x_ref[...], gains_ref[0:1, :], qkv_ref, out_ref, ghid,
        q_ref, k_ref, v_ref, probs_ref, ctx_ref, gctx_ref, dq_ref, dk_ref, dv_ref, bias_ref, masks,
    )
    gain_grad_ref[0:1, :] = gain_grad
    back = scatter_tokens(pick_ref[...], gblock.astype(BF16)).astype(BF16)
    put_source(back_own_ref, back_row_ref, back_side_ref, back_corner_ref, back)
    weight_grads(
        wbuf_ref, normed, dq_ref[...], dk_ref[...], dv_ref[...], ctx_ref[...], gbranch, normed_mlp, gpre_ref, expanded_ref, g
    )
    table_grad_ref[...] = collapse_table(bias_ref, trows_ref, tcols_ref)


def first_backward(
    back_ref, above_ref, side_ref, corner_ref, xw_ref, q_ref, k_ref, v_ref, probs_ref, ctx_ref, hidden_ref, expanded_ref, slope_ref,
    gains_ref, qkv_ref, out_ref, up_ref, down_ref, trows_ref, tcols_ref, pick_ref, returned_ref,
    last_wbuf_ref, last_gain_ref, last_table_ref,
    gin_ref, mine_ref, theirs_ref, tables_ref,
    source_ref, gctx_ref, dq_ref, dk_ref, dv_ref, gpre_ref, grad_ref, wbuf_ref, gain_grad_ref, sems,
):
    masks = head_rows()
    fetch = pltpu.make_async_copy(last_wbuf_ref, wbuf_ref.at[pl.ds(WBLOCK, WBLOCK), :], sems.at[0])
    fetch.start()
    fill_source(source_ref, back_ref[...], above_ref, side_ref, corner_ref)
    g32 = gather_tokens(returned_ref[...], source_ref[...])
    g = g32.astype(BF16)
    hat_mlp, inv_mlp = normalize(hidden_ref[...])
    normed_mlp = (hat_mlp * gains_ref[1:2, :]).astype(BF16)
    gnormed = jnp.zeros((TOKENS, DIM), F32)
    for j in range(3):
        cols = slice(j * 256, (j + 1) * 256)
        gact = nn(g, down_ref[:, cols]).astype(BF16).astype(F32)
        gpre = (slope_ref[:, cols].astype(F32) * gact).astype(BF16)
        gpre_ref[:, cols] = gpre
        gnormed = gnormed + nt(gpre, up_ref[:, cols])
    gnormed = gnormed.astype(BF16).astype(F32)
    gain_grad_ref[1:2, :] = jnp.sum(gnormed * hat_mlp, axis=0, keepdims=True)
    ghid = g32 + norm_backward(gnormed, gains_ref[1:2, :], hat_mlp, inv_mlp)
    gblock, normed, gbranch, gain_grad = attention_backward_part(
        xw_ref[...].astype(F32), gains_ref[0:1, :], qkv_ref, out_ref, ghid,
        q_ref, k_ref, v_ref, probs_ref, ctx_ref, gctx_ref, dq_ref, dk_ref, dv_ref, grad_ref, masks,
    )
    gain_grad_ref[0:1, :] = gain_grad
    gin_ref[...] = scatter_tokens(pick_ref[...], gblock.astype(BF16)).astype(BF16)
    weight_grads(
        wbuf_ref, normed, dq_ref[...], dk_ref[...], dv_ref[...], ctx_ref[...], gbranch, normed_mlp, gpre_ref, expanded_ref, g
    )
    tables_ref[0:TROWS, :] = collapse_table(grad_ref, trows_ref, tcols_ref)
    tables_ref[TROWS : 2 * TROWS, :] = last_table_ref[...]
    tables_ref[2 * TROWS :, :] = jnp.zeros((8 * TCHUNK - 2 * TROWS, 128), BF16)
    gains = jnp.concatenate([ref[i : i + 1, :] for ref in (gain_grad_ref, last_gain_ref) for i in range(2)], axis=1)
    wbuf_ref[2 * WBLOCK :, :] = jnp.zeros((2 * HALF - 2 * WBLOCK, 128), BF16)
    for j in range(6):
        tile = jnp.concatenate([gains[:, j * 128 : (j + 1) * 128], jnp.zeros((15, 128), F32)], axis=0)
        wbuf_ref[2 * WBLOCK + j * 16 : 2 * WBLOCK + (j + 1) * 16, :] = tile.astype(BF16)
    fetch.wait()
    core = lax.rem(lax.axis_index("lat"), 2)
    keep = pltpu.make_async_copy(wbuf_ref.at[pl.ds(core * HALF, HALF), :], mine_ref, sems.at[1])
    send = pltpu.make_async_copy(wbuf_ref.at[pl.ds((1 - core) * HALF, HALF), :], theirs_ref, sems.at[2])
    send.start()
    keep.start()
    send.wait()
    keep.wait()


def pack_core(mine_ref, other_ref, tables_ref, packed_ref):
    for j in range(8):
        rows = slice(j * CHUNK, (j + 1) * CHUNK)
        total = mine_ref[rows, :].astype(F32) + other_ref[rows, :].astype(F32)
        packed_ref[j, 0:CHUNK, :] = total.astype(BF16)
        packed_ref[j, CHUNK:, :] = tables_ref[j * TCHUNK : (j + 1) * TCHUNK, :]


def sum_eight(ref, rows):
    total = ref[0, rows, :].astype(F32)
    for j in range(1, 8):
        total += ref[j, rows, :].astype(F32)
    return total.astype(BF16)


def sum_lon(parts_ref, spread_ref, table_ref):
    total = sum_eight(parts_ref, slice(0, CHUNK))
    for j in range(8):
        spread_ref[j] = total
    table_ref[...] = sum_eight(parts_ref, slice(CHUNK, CHUNK + TCHUNK))


def sum_lat(parts_ref, table_ref, spread_ref):
    total = sum_eight(parts_ref, slice(0, CHUNK))
    for j in range(8):
        spread_ref[j, 0:CHUNK, :] = total
        spread_ref[j, CHUNK:, :] = table_ref[...]


def unpack(mine_ref, other_ref, qkv_ref, out_ref, up_ref, down_ref, gains_ref, table_ref):
    core = lax.rem(lax.axis_index("lat"), 2)

    def load(start, count):
        pieces = []
        while count:
            half, place = divmod(start, HALF)
            j, place = divmod(place, CHUNK)
            size = min(count, CHUNK - place)
            here = mine_ref[j, place : place + size, :].astype(F32)
            there = other_ref[j, place : place + size, :].astype(F32)
            pieces.append(jnp.where(core == half, here, there))
            start, count = start + size, count - size
        return pieces[0] if len(pieces) == 1 else jnp.concatenate(pieces, axis=0)

    for b in range(2):
        for j in range(18):
            tile = load(b * WBLOCK + j * DIM, DIM)
            if j < 6:
                up_ref[b, :, j * 128 : (j + 1) * 128] = tile
            elif j < 12:
                down_ref[b, :, (j - 6) * 128 : (j - 5) * 128] = tile
            elif j < 16:
                qkv_ref[b, :, (j - 12) * 128 : (j - 11) * 128] = tile
            elif j == 16:
                qkv_ref[b, :, 512:576] = tile[:, :64]
                out_ref[b, :, 0:64] = tile[:, 64:]
            else:
                out_ref[b, :, 64:192] = tile
        for j in range(26):
            k, place = divmod(b * TROWS + j * 8, TCHUNK)
            base = CHUNK + place // 16 * 16
            pair = mine_ref[k, base : base + 16, :].astype(F32)
            piece = pair[place % 16 : place % 16 + HEADS]
            width = min(128, TABLE - j * 128)
            table_ref[b, 0, :, j * 128 : j * 128 + width] = piece[:, :width]
    gains = jnp.concatenate([load(2 * WBLOCK + j * 16, 16)[0:1] for j in range(6)], axis=1)
    for b in range(2):
        for i in range(2):
            k = b * 2 + i
            gains_ref[b, i : i + 1, :] = gains[:, k * DIM : (k + 1) * DIM]


def whole(array):
    return pl.BlockSpec(array.shape, lambda i: (0,) * array.ndim)


def picked(array, index):
    rest = array.shape[1:]
    return pl.BlockSpec((None,) + rest, lambda i: (index,) + (0,) * len(rest))


def in_place():
    return pl.BlockSpec(memory_space=pl.ANY)


def call(kernel, operands, specs, outs, scratch=(), flops=0, out_specs=None):
    shapes = [jax.ShapeDtypeStruct(shape, dtype) for shape, dtype in outs]
    moved = sum(a.size * a.dtype.itemsize for a in (*operands, *shapes))
    return pl.pallas_call(
        kernel,
        grid=(1,),
        out_shape=shapes,
        in_specs=specs,
        out_specs=out_specs or [whole(s) for s in shapes],
        scratch_shapes=list(scratch),
        cost_estimate=pl.CostEstimate(flops=flops, bytes_accessed=moved, transcendentals=0),
        compiler_params=pltpu.CompilerParams(vmem_limit_bytes=56 * 1024 * 1024),
    )(*operands)


def neighbour(sizes, steps):
    pairs = []
    for a in range(sizes[0]):
        for b in range(sizes[1]):
            source = ((a + steps[0]) % sizes[0]) * sizes[1] + (b + steps[1]) % sizes[1]
            pairs.append((source, a * sizes[1] + b))
    return pairs


def exchange(rows, side, corner, sizes, step):
    both = ("lat", "lon")
    rows = lax.ppermute(rows, both, neighbour(sizes, (step, 0)))
    side = lax.ppermute(side, both, neighbour(sizes, (0, step)))
    corner = lax.ppermute(corner, both, neighbour(sizes, (step, step)))
    return rows, side, corner


def vmem(shape, dtype):
    return pltpu.VMEM(shape, dtype)


def sum_over_devices(mine, theirs, tables, sizes):
    pairs = [(i ^ 1, i) for i in range(sizes[0])]
    groups = [[core + 2 * k for k in range(sizes[0] // 2)] for core in range(2)]
    other = lax.ppermute(theirs, "lat", pairs)
    packed = (8, CHUNK + TCHUNK, 128)
    [sent] = call(pack_core, [mine, other, tables], [whole(a) for a in (mine, other, tables)], [(packed, BF16)])
    parts = lax.all_to_all(sent, "lon", 0, 0)
    spread, table = call(sum_lon, [parts], [whole(parts)], [((8, CHUNK, 128), BF16), ((TCHUNK, 128), BF16)])
    parts = lax.all_to_all(spread, "lat", 0, 0, axis_index_groups=groups)
    [spread] = call(sum_lat, [parts, table], [whole(parts), whole(table)], [(packed, BF16)])
    half = lax.all_to_all(spread, "lon", 0, 0)
    other = lax.ppermute(half, "lat", pairs)
    outs = [((2, DIM, 3 * DIM), F32), ((2, DIM, DIM), F32), ((2, DIM, UNITS), F32), ((2, DIM, UNITS), F32)]
    outs += [((2, 2, DIM), F32), ((2, 1, HEADS, TABLE), F32)]
    return call(unpack, [half, other], [whole(half), whole(other)], outs)


def on_device(sizes, inputs, cotangent, norm_gains, qkv_weight, out_weight, up_weight, down_weight, bias_table):
    x = inputs.reshape(GRID, 2 * DIM)
    cot = cotangent.reshape(GRID, 2 * DIM)
    trows, tcols = jnp.asarray(table_rows(), BF16), jnp.asarray(table_cols(), BF16)
    pick_grid, pick_shift, pick_back = (
        jnp.asarray(m, BF16) for m in (grid_picker(), shifted_picker(), returned_picker())
    )
    strips = jnp.asarray(strip_picker(), BF16)
    weights = (norm_gains, qkv_weight, out_weight, up_weight, jnp.swapaxes(down_weight, 1, 2))
    tok, src, hid = (TOKENS, DIM), (SOURCE, 2 * DIM), (TOKENS, UNITS)
    strip_shapes = [(144, 2 * DIM), (144, 2 * DIM), (STRIP, 2 * DIM), (STRIP, 2 * DIM)]
    probs = (WINDOWS, WIN_TOK, QLANES)

    def table_spec(index):
        return pl.BlockSpec((None, None, HEADS, TABLE), lambda i: (index, 0, 0, 0))

    cot_side = cotangent[3:, :6].reshape(18, 2 * DIM)
    cot_corner = cotangent[:3, :6].reshape(18, 2 * DIM)
    cot_strips = exchange(cot[:144], cot_side, cot_corner, sizes, 1)

    fixed = (trows, tcols, pick_grid, strips)
    operands = [x, *weights, bias_table, *fixed]
    specs = [whole(x)] + [picked(a, 0) for a in weights] + [table_spec(0)] + [whole(a) for a in fixed]
    outs = [(tok, BF16)] * 4 + [(probs, BF16), (tok, BF16), (tok, F32), (hid, BF16), (hid, BF16)]
    outs += [(shape, BF16) for shape in strip_shapes]
    results = call(first_forward, operands, specs, outs, [vmem((WIN_TOK, QLANES), F32)], 650_000_000)
    saved, (top, bottom, side, corner) = results[:9], results[9:]

    own_strips = exchange(top, side, corner, sizes, 1)
    fixed = (trows, tcols, pick_shift)
    fields = (bottom, *own_strips, cot, *cot_strips)
    operands = [*fields, *weights, bias_table, *fixed]
    specs = [whole(a) for a in fields] + [picked(a, 1) for a in weights] + [table_spec(1)] + [whole(a) for a in fixed]
    outs = [(shape, BF16) for shape in strip_shapes] * 2
    outs += [((WBLOCK, 128), BF16), ((2, DIM), F32), ((TROWS, 128), BF16)]
    scratch = [vmem(src, BF16), vmem(tok, F32)] + [vmem(tok, BF16)] * 3 + [vmem(probs, BF16), vmem(tok, BF16)]
    scratch += [vmem((WIN_TOK, QLANES), F32)] + [vmem(tok, BF16)] * 4 + [vmem(hid, BF16)] * 2
    results = call(second_both, operands, specs, outs, scratch, 2_000_000_000)
    y_strips, back_strips, last_grads = results[:4], results[4:8], results[8:]

    back = exchange(*back_strips[1:], sizes, -1)
    y_strips, back = lax.optimization_barrier((y_strips, back))
    fixed = (trows, tcols, pick_grid, pick_back)
    operands = [back_strips[0], *back, *saved, *weights, *fixed, *last_grads]
    specs = [whole(a) for a in (back_strips[0], *back, *saved)] + [picked(a, 0) for a in weights]
    specs += [whole(a) for a in fixed] + [in_place(), whole(last_grads[1]), whole(last_grads[2])]
    outs = [((GRID, 2 * DIM), BF16), ((HALF, 128), BF16), ((HALF, 128), BF16), ((8 * TCHUNK, 128), BF16)]
    out_specs = [pl.BlockSpec((GRID, 2 * DIM), lambda i: (0, 0)), in_place(), in_place()]
    out_specs += [pl.BlockSpec((8 * TCHUNK, 128), lambda i: (0, 0))]
    scratch = [vmem(src, BF16)] + [vmem(tok, BF16)] * 4 + [vmem(hid, BF16), vmem((WIN_TOK, QLANES), F32)]
    scratch += [vmem((2 * HALF, 128), BF16), vmem((2, DIM), F32), pltpu.SemaphoreType.DMA((3,))]
    grad_inputs, mine, theirs, tables = call(
        first_backward, operands, specs, outs, scratch, 1_300_000_000, out_specs
    )

    y_rows, y_side, y_corner = exchange(*y_strips[1:], sizes, -1)
    rows = jnp.concatenate([y_rows, y_strips[0]]).reshape(ROWS, COLS, 2 * DIM)
    edge = jnp.concatenate([y_corner[:18].reshape(3, 6, 2 * DIM), y_side[:18].reshape(3, 6, 2 * DIM)])
    output = jnp.concatenate([edge, rows[:, 6:]], axis=1)

    grad_qkv, grad_out, grad_up, grad_down, grad_gains, grad_table = sum_over_devices(mine, theirs, tables, sizes)
    grad_down = jnp.swapaxes(grad_down, 1, 2)
    return (output, grad_inputs.reshape(ROWS, COLS, 2 * DIM), grad_gains, grad_qkv, grad_out, grad_up, grad_down, grad_table)


def solution(mesh):
    sizes = (mesh.shape["lat"], mesh.shape["lon"])

    def program(*arguments):
        return on_device(sizes, *arguments)

    fields, tables = P("lat", "lon", None), P(None, "lat", None, None)
    return jax.shard_map(
        program,
        mesh=mesh,
        in_specs=(fields, fields, P(), P(), P(), P(), P(), tables),
        out_specs=(fields, fields, P(), P(), P(), P(), P(), tables),
        check_vma=False,
    )
```

```python
import math

import jax
import jax.numpy as jnp
import numpy as np
from jax import lax
from jax.experimental import pallas as pl
from jax.experimental.pallas import tpu as pltpu
from jax.sharding import PartitionSpec as P

DIM = 192
HEADS = 6
HEAD_DIM = 32
UNITS = 768
ROWS = 6
COLS = 48
WIN_COLS = 12
WINDOWS = 4
WIN_TOK = 144
TOKENS = 576
GRID = ROWS * COLS
GROUP = 12
SPAN = 23
WIDE = SPAN * GROUP
CELL = 6 * SPAN
TABLE = 24 * CELL
QLANES = HEADS * WIN_TOK
STRIP = 32
SOURCE = 288 + 2 * STRIP
NORM_EPS = 1e-05
MASK_VALUE = -100.0
LOG2E = math.log2(math.e)
SCALE = 1.0 / math.sqrt(HEAD_DIM)
WBLOCK = 18 * DIM
CHUNK = 448
HALF = 8 * CHUNK
TCHUNK = 64
TROWS = 208

F32 = jnp.float32
BF16 = jnp.bfloat16


def token_places():
    t = np.arange(TOKENS)
    w, rest = t // WIN_TOK, t % WIN_TOK
    c, l, r = rest // GROUP, rest % GROUP // ROWS, rest % ROWS
    return r, w * WIN_COLS + c, l


def one_hot(places, size):
    return (places[:, None] == np.arange(size)[None, :]).astype(np.float32)


def grid_picker():
    r, j, _ = token_places()
    return one_hot(r * COLS + j, GRID)


def shifted_picker():
    r, j, _ = token_places()
    half = np.where(r < 3, r, r - 3)
    inner = np.where(r < 3, 0, 144) + half * COLS + j + 6
    edge = np.where(r < 3, 288, 288 + STRIP) + half * 6 + j - 42
    return one_hot(np.where(j < 42, inner, edge), SOURCE)


def returned_picker():
    r, j, _ = token_places()
    half = np.where(r >= 3, r - 3, r)
    inner = np.where(r >= 3, 0, 144) + half * COLS + j
    edge = np.where(r >= 3, 288, 288 + STRIP) + half * 6 + j
    return one_hot(np.where(j >= 6, inner, edge), SOURCE)


def strip_picker():
    picked = np.zeros((2 * STRIP, GRID), np.float32)
    for i in range(3):
        for j in range(6):
            picked[i * 6 + j, (i + 3) * COLS + j] = 1
            picked[STRIP + i * 6 + j, i * COLS + j] = 1
    return picked


def table_rows():
    picked = np.zeros((2, HEADS * 16, 24 * 8), np.float32)
    for h in range(HEADS):
        for lq in range(2):
            for lp in range(2):
                for rq in range(6):
                    picked[lp, h * 16 + lq * 6 + rq, (lq * 12 + lp * 6 + rq) * 8 + h] = 1
    return picked


def table_cols():
    picked = np.zeros((2, 6 * SPAN, WIDE), np.float32)
    for lp in range(2):
        for rp in range(6):
            for d in range(SPAN):
                picked[lp, rp * SPAN + d, d * GROUP + lp * 6 + rp] = 1
    return picked


def nn(a, b):
    return jnp.dot(a, b, preferred_element_type=F32)


def nt(a, b):
    return lax.dot_general(a, b, (((1,), (1,)), ((), ())), preferred_element_type=F32)


def tn(a, b):
    return lax.dot_general(a, b, (((0,), (0,)), ((), ())), preferred_element_type=F32)


def level_mask():
    t = lax.broadcasted_iota(jnp.int32, (TOKENS, DIM), 0)
    return (lax.div(t, 6) & 1) == 1


def gather_tokens(picker, source):
    both = nn(picker, source)
    return jnp.where(level_mask(), both[:, DIM:], both[:, :DIM])


def scatter_tokens(picker, tokens):
    upper = level_mask()
    zero = jnp.zeros_like(tokens)
    both = jnp.concatenate([jnp.where(upper, zero, tokens), jnp.where(upper, tokens, zero)], axis=1)
    return tn(picker, both.astype(BF16))


def normalize(x):
    centre = jnp.mean(x, axis=-1, keepdims=True)
    off = x - centre
    spread = jnp.mean(off * off, axis=-1, keepdims=True)
    inv = lax.rsqrt(spread + NORM_EPS)
    return off * inv, inv


def norm_backward(grad, gain, hat, inv):
    scaled = grad * gain
    mean_one = jnp.mean(scaled, axis=-1, keepdims=True)
    mean_two = jnp.mean(scaled * hat, axis=-1, keepdims=True)
    return inv * (scaled - mean_one - hat * mean_two)


def gelu_parts(x):
    bell = jnp.exp2(x * x * (-0.5 * LOG2E))
    t = 1.0 / (1.0 + (0.3275911 * math.sqrt(0.5)) * jnp.abs(x))
    poly = t * (0.254829592 + t * (-0.284496736 + t * (1.421413741 + t * (-1.453152027 + t * 1.061405429))))
    tail = 0.5 * poly * bell
    below = jnp.where(x >= 0, 1.0 - tail, tail)
    return below, bell * (1.0 / math.sqrt(2.0 * math.pi))


def head_rows():
    lane = lax.div(lax.broadcasted_iota(jnp.int32, (1, DIM), 1), HEAD_DIM)
    return [(lane == h) for h in range(HEADS)]


def stack_heads(x, masks):
    return jnp.concatenate([jnp.where(m, x, jnp.zeros_like(x)) for m in masks], axis=0)


def fold_heads(x, masks):
    folded = x[:WIN_TOK]
    for h in range(1, HEADS):
        folded = jnp.where(masks[h], x[h * WIN_TOK : (h + 1) * WIN_TOK], folded)
    return folded


def expand_table(table_ref, trows_ref, tcols_ref, bias_ref):
    table = jnp.concatenate([table_ref[h] for h in range(HEADS)] + [jnp.zeros((2, TABLE), F32)], axis=0) * LOG2E
    table = jnp.concatenate([table[:, k * CELL : (k + 1) * CELL] for k in range(24)], axis=0)
    high = table.astype(BF16)
    low = (table - high.astype(F32)).astype(BF16)
    wide = jnp.zeros((HEADS * 16, WIDE), F32)
    for lp in range(2):
        for part in (high, low):
            wide += nn(nn(trows_ref[lp], part).astype(BF16), tcols_ref[lp])
    for cq in range(WIN_COLS):
        start = GROUP * (WIN_COLS - 1 - cq)
        row = jnp.concatenate(
            [wide[h * 16 : h * 16 + GROUP, start : start + WIN_TOK] for h in range(HEADS)], axis=1
        )
        bias_ref[cq * GROUP : (cq + 1) * GROUP, :] = row


def add_mask(bias_ref, flag):
    key = lax.broadcasted_iota(jnp.int32, (WIN_TOK, 1), 0)
    query = lax.broadcasted_iota(jnp.int32, (1, QLANES), 1)
    key_up = (lax.div(key, 3) & 1).astype(F32)
    query_up = (lax.div(query, 3) & 1).astype(F32)
    apart = jnp.abs(key_up - query_up)
    bias_ref[...] += apart * (flag * (MASK_VALUE * LOG2E))


def collapse_table(grad_ref, trows_ref, tcols_ref):
    parts = []
    for h in range(HEADS):
        total = None
        for cq in range(WIN_COLS):
            start = GROUP * (WIN_COLS - 1 - cq)
            piece = grad_ref[cq * GROUP : (cq + 1) * GROUP, h * WIN_TOK : (h + 1) * WIN_TOK]
            pads = [jnp.zeros((GROUP, start), F32)] if start else []
            tail = WIDE - start - WIN_TOK
            pads_after = [jnp.zeros((GROUP, tail), F32)] if tail else []
            piece = jnp.concatenate(pads + [piece] + pads_after, axis=1)
            total = piece if total is None else total + piece
        parts.append(jnp.concatenate([total, jnp.zeros((16 - GROUP, WIDE), F32)], axis=0))
    wide = jnp.concatenate(parts, axis=0).astype(BF16)
    result = jnp.zeros((24 * 8, CELL), F32)
    for lp in range(2):
        narrow = nt(wide, tcols_ref[lp]).astype(BF16)
        result += tn(trows_ref[lp], narrow)
    cells = [result[k * 8 : (k + 1) * 8] for k in range(24)] + [jnp.zeros((8, 26 * 128 - TABLE), F32)]
    flat = jnp.concatenate(cells, axis=1)
    return jnp.concatenate([flat[:, j * 128 : (j + 1) * 128] for j in range(26)], axis=0).astype(BF16)


def attention(q_ref, k_ref, v_ref, bias_ref, probs_ref, ctx_ref, masks):
    for w in range(WINDOWS):
        rows = pl.ds(w * WIN_TOK, WIN_TOK)
        stacked = stack_heads(q_ref[rows, :], masks)
        scores = nt(k_ref[rows, :], stacked) * (SCALE * LOG2E) + bias_ref[...]
        weights = jnp.exp2(scores)
        inverse = 1.0 / jnp.sum(weights, axis=0, keepdims=True)
        probs = (weights * inverse).astype(BF16)
        probs_ref[w] = probs
        ctx_ref[rows, :] = fold_heads(tn(probs, v_ref[rows, :]), masks).astype(BF16)


def attention_back(q_ref, k_ref, v_ref, probs_ref, gctx_ref, dq_ref, dk_ref, dv_ref, grad_ref, masks):
    for w in range(WINDOWS):
        rows = pl.ds(w * WIN_TOK, WIN_TOK)
        stacked_g = stack_heads(gctx_ref[rows, :], masks)
        stacked_q = stack_heads(q_ref[rows, :], masks)
        probs_half = probs_ref[w]
        probs = probs_half.astype(F32)
        grad_probs = nt(v_ref[rows, :], stacked_g)
        inner = jnp.sum(grad_probs * probs, axis=0, keepdims=True)
        grad_scores = probs * (grad_probs - inner)
        if w == 0:
            grad_ref[...] = grad_scores
        else:
            grad_ref[...] += grad_scores
        half = grad_scores.astype(BF16)
        dv_ref[rows, :] = nn(probs_half, stacked_g).astype(BF16)
        dk_ref[rows, :] = (nn(half, stacked_q) * SCALE).astype(BF16)
        dq_ref[rows, :] = (fold_heads(tn(half, k_ref[rows, :]), masks) * SCALE).astype(BF16)


def project(normed, qkv_ref, q_ref, k_ref, v_ref):
    for i, ref in enumerate((q_ref, k_ref, v_ref)):
        ref[...] = nn(normed, qkv_ref[:, i * DIM : (i + 1) * DIM]).astype(BF16)


def put_weights(wbuf_ref, offset, value):
    tiles = value.shape[1] // 128
    for j in range(tiles):
        wbuf_ref[(offset + j) * DIM : (offset + j + 1) * DIM, :] = value[:, j * 128 : (j + 1) * 128].astype(BF16)


def weight_grads(wbuf_ref, normed, dq, dk, dv, ctx, gbranch, normed_mlp, gpre_ref, expanded_ref, g):
    for j in range(3):
        cols = slice(j * 256, (j + 1) * 256)
        put_weights(wbuf_ref, 2 * j, tn(normed_mlp, gpre_ref[:, cols]))
        put_weights(wbuf_ref, 6 + 2 * j, tn(g, expanded_ref[:, cols]))
    put_weights(wbuf_ref, 12, tn(normed, jnp.concatenate([dq, dk], axis=1)))
    put_weights(wbuf_ref, 15, jnp.concatenate([tn(normed, dv), tn(ctx, gbranch)], axis=1))


def attention_backward_part(
    x, gain, qkv_ref, out_ref, ghid, q_ref, k_ref, v_ref, probs_ref, ctx_ref, gctx_ref, dq_ref, dk_ref, dv_ref, grad_ref, masks
):
    gbranch = ghid.astype(BF16)
    gctx_ref[...] = nt(gbranch, out_ref[...]).astype(BF16)
    attention_back(q_ref, k_ref, v_ref, probs_ref, gctx_ref, dq_ref, dk_ref, dv_ref, grad_ref, masks)
    gnormed = nt(dq_ref[...], qkv_ref[:, :DIM])
    gnormed += nt(dk_ref[...], qkv_ref[:, DIM : 2 * DIM])
    gnormed += nt(dv_ref[...], qkv_ref[:, 2 * DIM :])
    gnormed = gnormed.astype(BF16).astype(F32)
    hat, inv = normalize(x)
    gain_grad = jnp.sum(gnormed * hat, axis=0, keepdims=True)
    gblock = norm_backward(gnormed, gain, hat, inv) + ghid
    normed = (hat * gain).astype(BF16)
    return gblock, normed, gbranch, gain_grad


def first_attention(
    x_ref, gains_ref, qkv_ref, out_ref, table_ref, trows_ref, tcols_ref, pick_ref,
    xw_ref, q_ref, k_ref, v_ref, probs_ref, ctx_ref, hidden_ref, bias_ref,
):
    x = gather_tokens(pick_ref[...], x_ref[...])
    xw_ref[...] = x.astype(BF16)
    hat, _ = normalize(x)
    project((hat * gains_ref[0:1, :]).astype(BF16), qkv_ref, q_ref, k_ref, v_ref)
    expand_table(table_ref, trows_ref, tcols_ref, bias_ref)
    attention(q_ref, k_ref, v_ref, bias_ref, probs_ref, ctx_ref, head_rows())
    branch = nn(ctx_ref[...], out_ref[...]).astype(BF16)
    hidden_ref[...] = xw_ref[...].astype(F32) + branch.astype(F32)


def first_mlp(
    hidden_ref, gains_ref, up_ref, down_ref, pick_ref, strips_ref,
    expanded_ref, slope_ref, top_ref, bottom_ref, side_ref, corner_ref,
):
    hidden = hidden_ref[...]
    hat, _ = normalize(hidden)
    normed_mlp = (hat * gains_ref[1:2, :]).astype(BF16)
    total = hidden
    for j in range(3):
        cols = slice(j * 256, (j + 1) * 256)
        pre = nn(normed_mlp, up_ref[:, cols])
        below, density = gelu_parts(pre)
        expanded = (pre * below).astype(BF16)
        expanded_ref[:, cols] = expanded
        slope_ref[:, cols] = (below + pre * density).astype(BF16)
        total = total + nt(expanded, down_ref[:, cols])
    grid = scatter_tokens(pick_ref[...], total.astype(BF16)).astype(BF16)
    top_ref[...] = grid[:144]
    bottom_ref[...] = grid[144:]
    edges = nn(strips_ref[...], grid).astype(BF16)
    side_ref[...] = edges[:STRIP]
    corner_ref[...] = edges[STRIP:]


def fill_source(source_ref, own, above_ref, side_ref, corner_ref):
    source_ref[0:144, :] = own
    source_ref[144:288, :] = above_ref[...]
    source_ref[288:SOURCE, :] = jnp.zeros((2 * STRIP, 2 * DIM), BF16)
    source_ref[288 : 288 + side_ref.shape[0], :] = side_ref[...]
    source_ref[288 + STRIP : 288 + STRIP + corner_ref.shape[0], :] = corner_ref[...]


def put_source(own_ref, row_ref, side_ref, corner_ref, value):
    own_ref[...] = value[0:144]
    row_ref[...] = value[144:288]
    side_ref[...] = value[288 : 288 + STRIP]
    corner_ref[...] = value[288 + STRIP :]


def prepare_second(
    cot_ref, above_ref, side_ref, corner_ref, down_ref, table_ref, trows_ref, tcols_ref, pick_ref,
    g_ref, gact_ref, bias_ref, source_ref,
):
    fill_source(source_ref, cot_ref[144:288, :], above_ref, side_ref, corner_ref)
    g_ref[...] = gather_tokens(pick_ref[...], source_ref[...]).astype(BF16)
    for j in range(3):
        cols = slice(j * 256, (j + 1) * 256)
        gact_ref[:, cols] = nn(g_ref[...], down_ref[:, cols]).astype(BF16)
    expand_table(table_ref, trows_ref, tcols_ref, bias_ref)
    add_mask(bias_ref, (lax.axis_index("lat") == lax.axis_size("lat") - 1).astype(F32))


def second_both(
    own_ref, above_ref, side_ref, corner_ref, g_ref, gact_ref, bias_ref,
    gains_ref, qkv_ref, out_ref, up_ref, down_ref, pick_ref,
    y_own_ref, y_row_ref, y_side_ref, y_corner_ref, back_own_ref, back_row_ref, back_side_ref, back_corner_ref,
    normed_ref, dq_ref, dk_ref, dv_ref, ctx_ref, gbranch_ref, normed_mlp_ref, gpre_ref, expanded_ref, grad_ref, gain_grad_ref,
    source_ref, x_ref, q_ref, k_ref, v_ref, probs_ref, gctx_ref,
):
    masks = head_rows()
    fill_source(source_ref, own_ref[...], above_ref, side_ref, corner_ref)
    x_ref[...] = gather_tokens(pick_ref[...], source_ref[...])
    hat, _ = normalize(x_ref[...])
    project((hat * gains_ref[0:1, :]).astype(BF16), qkv_ref, q_ref, k_ref, v_ref)
    attention(q_ref, k_ref, v_ref, bias_ref, probs_ref, ctx_ref, masks)
    branch = nn(ctx_ref[...], out_ref[...]).astype(BF16)
    hidden = x_ref[...] + branch.astype(F32)
    hat_mlp, inv_mlp = normalize(hidden)
    normed_mlp = (hat_mlp * gains_ref[1:2, :]).astype(BF16)
    normed_mlp_ref[...] = normed_mlp
    total = hidden
    gnormed = jnp.zeros((TOKENS, DIM), F32)
    for j in range(3):
        cols = slice(j * 256, (j + 1) * 256)
        pre = nn(normed_mlp, up_ref[:, cols])
        below, density = gelu_parts(pre)
        expanded = (pre * below).astype(BF16)
        expanded_ref[:, cols] = expanded
        total = total + nt(expanded, down_ref[:, cols])
        gpre = ((below + pre * density) * gact_ref[:, cols].astype(F32)).astype(BF16)
        gpre_ref[:, cols] = gpre
        gnormed = gnormed + nt(gpre, up_ref[:, cols])
    y = scatter_tokens(pick_ref[...], total.astype(BF16)).astype(BF16)
    put_source(y_own_ref, y_row_ref, y_side_ref, y_corner_ref, y)
    gnormed = gnormed.astype(BF16).astype(F32)
    gain_grad_ref[1:2, :] = jnp.sum(gnormed * hat_mlp, axis=0, keepdims=True)
    ghid = g_ref[...].astype(F32) + norm_backward(gnormed, gains_ref[1:2, :], hat_mlp, inv_mlp)
    gblock, normed, gbranch, gain_grad = attention_backward_part(
        x_ref[...], gains_ref[0:1, :], qkv_ref, out_ref, ghid,
        q_ref, k_ref, v_ref, probs_ref, ctx_ref, gctx_ref, dq_ref, dk_ref, dv_ref, grad_ref, masks,
    )
    gain_grad_ref[0:1, :] = gain_grad
    back = scatter_tokens(pick_ref[...], gblock.astype(BF16)).astype(BF16)
    put_source(back_own_ref, back_row_ref, back_side_ref, back_corner_ref, back)
    normed_ref[...] = normed
    gbranch_ref[...] = gbranch


def second_weights(
    normed_ref, dq_ref, dk_ref, dv_ref, ctx_ref, gbranch_ref, normed_mlp_ref, gpre_ref, expanded_ref, grad_ref, g_ref,
    trows_ref, tcols_ref, wbuf_ref, table_grad_ref,
):
    weight_grads(
        wbuf_ref, normed_ref[...], dq_ref[...], dk_ref[...], dv_ref[...], ctx_ref[...], gbranch_ref[...],
        normed_mlp_ref[...], gpre_ref, expanded_ref, g_ref[...],
    )
    table_grad_ref[...] = collapse_table(grad_ref, trows_ref, tcols_ref)


def first_mlp_back(
    back_ref, above_ref, side_ref, corner_ref, hidden_ref, slope_ref, gains_ref, up_ref, down_ref, returned_ref,
    g_ref, ghid_ref, normed_mlp_ref, gpre_ref, gain_grad_ref, source_ref,
):
    fill_source(source_ref, back_ref[...], above_ref, side_ref, corner_ref)
    g32 = gather_tokens(returned_ref[...], source_ref[...])
    g = g32.astype(BF16)
    g_ref[...] = g
    hat_mlp, inv_mlp = normalize(hidden_ref[...])
    normed_mlp_ref[...] = (hat_mlp * gains_ref[1:2, :]).astype(BF16)
    gnormed = jnp.zeros((TOKENS, DIM), F32)
    for j in range(3):
        cols = slice(j * 256, (j + 1) * 256)
        gact = nn(g, down_ref[:, cols]).astype(BF16).astype(F32)
        gpre = (slope_ref[:, cols].astype(F32) * gact).astype(BF16)
        gpre_ref[:, cols] = gpre
        gnormed = gnormed + nt(gpre, up_ref[:, cols])
    gnormed = gnormed.astype(BF16).astype(F32)
    gain_grad_ref[...] = jnp.sum(gnormed * hat_mlp, axis=0, keepdims=True)
    ghid_ref[...] = g32 + norm_backward(gnormed, gains_ref[1:2, :], hat_mlp, inv_mlp)


def first_attention_back(
    ghid_ref, g_ref, normed_mlp_ref, gpre_ref, mlp_gain_ref, xw_ref, q_ref, k_ref, v_ref, probs_ref, ctx_ref, expanded_ref,
    gains_ref, qkv_ref, out_ref, trows_ref, tcols_ref, pick_ref, last_wbuf_ref, last_gain_ref, last_table_ref,
    gin_ref, mine_ref, theirs_ref, tables_ref,
    gctx_ref, dq_ref, dk_ref, dv_ref, grad_ref, wbuf_ref, sems,
):
    masks = head_rows()
    fetch = pltpu.make_async_copy(last_wbuf_ref, wbuf_ref.at[pl.ds(WBLOCK, WBLOCK), :], sems.at[0])
    fetch.start()
    gblock, normed, gbranch, gain_grad = attention_backward_part(
        xw_ref[...].astype(F32), gains_ref[0:1, :], qkv_ref, out_ref, ghid_ref[...],
        q_ref, k_ref, v_ref, probs_ref, ctx_ref, gctx_ref, dq_ref, dk_ref, dv_ref, grad_ref, masks,
    )
    gin_ref[...] = scatter_tokens(pick_ref[...], gblock.astype(BF16)).astype(BF16)
    weight_grads(
        wbuf_ref, normed, dq_ref[...], dk_ref[...], dv_ref[...], ctx_ref[...], gbranch,
        normed_mlp_ref[...], gpre_ref, expanded_ref, g_ref[...],
    )
    tables_ref[0:TROWS, :] = collapse_table(grad_ref, trows_ref, tcols_ref)
    tables_ref[TROWS : 2 * TROWS, :] = last_table_ref[...]
    tables_ref[2 * TROWS :, :] = jnp.zeros((8 * TCHUNK - 2 * TROWS, 128), BF16)
    gains = jnp.concatenate([gain_grad, mlp_gain_ref[...], last_gain_ref[0:1, :], last_gain_ref[1:2, :]], axis=1)
    wbuf_ref[2 * WBLOCK :, :] = jnp.zeros((2 * HALF - 2 * WBLOCK, 128), BF16)
    for j in range(6):
        tile = jnp.concatenate([gains[:, j * 128 : (j + 1) * 128], jnp.zeros((15, 128), F32)], axis=0)
        wbuf_ref[2 * WBLOCK + j * 16 : 2 * WBLOCK + (j + 1) * 16, :] = tile.astype(BF16)
    fetch.wait()
    core = lax.rem(lax.axis_index("lat"), 2)
    keep = pltpu.make_async_copy(wbuf_ref.at[pl.ds(core * HALF, HALF), :], mine_ref, sems.at[1])
    send = pltpu.make_async_copy(wbuf_ref.at[pl.ds((1 - core) * HALF, HALF), :], theirs_ref, sems.at[2])
    send.start()
    keep.start()
    send.wait()
    keep.wait()


def pack_core(mine_ref, other_ref, tables_ref, packed_ref):
    for j in range(8):
        rows = slice(j * CHUNK, (j + 1) * CHUNK)
        total = mine_ref[rows, :].astype(F32) + other_ref[rows, :].astype(F32)
        packed_ref[j, 0:CHUNK, :] = total.astype(BF16)
        packed_ref[j, CHUNK:, :] = tables_ref[j * TCHUNK : (j + 1) * TCHUNK, :]


def sum_eight(ref, rows):
    total = ref[0, rows, :].astype(F32)
    for j in range(1, 8):
        total += ref[j, rows, :].astype(F32)
    return total.astype(BF16)


def sum_lon(parts_ref, spread_ref, table_ref):
    total = sum_eight(parts_ref, slice(0, CHUNK))
    for j in range(8):
        spread_ref[j] = total
    table_ref[...] = sum_eight(parts_ref, slice(CHUNK, CHUNK + TCHUNK))


def sum_lat(parts_ref, table_ref, spread_ref):
    total = sum_eight(parts_ref, slice(0, CHUNK))
    for j in range(8):
        spread_ref[j, 0:CHUNK, :] = total
        spread_ref[j, CHUNK:, :] = table_ref[...]


def unpack(mine_ref, other_ref, qkv_ref, out_ref, up_ref, down_ref, gains_ref, table_ref):
    core = lax.rem(lax.axis_index("lat"), 2)

    def load(start, count):
        pieces = []
        while count:
            half, place = divmod(start, HALF)
            j, place = divmod(place, CHUNK)
            size = min(count, CHUNK - place)
            here = mine_ref[j, place : place + size, :].astype(F32)
            there = other_ref[j, place : place + size, :].astype(F32)
            pieces.append(jnp.where(core == half, here, there))
            start, count = start + size, count - size
        return pieces[0] if len(pieces) == 1 else jnp.concatenate(pieces, axis=0)

    for b in range(2):
        for j in range(18):
            tile = load(b * WBLOCK + j * DIM, DIM)
            if j < 6:
                up_ref[b, :, j * 128 : (j + 1) * 128] = tile
            elif j < 12:
                down_ref[b, :, (j - 6) * 128 : (j - 5) * 128] = tile
            elif j < 16:
                qkv_ref[b, :, (j - 12) * 128 : (j - 11) * 128] = tile
            elif j == 16:
                qkv_ref[b, :, 512:576] = tile[:, :64]
                out_ref[b, :, 0:64] = tile[:, 64:]
            else:
                out_ref[b, :, 64:192] = tile
        for j in range(26):
            k, place = divmod(b * TROWS + j * 8, TCHUNK)
            base = CHUNK + place // 16 * 16
            pair = mine_ref[k, base : base + 16, :].astype(F32)
            piece = pair[place % 16 : place % 16 + HEADS]
            width = min(128, TABLE - j * 128)
            for h in range(HEADS):
                table_ref[b * HEADS + h, :, j * 128 : j * 128 + width] = piece[h : h + 1, :width]
    gains = jnp.concatenate([load(2 * WBLOCK + j * 16, 16)[0:1] for j in range(6)], axis=1)
    for b in range(2):
        for i in range(2):
            k = b * 2 + i
            gains_ref[b, i : i + 1, :] = gains[:, k * DIM : (k + 1) * DIM]


def whole(array):
    return pl.BlockSpec(array.shape, lambda i: (0,) * array.ndim)


def picked(array, index):
    rest = array.shape[1:]
    return pl.BlockSpec((None,) + rest, lambda i: (index,) + (0,) * len(rest))


def in_place():
    return pl.BlockSpec(memory_space=pl.ANY)


def call(kernel, operands, specs, outs, scratch=(), micros=2, out_specs=None, mebibytes=10):
    shapes = [jax.ShapeDtypeStruct(shape, dtype) for shape, dtype in outs]
    moved = sum(a.size * a.dtype.itemsize for a in (*operands, *shapes))
    return pl.pallas_call(
        kernel,
        grid=(1,),
        out_shape=shapes,
        in_specs=specs,
        out_specs=out_specs or [whole(s) for s in shapes],
        scratch_shapes=list(scratch),
        cost_estimate=pl.CostEstimate(flops=micros * 1_100_000_000, bytes_accessed=moved, transcendentals=0),
        compiler_params=pltpu.CompilerParams(vmem_limit_bytes=mebibytes * 1024 * 1024),
    )(*operands)


def neighbour(sizes, steps):
    pairs = []
    for a in range(sizes[0]):
        for b in range(sizes[1]):
            source = ((a + steps[0]) % sizes[0]) * sizes[1] + (b + steps[1]) % sizes[1]
            pairs.append((source, a * sizes[1] + b))
    return pairs


def exchange(rows, side, corner, sizes, step):
    both = ("lat", "lon")
    rows = lax.ppermute(rows, both, neighbour(sizes, (step, 0)))
    side = lax.ppermute(side, both, neighbour(sizes, (0, step)))
    corner = lax.ppermute(corner, both, neighbour(sizes, (step, step)))
    return rows, side, corner


def vmem(shape, dtype):
    return pltpu.VMEM(shape, dtype)


def sum_over_devices(mine, theirs, tables, sizes):
    pairs = [(i ^ 1, i) for i in range(sizes[0])]
    groups = [[core + 2 * k for k in range(sizes[0] // 2)] for core in range(2)]
    other = lax.ppermute(theirs, "lat", pairs)
    packed = (8, CHUNK + TCHUNK, 128)
    [sent] = call(pack_core, [mine, other, tables], [whole(a) for a in (mine, other, tables)], [(packed, BF16)])
    parts = lax.all_to_all(sent, "lon", 0, 0)
    spread, table = call(sum_lon, [parts], [whole(parts)], [((8, CHUNK, 128), BF16), ((TCHUNK, 128), BF16)])
    parts = lax.all_to_all(spread, "lat", 0, 0, axis_index_groups=groups)
    [spread] = call(sum_lat, [parts, table], [whole(parts), whole(table)], [(packed, BF16)])
    half = lax.all_to_all(spread, "lon", 0, 0)
    other = lax.ppermute(half, "lat", pairs)
    outs = [((2, DIM, 3 * DIM), F32), ((2, DIM, DIM), F32), ((2, DIM, UNITS), F32), ((2, DIM, UNITS), F32)]
    outs += [((2, 2, DIM), F32), ((2 * HEADS, 1, TABLE), F32)]
    return call(unpack, [half, other], [whole(half), whole(other)], outs)


def on_device(sizes, inputs, cotangent, norm_gains, qkv_weight, out_weight, up_weight, down_weight, bias_table):
    x = inputs.reshape(GRID, 2 * DIM)
    cot = cotangent.reshape(GRID, 2 * DIM)
    trows, tcols = jnp.asarray(table_rows(), BF16), jnp.asarray(table_cols(), BF16)
    pick_grid, pick_shift, pick_back = (
        jnp.asarray(m, BF16) for m in (grid_picker(), shifted_picker(), returned_picker())
    )
    strips = jnp.asarray(strip_picker(), BF16)
    weights = (norm_gains, qkv_weight, out_weight, up_weight, jnp.swapaxes(down_weight, 1, 2))
    tok, src, hid = (TOKENS, DIM), (SOURCE, 2 * DIM), (TOKENS, UNITS)
    strip_shapes = [(144, 2 * DIM), (144, 2 * DIM), (STRIP, 2 * DIM), (STRIP, 2 * DIM)]
    probs = (WINDOWS, WIN_TOK, QLANES)

    def table_spec(index):
        return pl.BlockSpec((HEADS, 1, TABLE), lambda i: (index, 0, 0))

    bias_table = bias_table.reshape(2 * HEADS, 1, TABLE)
    cot_side = cotangent[3:, :6].reshape(18, 2 * DIM)
    cot_corner = cotangent[:3, :6].reshape(18, 2 * DIM)
    cot_strips = exchange(cot[:144], cot_side, cot_corner, sizes, 1)

    gains, qkv, out, up, down = weights
    wide_tok, wide_hid = (tok, BF16), (hid, BF16)
    bias = (WIN_TOK, QLANES)

    def specs_for(arrays, index):
        specs = []
        for a in arrays:
            if any(a is w for w in weights):
                specs.append(picked(a, index))
            elif a is bias_table:
                specs.append(table_spec(index))
            else:
                specs.append(whole(a))
        return specs

    operands = [x, gains, qkv, out, bias_table, trows, tcols, pick_grid]
    outs = [wide_tok] * 4 + [(probs, BF16), wide_tok, (tok, F32)]
    results = call(first_attention, operands, specs_for(operands, 0), outs, [vmem(bias, F32)], 7, mebibytes=14)
    xw, q, k, v, probs_first, ctx, hidden = results
    hidden, cot_strips = lax.optimization_barrier((hidden, cot_strips))

    operands = [hidden, gains, up, down, pick_grid, strips]
    outs = [wide_hid, wide_hid] + [(shape, BF16) for shape in strip_shapes]
    results = call(first_mlp, operands, specs_for(operands, 0), outs, (), 4, mebibytes=14)
    expanded, slope, top, bottom, side, corner = results
    (top, side, corner), cot_strips = lax.optimization_barrier(((top, side, corner), cot_strips))

    own_strips = exchange(top, side, corner, sizes, 1)
    operands = [cot, *cot_strips, down, bias_table, trows, tcols, pick_shift]
    outs = [wide_tok, wide_hid, (bias, F32)]
    g, gact, bias_last = call(
        prepare_second, operands, specs_for(operands, 1), outs, [vmem(src, BF16)], 3, mebibytes=14
    )

    operands = [bottom, *own_strips, g, gact, bias_last, *weights, pick_shift]
    outs = [(shape, BF16) for shape in strip_shapes] * 2 + [wide_tok] * 7 + [wide_hid] * 2 + [(bias, F32), ((2, DIM), F32)]
    scratch = [vmem(src, BF16), vmem(tok, F32)] + [vmem(tok, BF16)] * 3 + [vmem(probs, BF16), vmem(tok, BF16)]
    results = call(second_both, operands, specs_for(operands, 1), outs, scratch, 12, mebibytes=14)
    y_strips, back_strips, terms, last_gain = results[:4], results[4:8], results[8:18], results[18]

    back = exchange(*back_strips[1:], sizes, -1)
    operands = [*terms, g, trows, tcols]
    outs = [((WBLOCK, 128), BF16), ((TROWS, 128), BF16)]
    last_wbuf, last_table = call(second_weights, operands, specs_for(operands, 1), outs, (), 4, mebibytes=14)
    y_strips, back = lax.optimization_barrier((y_strips, back))
    y_moved = exchange(*y_strips[1:], sizes, -1)

    operands = [back_strips[0], *back, hidden, slope, gains, up, down, pick_back]
    outs = [wide_tok, (tok, F32), wide_tok, wide_hid, ((1, DIM), F32)]
    results = call(first_mlp_back, operands, specs_for(operands, 0), outs, [vmem(src, BF16)], 3, mebibytes=14)
    g, ghid, normed_mlp, gpre, mlp_gain = results
    ghid, y_moved = lax.optimization_barrier((ghid, y_moved))

    operands = [ghid, g, normed_mlp, gpre, mlp_gain, xw, q, k, v, probs_first, ctx, expanded, gains, qkv, out]
    operands += [trows, tcols, pick_grid, last_wbuf, last_gain, last_table]
    specs = specs_for(operands, 0)
    specs[-3] = in_place()
    outs = [((GRID, 2 * DIM), BF16), ((HALF, 128), BF16), ((HALF, 128), BF16), ((8 * TCHUNK, 128), BF16)]
    out_specs = [pl.BlockSpec((GRID, 2 * DIM), lambda i: (0, 0)), in_place(), in_place()]
    out_specs += [pl.BlockSpec((8 * TCHUNK, 128), lambda i: (0, 0))]
    scratch = [vmem(tok, BF16)] * 4 + [vmem(bias, F32), vmem((2 * HALF, 128), BF16), pltpu.SemaphoreType.DMA((3,))]
    grad_inputs, mine, theirs, tables = call(
        first_attention_back, operands, specs, outs, scratch, 8, out_specs, 14
    )

    y_rows, y_side, y_corner = y_moved
    rows = jnp.concatenate([y_rows, y_strips[0]]).reshape(ROWS, COLS, 2 * DIM)
    edge = jnp.concatenate([y_corner[:18].reshape(3, 6, 2 * DIM), y_side[:18].reshape(3, 6, 2 * DIM)])
    output = jnp.concatenate([edge, rows[:, 6:]], axis=1)

    grad_qkv, grad_out, grad_up, grad_down, grad_gains, grad_table = sum_over_devices(mine, theirs, tables, sizes)
    grad_down = jnp.swapaxes(grad_down, 1, 2)
    grad_table = grad_table.reshape(2, 1, HEADS, TABLE)
    return (output, grad_inputs.reshape(ROWS, COLS, 2 * DIM), grad_gains, grad_qkv, grad_out, grad_up, grad_down, grad_table)


def solution(mesh):
    sizes = (mesh.shape["lat"], mesh.shape["lon"])

    def program(*arguments):
        return on_device(sizes, *arguments)

    fields, tables = P("lat", "lon", None), P(None, "lat", None, None)
    return jax.shard_map(
        program,
        mesh=mesh,
        in_specs=(fields, fields, P(), P(), P(), P(), P(), tables),
        out_specs=(fields, fields, P(), P(), P(), P(), P(), tables),
        check_vma=False,
    )
```

```python
import math

import jax
import jax.numpy as jnp
import numpy as np
from jax import lax
from jax.experimental import pallas as pl
from jax.experimental.pallas import tpu as pltpu
from jax.sharding import PartitionSpec as P

DIM = 192
HEADS = 6
HEAD_DIM = 32
UNITS = 768
ROWS = 6
COLS = 48
WIN_COLS = 12
WINDOWS = 4
WIN_TOK = 144
TOKENS = 576
GRID = ROWS * COLS
GROUP = 12
SPAN = 23
WIDE = SPAN * GROUP
CELL = 6 * SPAN
TABLE = 24 * CELL
QLANES = HEADS * WIN_TOK
STRIP = 32
SOURCE = 288 + 2 * STRIP
NORM_EPS = 1e-05
MASK_VALUE = -100.0
LOG2E = math.log2(math.e)
SCALE = 1.0 / math.sqrt(HEAD_DIM)
WBLOCK = 18 * DIM
CHUNK = 448
HALF = 8 * CHUNK
TCHUNK = 64
TROWS = 208

F32 = jnp.float32
BF16 = jnp.bfloat16


def token_places():
    t = np.arange(TOKENS)
    w, rest = t // WIN_TOK, t % WIN_TOK
    c, l, r = rest // GROUP, rest % GROUP // ROWS, rest % ROWS
    return r, w * WIN_COLS + c, l


def one_hot(places, size):
    return (places[:, None] == np.arange(size)[None, :]).astype(np.float32)


def grid_picker():
    r, j, _ = token_places()
    return one_hot(r * COLS + j, GRID)


def shifted_picker():
    r, j, _ = token_places()
    half = np.where(r < 3, r, r - 3)
    inner = np.where(r < 3, 0, 144) + half * COLS + j + 6
    edge = np.where(r < 3, 288, 288 + STRIP) + half * 6 + j - 42
    return one_hot(np.where(j < 42, inner, edge), SOURCE)


def returned_picker():
    r, j, _ = token_places()
    half = np.where(r >= 3, r - 3, r)
    inner = np.where(r >= 3, 0, 144) + half * COLS + j
    edge = np.where(r >= 3, 288, 288 + STRIP) + half * 6 + j
    return one_hot(np.where(j >= 6, inner, edge), SOURCE)


def strip_picker():
    picked = np.zeros((2 * STRIP, GRID), np.float32)
    for i in range(3):
        for j in range(6):
            picked[i * 6 + j, (i + 3) * COLS + j] = 1
            picked[STRIP + i * 6 + j, i * COLS + j] = 1
    return picked


def table_rows():
    picked = np.zeros((2, HEADS * 16, 24 * 8), np.float32)
    for h in range(HEADS):
        for lq in range(2):
            for lp in range(2):
                for rq in range(6):
                    picked[lp, h * 16 + lq * 6 + rq, (lq * 12 + lp * 6 + rq) * 8 + h] = 1
    return picked


def table_cols():
    picked = np.zeros((2, 6 * SPAN, WIDE), np.float32)
    for lp in range(2):
        for rp in range(6):
            for d in range(SPAN):
                picked[lp, rp * SPAN + d, d * GROUP + lp * 6 + rp] = 1
    return picked


def nn(a, b):
    return jnp.dot(a, b, preferred_element_type=F32)


def nt(a, b):
    return lax.dot_general(a, b, (((1,), (1,)), ((), ())), preferred_element_type=F32)


def tn(a, b):
    return lax.dot_general(a, b, (((0,), (0,)), ((), ())), preferred_element_type=F32)


def level_mask():
    t = lax.broadcasted_iota(jnp.int32, (TOKENS, DIM), 0)
    return (lax.div(t, 6) & 1) == 1


def gather_tokens(picker, source):
    both = nn(picker, source)
    return jnp.where(level_mask(), both[:, DIM:], both[:, :DIM])


def scatter_tokens(picker, tokens):
    upper = level_mask()
    zero = jnp.zeros_like(tokens)
    both = jnp.concatenate([jnp.where(upper, zero, tokens), jnp.where(upper, tokens, zero)], axis=1)
    return tn(picker, both.astype(BF16))


def normalize(x):
    centre = jnp.mean(x, axis=-1, keepdims=True)
    off = x - centre
    spread = jnp.mean(off * off, axis=-1, keepdims=True)
    inv = lax.rsqrt(spread + NORM_EPS)
    return off * inv, inv


def norm_backward(grad, gain, hat, inv):
    scaled = grad * gain
    mean_one = jnp.mean(scaled, axis=-1, keepdims=True)
    mean_two = jnp.mean(scaled * hat, axis=-1, keepdims=True)
    return inv * (scaled - mean_one - hat * mean_two)


def gelu_parts(x):
    bell = jnp.exp2(x * x * (-0.5 * LOG2E))
    t = 1.0 / (1.0 + (0.3275911 * math.sqrt(0.5)) * jnp.abs(x))
    poly = t * (0.254829592 + t * (-0.284496736 + t * (1.421413741 + t * (-1.453152027 + t * 1.061405429))))
    tail = 0.5 * poly * bell
    below = jnp.where(x >= 0, 1.0 - tail, tail)
    return below, bell * (1.0 / math.sqrt(2.0 * math.pi))


def head_rows():
    lane = lax.div(lax.broadcasted_iota(jnp.int32, (1, DIM), 1), HEAD_DIM)
    return [(lane == h) for h in range(HEADS)]


def stack_heads(x, masks):
    return jnp.concatenate([jnp.where(m, x, jnp.zeros_like(x)) for m in masks], axis=0)


def fold_heads(x, masks):
    folded = x[:WIN_TOK]
    for h in range(1, HEADS):
        folded = jnp.where(masks[h], x[h * WIN_TOK : (h + 1) * WIN_TOK], folded)
    return folded


def expand_table(table_ref, trows_ref, tcols_ref, bias_ref):
    table = jnp.concatenate([table_ref[h] for h in range(HEADS)] + [jnp.zeros((2, TABLE), F32)], axis=0) * LOG2E
    table = jnp.concatenate([table[:, k * CELL : (k + 1) * CELL] for k in range(24)], axis=0)
    high = table.astype(BF16)
    low = (table - high.astype(F32)).astype(BF16)
    wide = jnp.zeros((HEADS * 16, WIDE), F32)
    for lp in range(2):
        for part in (high, low):
            wide += nn(nn(trows_ref[lp], part).astype(BF16), tcols_ref[lp])
    for cq in range(WIN_COLS):
        start = GROUP * (WIN_COLS - 1 - cq)
        row = jnp.concatenate(
            [wide[h * 16 : h * 16 + GROUP, start : start + WIN_TOK] for h in range(HEADS)], axis=1
        )
        bias_ref[cq * GROUP : (cq + 1) * GROUP, :] = row


def add_mask(bias_ref, flag):
    key = lax.broadcasted_iota(jnp.int32, (WIN_TOK, 1), 0)
    query = lax.broadcasted_iota(jnp.int32, (1, QLANES), 1)
    key_up = (lax.div(key, 3) & 1).astype(F32)
    query_up = (lax.div(query, 3) & 1).astype(F32)
    apart = jnp.abs(key_up - query_up)
    bias_ref[...] += apart * (flag * (MASK_VALUE * LOG2E))


def collapse_table(grad_ref, trows_ref, tcols_ref):
    parts = []
    for h in range(HEADS):
        total = None
        for cq in range(WIN_COLS):
            start = GROUP * (WIN_COLS - 1 - cq)
            piece = grad_ref[cq * GROUP : (cq + 1) * GROUP, h * WIN_TOK : (h + 1) * WIN_TOK]
            pads = [jnp.zeros((GROUP, start), F32)] if start else []
            tail = WIDE - start - WIN_TOK
            pads_after = [jnp.zeros((GROUP, tail), F32)] if tail else []
            piece = jnp.concatenate(pads + [piece] + pads_after, axis=1)
            total = piece if total is None else total + piece
        parts.append(jnp.concatenate([total, jnp.zeros((16 - GROUP, WIDE), F32)], axis=0))
    wide = jnp.concatenate(parts, axis=0).astype(BF16)
    result = jnp.zeros((24 * 8, CELL), F32)
    for lp in range(2):
        narrow = nt(wide, tcols_ref[lp]).astype(BF16)
        result += tn(trows_ref[lp], narrow)
    cells = [result[k * 8 : (k + 1) * 8] for k in range(24)] + [jnp.zeros((8, 26 * 128 - TABLE), F32)]
    flat = jnp.concatenate(cells, axis=1)
    return jnp.concatenate([flat[:, j * 128 : (j + 1) * 128] for j in range(26)], axis=0).astype(BF16)


def attention(q_ref, k_ref, v_ref, bias_ref, probs_ref, ctx_ref, masks):
    for w in range(WINDOWS):
        rows = pl.ds(w * WIN_TOK, WIN_TOK)
        stacked = stack_heads(q_ref[rows, :], masks)
        scores = nt(k_ref[rows, :], stacked) * (SCALE * LOG2E) + bias_ref[...]
        weights = jnp.exp2(scores)
        inverse = 1.0 / jnp.sum(weights, axis=0, keepdims=True)
        probs = (weights * inverse).astype(BF16)
        probs_ref[w] = probs
        ctx_ref[rows, :] = fold_heads(tn(probs, v_ref[rows, :]), masks).astype(BF16)


def attention_back(q_ref, k_ref, v_ref, probs_ref, gctx_ref, dq_ref, dk_ref, dv_ref, grad_ref, masks):
    for w in range(WINDOWS):
        rows = pl.ds(w * WIN_TOK, WIN_TOK)
        stacked_g = stack_heads(gctx_ref[rows, :], masks)
        stacked_q = stack_heads(q_ref[rows, :], masks)
        probs_half = probs_ref[w]
        probs = probs_half.astype(F32)
        grad_probs = nt(v_ref[rows, :], stacked_g)
        inner = jnp.sum(grad_probs * probs, axis=0, keepdims=True)
        grad_scores = probs * (grad_probs - inner)
        if w == 0:
            grad_ref[...] = grad_scores
        else:
            grad_ref[...] += grad_scores
        half = grad_scores.astype(BF16)
        dv_ref[rows, :] = nn(probs_half, stacked_g).astype(BF16)
        dk_ref[rows, :] = (nn(half, stacked_q) * SCALE).astype(BF16)
        dq_ref[rows, :] = (fold_heads(tn(half, k_ref[rows, :]), masks) * SCALE).astype(BF16)


def project(normed, qkv_ref, q_ref, k_ref, v_ref):
    for i, ref in enumerate((q_ref, k_ref, v_ref)):
        ref[...] = nn(normed, qkv_ref[:, i * DIM : (i + 1) * DIM]).astype(BF16)


def put_weights(wbuf_ref, offset, value):
    tiles = value.shape[1] // 128
    for j in range(tiles):
        wbuf_ref[(offset + j) * DIM : (offset + j + 1) * DIM, :] = value[:, j * 128 : (j + 1) * 128].astype(BF16)


def weight_grads(wbuf_ref, normed, dq, dk, dv, ctx, gbranch, normed_mlp, gpre_ref, expanded_ref, g):
    for j in range(3):
        cols = slice(j * 256, (j + 1) * 256)
        put_weights(wbuf_ref, 2 * j, tn(normed_mlp, gpre_ref[:, cols]))
        put_weights(wbuf_ref, 6 + 2 * j, tn(g, expanded_ref[:, cols]))
    put_weights(wbuf_ref, 12, tn(normed, jnp.concatenate([dq, dk], axis=1)))
    put_weights(wbuf_ref, 15, jnp.concatenate([tn(normed, dv), tn(ctx, gbranch)], axis=1))


def attention_backward_part(
    x, gain, qkv_ref, out_ref, ghid, q_ref, k_ref, v_ref, probs_ref, ctx_ref, gctx_ref, dq_ref, dk_ref, dv_ref, grad_ref, masks
):
    gbranch = ghid.astype(BF16)
    gctx_ref[...] = nt(gbranch, out_ref[...]).astype(BF16)
    attention_back(q_ref, k_ref, v_ref, probs_ref, gctx_ref, dq_ref, dk_ref, dv_ref, grad_ref, masks)
    gnormed = nt(dq_ref[...], qkv_ref[:, :DIM])
    gnormed += nt(dk_ref[...], qkv_ref[:, DIM : 2 * DIM])
    gnormed += nt(dv_ref[...], qkv_ref[:, 2 * DIM :])
    gnormed = gnormed.astype(BF16).astype(F32)
    hat, inv = normalize(x)
    gain_grad = jnp.sum(gnormed * hat, axis=0, keepdims=True)
    gblock = norm_backward(gnormed, gain, hat, inv) + ghid
    normed = (hat * gain).astype(BF16)
    return gblock, normed, gbranch, gain_grad


def first_attention(
    far_x, far_pick, far_gains, far_qkv, far_table, far_trows, far_tcols, far_out,
    xw_ref, q_ref, k_ref, v_ref, probs_ref, ctx_ref, hidden_ref,
    bias_ref, x_ref, pick_ref, gains_ref, qkv_ref, table_ref, trows_ref, tcols_ref, out_ref, sems,
):
    pairs = [
        (far_x, x_ref), (far_pick, pick_ref), (far_gains.at[0], gains_ref), (far_qkv.at[0], qkv_ref),
        (far_table.at[pl.ds(0, HEADS)], table_ref), (far_trows, trows_ref), (far_tcols, tcols_ref), (far_out.at[0], out_ref),
    ]
    fetches = [pltpu.make_async_copy(far, near, sems.at[i]) for i, (far, near) in enumerate(pairs)]
    for fetch in fetches:
        fetch.start()
    for fetch in fetches[:4]:
        fetch.wait()
    x = gather_tokens(pick_ref[...], x_ref[...])
    xw_ref[...] = x.astype(BF16)
    hat, _ = normalize(x)
    project((hat * gains_ref[0:1, :]).astype(BF16), qkv_ref, q_ref, k_ref, v_ref)
    for fetch in fetches[4:]:
        fetch.wait()
    expand_table(table_ref, trows_ref, tcols_ref, bias_ref)
    attention(q_ref, k_ref, v_ref, bias_ref, probs_ref, ctx_ref, head_rows())
    branch = nn(ctx_ref[...], out_ref[...]).astype(BF16)
    hidden_ref[...] = xw_ref[...].astype(F32) + branch.astype(F32)


def first_mlp(
    hidden_ref, cot_ref, gains_ref, up_ref, down_ref, pick_ref, strips_ref,
    expanded_ref, slope_ref, bottom_ref, row_ref, side_ref, corner_ref,
):
    row_ref[144:, :] = cot_ref[:144, :]
    edges = nn(strips_ref[...], cot_ref[...]).astype(BF16)
    side_ref[STRIP:, :] = edges[:STRIP]
    corner_ref[STRIP:, :] = edges[STRIP:]
    hidden = hidden_ref[...]
    hat, _ = normalize(hidden)
    normed_mlp = (hat * gains_ref[1:2, :]).astype(BF16)
    total = hidden
    for j in range(3):
        cols = slice(j * 256, (j + 1) * 256)
        pre = nn(normed_mlp, up_ref[:, cols])
        below, density = gelu_parts(pre)
        expanded = (pre * below).astype(BF16)
        expanded_ref[:, cols] = expanded
        slope_ref[:, cols] = (below + pre * density).astype(BF16)
        total = total + nt(expanded, down_ref[:, cols])
    grid = scatter_tokens(pick_ref[...], total.astype(BF16)).astype(BF16)
    row_ref[:144, :] = grid[:144]
    bottom_ref[...] = grid[144:]
    edges = nn(strips_ref[...], grid).astype(BF16)
    side_ref[:STRIP, :] = edges[:STRIP]
    corner_ref[:STRIP, :] = edges[STRIP:]


def fill_source(source_ref, own, row_ref, side_ref, corner_ref, part):
    source_ref[0:144, :] = own
    source_ref[144:288, :] = row_ref[part * 144 : (part + 1) * 144, :]
    source_ref[288 : 288 + STRIP, :] = side_ref[part * STRIP : (part + 1) * STRIP, :]
    source_ref[288 + STRIP :, :] = corner_ref[part * STRIP : (part + 1) * STRIP, :]


def put_source(own_ref, row_ref, side_ref, corner_ref, part, value):
    own_ref[...] = value[0:144]
    row_ref[part * 144 : (part + 1) * 144, :] = value[144:288]
    side_ref[part * STRIP : (part + 1) * STRIP, :] = value[288 : 288 + STRIP]
    corner_ref[part * STRIP : (part + 1) * STRIP, :] = value[288 + STRIP :]


def second_bias(table_ref, trows_ref, tcols_ref, bias_ref):
    expand_table(table_ref, trows_ref, tcols_ref, bias_ref)
    add_mask(bias_ref, (lax.axis_index("lat") == lax.axis_size("lat") - 1).astype(F32))


def second_both(
    own_ref, row_ref, side_ref, corner_ref, cot_ref, bias_ref,
    gains_ref, qkv_ref, out_ref, up_ref, down_ref, pick_ref,
    back_own_ref, y_own_ref, sent_row_ref, sent_side_ref, sent_corner_ref,
    g_ref, normed_ref, dq_ref, dk_ref, dv_ref, ctx_ref, gbranch_ref, normed_mlp_ref, gpre_ref, expanded_ref, grad_ref, gain_grad_ref,
    source_ref, x_ref, q_ref, k_ref, v_ref, probs_ref, gctx_ref,
):
    masks = head_rows()
    fill_source(source_ref, own_ref[...], row_ref, side_ref, corner_ref, 0)
    x_ref[...] = gather_tokens(pick_ref[...], source_ref[...])
    fill_source(source_ref, cot_ref[144:288, :], row_ref, side_ref, corner_ref, 1)
    g_ref[...] = gather_tokens(pick_ref[...], source_ref[...]).astype(BF16)
    hat, _ = normalize(x_ref[...])
    project((hat * gains_ref[0:1, :]).astype(BF16), qkv_ref, q_ref, k_ref, v_ref)
    attention(q_ref, k_ref, v_ref, bias_ref, probs_ref, ctx_ref, masks)
    branch = nn(ctx_ref[...], out_ref[...]).astype(BF16)
    hidden = x_ref[...] + branch.astype(F32)
    hat_mlp, inv_mlp = normalize(hidden)
    normed_mlp = (hat_mlp * gains_ref[1:2, :]).astype(BF16)
    normed_mlp_ref[...] = normed_mlp
    total = hidden
    gnormed = jnp.zeros((TOKENS, DIM), F32)
    for j in range(3):
        cols = slice(j * 256, (j + 1) * 256)
        pre = nn(normed_mlp, up_ref[:, cols])
        below, density = gelu_parts(pre)
        expanded = (pre * below).astype(BF16)
        expanded_ref[:, cols] = expanded
        total = total + nt(expanded, down_ref[:, cols])
        gact = nn(g_ref[...], down_ref[:, cols]).astype(BF16).astype(F32)
        gpre = ((below + pre * density) * gact).astype(BF16)
        gpre_ref[:, cols] = gpre
        gnormed = gnormed + nt(gpre, up_ref[:, cols])
    y = scatter_tokens(pick_ref[...], total.astype(BF16)).astype(BF16)
    put_source(y_own_ref, sent_row_ref, sent_side_ref, sent_corner_ref, 1, y)
    gnormed = gnormed.astype(BF16).astype(F32)
    gain_grad_ref[1:2, :] = jnp.sum(gnormed * hat_mlp, axis=0, keepdims=True)
    ghid = g_ref[...].astype(F32) + norm_backward(gnormed, gains_ref[1:2, :], hat_mlp, inv_mlp)
    gblock, normed, gbranch, gain_grad = attention_backward_part(
        x_ref[...], gains_ref[0:1, :], qkv_ref, out_ref, ghid,
        q_ref, k_ref, v_ref, probs_ref, ctx_ref, gctx_ref, dq_ref, dk_ref, dv_ref, grad_ref, masks,
    )
    gain_grad_ref[0:1, :] = gain_grad
    back = scatter_tokens(pick_ref[...], gblock.astype(BF16)).astype(BF16)
    put_source(back_own_ref, sent_row_ref, sent_side_ref, sent_corner_ref, 0, back)
    normed_ref[...] = normed
    gbranch_ref[...] = gbranch


def second_weights(
    normed_ref, dq_ref, dk_ref, dv_ref, ctx_ref, gbranch_ref, normed_mlp_ref, gpre_ref, expanded_ref, grad_ref, g_ref,
    trows_ref, tcols_ref, wbuf_ref, table_grad_ref,
):
    weight_grads(
        wbuf_ref, normed_ref[...], dq_ref[...], dk_ref[...], dv_ref[...], ctx_ref[...], gbranch_ref[...],
        normed_mlp_ref[...], gpre_ref, expanded_ref, g_ref[...],
    )
    table_grad_ref[...] = collapse_table(grad_ref, trows_ref, tcols_ref)


def first_mlp_back(
    back_ref, row_ref, side_ref, corner_ref, hidden_ref, slope_ref, gains_ref, up_ref, down_ref, returned_ref,
    g_ref, ghid_ref, normed_mlp_ref, gpre_ref, gain_grad_ref, source_ref,
):
    fill_source(source_ref, back_ref[...], row_ref, side_ref, corner_ref, 0)
    g32 = gather_tokens(returned_ref[...], source_ref[...])
    g = g32.astype(BF16)
    g_ref[...] = g
    hat_mlp, inv_mlp = normalize(hidden_ref[...])
    normed_mlp_ref[...] = (hat_mlp * gains_ref[1:2, :]).astype(BF16)
    gnormed = jnp.zeros((TOKENS, DIM), F32)
    for j in range(3):
        cols = slice(j * 256, (j + 1) * 256)
        gact = nn(g, down_ref[:, cols]).astype(BF16).astype(F32)
        gpre = (slope_ref[:, cols].astype(F32) * gact).astype(BF16)
        gpre_ref[:, cols] = gpre
        gnormed = gnormed + nt(gpre, up_ref[:, cols])
    gnormed = gnormed.astype(BF16).astype(F32)
    gain_grad_ref[...] = jnp.sum(gnormed * hat_mlp, axis=0, keepdims=True)
    ghid_ref[...] = g32 + norm_backward(gnormed, gains_ref[1:2, :], hat_mlp, inv_mlp)


def first_attention_back(
    ghid_ref, g_ref, normed_mlp_ref, gpre_ref, mlp_gain_ref, xw_ref, q_ref, k_ref, v_ref, probs_ref, ctx_ref, expanded_ref,
    gains_ref, qkv_ref, out_ref, trows_ref, tcols_ref, pick_ref, last_wbuf_ref, last_gain_ref, last_table_ref,
    gin_ref, mine_ref, theirs_ref, tables_ref,
    gctx_ref, dq_ref, dk_ref, dv_ref, grad_ref, wbuf_ref, sems,
):
    masks = head_rows()
    fetch = pltpu.make_async_copy(last_wbuf_ref, wbuf_ref.at[pl.ds(WBLOCK, WBLOCK), :], sems.at[0])
    fetch.start()
    gblock, normed, gbranch, gain_grad = attention_backward_part(
        xw_ref[...].astype(F32), gains_ref[0:1, :], qkv_ref, out_ref, ghid_ref[...],
        q_ref, k_ref, v_ref, probs_ref, ctx_ref, gctx_ref, dq_ref, dk_ref, dv_ref, grad_ref, masks,
    )
    gin_ref[...] = scatter_tokens(pick_ref[...], gblock.astype(BF16)).astype(BF16)
    weight_grads(
        wbuf_ref, normed, dq_ref[...], dk_ref[...], dv_ref[...], ctx_ref[...], gbranch,
        normed_mlp_ref[...], gpre_ref, expanded_ref, g_ref[...],
    )
    tables_ref[0:TROWS, :] = collapse_table(grad_ref, trows_ref, tcols_ref)
    tables_ref[TROWS : 2 * TROWS, :] = last_table_ref[...]
    tables_ref[2 * TROWS :, :] = jnp.zeros((8 * TCHUNK - 2 * TROWS, 128), BF16)
    gains = jnp.concatenate([gain_grad, mlp_gain_ref[...], last_gain_ref[0:1, :], last_gain_ref[1:2, :]], axis=1)
    wbuf_ref[2 * WBLOCK :, :] = jnp.zeros((2 * HALF - 2 * WBLOCK, 128), BF16)
    for j in range(6):
        tile = jnp.concatenate([gains[:, j * 128 : (j + 1) * 128], jnp.zeros((15, 128), F32)], axis=0)
        wbuf_ref[2 * WBLOCK + j * 16 : 2 * WBLOCK + (j + 1) * 16, :] = tile.astype(BF16)
    fetch.wait()
    core = lax.rem(lax.axis_index("lat"), 2)
    keep = pltpu.make_async_copy(wbuf_ref.at[pl.ds(core * HALF, HALF), :], mine_ref, sems.at[1])
    send = pltpu.make_async_copy(wbuf_ref.at[pl.ds((1 - core) * HALF, HALF), :], theirs_ref, sems.at[2])
    send.start()
    keep.start()
    send.wait()
    keep.wait()


def pack_core(mine_ref, other_ref, tables_ref, packed_ref):
    for j in range(8):
        rows = slice(j * CHUNK, (j + 1) * CHUNK)
        total = mine_ref[rows, :].astype(F32) + other_ref[rows, :].astype(F32)
        packed_ref[j, 0:CHUNK, :] = total.astype(BF16)
        packed_ref[j, CHUNK:, :] = tables_ref[j * TCHUNK : (j + 1) * TCHUNK, :]


def sum_eight(ref, rows):
    total = ref[0, rows, :].astype(F32)
    for j in range(1, 8):
        total += ref[j, rows, :].astype(F32)
    return total.astype(BF16)


def sum_lon(parts_ref, spread_ref, table_ref):
    total = sum_eight(parts_ref, slice(0, CHUNK))
    for j in range(8):
        spread_ref[j] = total
    table_ref[...] = sum_eight(parts_ref, slice(CHUNK, CHUNK + TCHUNK))


def sum_lat(parts_ref, table_ref, spread_ref):
    total = sum_eight(parts_ref, slice(0, CHUNK))
    for j in range(8):
        spread_ref[j, 0:CHUNK, :] = total
        spread_ref[j, CHUNK:, :] = table_ref[...]


def unpack(mine_ref, other_ref, qkv_ref, out_ref, up_ref, down_ref, gains_ref, table_ref):
    core = lax.rem(lax.axis_index("lat"), 2)

    def load(start, count):
        pieces = []
        while count:
            half, place = divmod(start, HALF)
            j, place = divmod(place, CHUNK)
            size = min(count, CHUNK - place)
            here = mine_ref[j, place : place + size, :].astype(F32)
            there = other_ref[j, place : place + size, :].astype(F32)
            pieces.append(jnp.where(core == half, here, there))
            start, count = start + size, count - size
        return pieces[0] if len(pieces) == 1 else jnp.concatenate(pieces, axis=0)

    for b in range(2):
        for j in range(18):
            tile = load(b * WBLOCK + j * DIM, DIM)
            if j < 6:
                up_ref[b, :, j * 128 : (j + 1) * 128] = tile
            elif j < 12:
                down_ref[b, :, (j - 6) * 128 : (j - 5) * 128] = tile
            elif j < 16:
                qkv_ref[b, :, (j - 12) * 128 : (j - 11) * 128] = tile
            elif j == 16:
                qkv_ref[b, :, 512:576] = tile[:, :64]
                out_ref[b, :, 0:64] = tile[:, 64:]
            else:
                out_ref[b, :, 64:192] = tile
        for j in range(26):
            k, place = divmod(b * TROWS + j * 8, TCHUNK)
            base = CHUNK + place // 16 * 16
            pair = mine_ref[k, base : base + 16, :].astype(F32)
            piece = pair[place % 16 : place % 16 + HEADS]
            width = min(128, TABLE - j * 128)
            for h in range(HEADS):
                table_ref[b * HEADS + h, :, j * 128 : j * 128 + width] = piece[h : h + 1, :width]
    gains = jnp.concatenate([load(2 * WBLOCK + j * 16, 16)[0:1] for j in range(6)], axis=1)
    for b in range(2):
        for i in range(2):
            k = b * 2 + i
            gains_ref[b, i : i + 1, :] = gains[:, k * DIM : (k + 1) * DIM]


def whole(array):
    return pl.BlockSpec(array.shape, lambda i: (0,) * array.ndim)


def picked(array, index):
    rest = array.shape[1:]
    return pl.BlockSpec((None,) + rest, lambda i: (index,) + (0,) * len(rest))


def in_place():
    return pl.BlockSpec(memory_space=pl.ANY)


def call(kernel, operands, specs, outs, scratch=(), micros=2, out_specs=None, mebibytes=10):
    shapes = [jax.ShapeDtypeStruct(shape, dtype) for shape, dtype in outs]
    moved = sum(a.size * a.dtype.itemsize for a in (*operands, *shapes))
    return pl.pallas_call(
        kernel,
        grid=(1,),
        out_shape=shapes,
        in_specs=specs,
        out_specs=out_specs or [whole(s) for s in shapes],
        scratch_shapes=list(scratch),
        cost_estimate=pl.CostEstimate(flops=micros * 1_100_000_000, bytes_accessed=moved, transcendentals=0),
        compiler_params=pltpu.CompilerParams(vmem_limit_bytes=mebibytes * 1024 * 1024),
    )(*operands)


def neighbour(sizes, steps):
    pairs = []
    for a in range(sizes[0]):
        for b in range(sizes[1]):
            source = ((a + steps[0]) % sizes[0]) * sizes[1] + (b + steps[1]) % sizes[1]
            pairs.append((source, a * sizes[1] + b))
    return pairs


def exchange(rows, side, corner, sizes, step):
    both = ("lat", "lon")
    rows = lax.ppermute(rows, both, neighbour(sizes, (step, 0)))
    side = lax.ppermute(side, both, neighbour(sizes, (0, step)))
    corner = lax.ppermute(corner, both, neighbour(sizes, (step, step)))
    return rows, side, corner


def vmem(shape, dtype):
    return pltpu.VMEM(shape, dtype)


def sum_over_devices(mine, theirs, tables, sizes):
    pairs = [(i ^ 1, i) for i in range(sizes[0])]
    groups = [[core + 2 * k for k in range(sizes[0] // 2)] for core in range(2)]
    other = lax.ppermute(theirs, "lat", pairs)
    packed = (8, CHUNK + TCHUNK, 128)
    [sent] = call(pack_core, [mine, other, tables], [whole(a) for a in (mine, other, tables)], [(packed, BF16)])
    parts = lax.all_to_all(sent, "lon", 0, 0)
    spread, table = call(sum_lon, [parts], [whole(parts)], [((8, CHUNK, 128), BF16), ((TCHUNK, 128), BF16)])
    parts = lax.all_to_all(spread, "lat", 0, 0, axis_index_groups=groups)
    [spread] = call(sum_lat, [parts, table], [whole(parts), whole(table)], [(packed, BF16)])
    half = lax.all_to_all(spread, "lon", 0, 0)
    other = lax.ppermute(half, "lat", pairs)
    outs = [((2, DIM, 3 * DIM), F32), ((2, DIM, DIM), F32), ((2, DIM, UNITS), F32), ((2, DIM, UNITS), F32)]
    outs += [((2, 2, DIM), F32), ((2 * HEADS, 1, TABLE), F32)]
    return call(unpack, [half, other], [whole(half), whole(other)], outs)


def on_device(sizes, inputs, cotangent, norm_gains, qkv_weight, out_weight, up_weight, down_weight, bias_table):
    x = inputs.reshape(GRID, 2 * DIM)
    cot = cotangent.reshape(GRID, 2 * DIM)
    trows, tcols = jnp.asarray(table_rows(), BF16), jnp.asarray(table_cols(), BF16)
    pick_grid, pick_shift, pick_back = (
        jnp.asarray(m, BF16) for m in (grid_picker(), shifted_picker(), returned_picker())
    )
    strips = jnp.asarray(strip_picker(), BF16)
    weights = (norm_gains, qkv_weight, out_weight, up_weight, jnp.swapaxes(down_weight, 1, 2))
    tok, src, hid = (TOKENS, DIM), (SOURCE, 2 * DIM), (TOKENS, UNITS)
    probs = (WINDOWS, WIN_TOK, QLANES)

    def table_spec(index):
        return pl.BlockSpec((HEADS, 1, TABLE), lambda i: (index, 0, 0))

    bias_table = bias_table.reshape(2 * HEADS, 1, TABLE)
    gains, qkv, out, up, down = weights
    wide_tok, wide_hid = (tok, BF16), (hid, BF16)
    bias = (WIN_TOK, QLANES)

    def specs_for(arrays, index):
        specs = []
        for a in arrays:
            if any(a is w for w in weights):
                specs.append(picked(a, index))
            elif a is bias_table:
                specs.append(table_spec(index))
            else:
                specs.append(whole(a))
        return specs

    operands = [x, pick_grid, gains, qkv, bias_table, trows, tcols, out]
    outs = [wide_tok] * 4 + [(probs, BF16), wide_tok, (tok, F32)]
    scratch = [vmem(bias, F32), vmem(x.shape, BF16), vmem(pick_grid.shape, BF16), vmem((2, DIM), F32), vmem((DIM, 3 * DIM), BF16)]
    scratch += [vmem((HEADS, 1, TABLE), F32), vmem(trows.shape, BF16), vmem(tcols.shape, BF16), vmem((DIM, DIM), BF16)]
    scratch += [pltpu.SemaphoreType.DMA((8,))]
    operands = [pltpu.with_memory_space_constraint(a, pltpu.HBM) for a in operands]
    specs = [in_place()] * 8
    results = call(first_attention, operands, specs, outs, scratch, 7, mebibytes=14)
    xw, q, k, v, probs_first, ctx, hidden = results

    operands = [hidden, cot, gains, up, down, pick_grid, strips]
    strip_outs = [((288, 2 * DIM), BF16), ((2 * STRIP, 2 * DIM), BF16), ((2 * STRIP, 2 * DIM), BF16)]
    outs = [wide_hid, wide_hid, ((144, 2 * DIM), BF16)] + strip_outs
    results = call(first_mlp, operands, specs_for(operands, 0), outs, (), 4, mebibytes=14)
    expanded, slope, bottom, *sent = results
    sent, bias_table = lax.optimization_barrier((sent, bias_table))

    arrived = exchange(*sent, sizes, 1)
    operands = [bias_table, trows, tcols]
    [bias_last] = call(second_bias, operands, specs_for(operands, 1), [(bias, F32)], (), 2, mebibytes=14)

    operands = [bottom, *arrived, cot, bias_last, *weights, pick_shift]
    outs = [((144, 2 * DIM), BF16)] * 2 + strip_outs + [wide_tok] * 8 + [wide_hid] * 2 + [(bias, F32), ((2, DIM), F32)]
    scratch = [vmem(src, BF16), vmem(tok, F32)] + [vmem(tok, BF16)] * 3 + [vmem(probs, BF16), vmem(tok, BF16)]
    results = call(second_both, operands, specs_for(operands, 1), outs, scratch, 12, mebibytes=14)
    back_own, y_own, sent, terms, last_gain = results[0], results[1], results[2:5], results[5:16], results[16]

    arrived = exchange(*sent, sizes, -1)
    g, *terms = terms
    operands = [*terms, g, trows, tcols]
    outs = [((WBLOCK, 128), BF16), ((TROWS, 128), BF16)]
    last_wbuf, last_table = call(second_weights, operands, specs_for(operands, 1), outs, (), 4, mebibytes=14)

    operands = [back_own, *arrived, hidden, slope, gains, up, down, pick_back]
    outs = [wide_tok, (tok, F32), wide_tok, wide_hid, ((1, DIM), F32)]
    results = call(first_mlp_back, operands, specs_for(operands, 0), outs, [vmem(src, BF16)], 3, mebibytes=14)
    g, ghid, normed_mlp, gpre, mlp_gain = results

    operands = [ghid, g, normed_mlp, gpre, mlp_gain, xw, q, k, v, probs_first, ctx, expanded, gains, qkv, out]
    operands += [trows, tcols, pick_grid, last_wbuf, last_gain, last_table]
    specs = specs_for(operands, 0)
    specs[-3] = in_place()
    outs = [((GRID, 2 * DIM), BF16), ((HALF, 128), BF16), ((HALF, 128), BF16), ((8 * TCHUNK, 128), BF16)]
    out_specs = [pl.BlockSpec((GRID, 2 * DIM), lambda i: (0, 0)), in_place(), in_place()]
    out_specs += [pl.BlockSpec((8 * TCHUNK, 128), lambda i: (0, 0))]
    scratch = [vmem(tok, BF16)] * 4 + [vmem(bias, F32), vmem((2 * HALF, 128), BF16), pltpu.SemaphoreType.DMA((3,))]
    grad_inputs, mine, theirs, tables = call(
        first_attention_back, operands, specs, outs, scratch, 8, out_specs, 14
    )

    y_rows, y_side, y_corner = arrived
    rows = jnp.concatenate([y_rows[144:], y_own]).reshape(ROWS, COLS, 2 * DIM)
    edge = jnp.concatenate([a[STRIP : STRIP + 18].reshape(3, 6, 2 * DIM) for a in (y_corner, y_side)])
    output = jnp.concatenate([edge, rows[:, 6:]], axis=1)

    grad_qkv, grad_out, grad_up, grad_down, grad_gains, grad_table = sum_over_devices(mine, theirs, tables, sizes)
    grad_down = jnp.swapaxes(grad_down, 1, 2)
    grad_table = grad_table.reshape(2, 1, HEADS, TABLE)
    return (output, grad_inputs.reshape(ROWS, COLS, 2 * DIM), grad_gains, grad_qkv, grad_out, grad_up, grad_down, grad_table)


def solution(mesh):
    sizes = (mesh.shape["lat"], mesh.shape["lon"])

    def program(*arguments):
        return on_device(sizes, *arguments)

    fields, tables = P("lat", "lon", None), P(None, "lat", None, None)
    return jax.shard_map(
        program,
        mesh=mesh,
        in_specs=(fields, fields, P(), P(), P(), P(), P(), tables),
        out_specs=(fields, fields, P(), P(), P(), P(), P(), tables),
        check_vma=False,
    )
```

```python
import math

import jax
import jax.numpy as jnp
import numpy as np
from jax import lax
from jax.experimental import pallas as pl
from jax.experimental.pallas import tpu as pltpu
from jax.sharding import PartitionSpec as P

DIM = 192
HEADS = 6
HEAD_DIM = 32
UNITS = 768
ROWS = 6
COLS = 48
WIN_COLS = 12
WINDOWS = 4
WIN_TOK = 144
TOKENS = 576
GRID = ROWS * COLS
GROUP = 12
SPAN = 23
WIDE = SPAN * GROUP
CELL = 6 * SPAN
TABLE = 24 * CELL
QLANES = HEADS * WIN_TOK
STRIP = 32
SOURCE = 288 + 2 * STRIP
NORM_EPS = 1e-05
MASK_VALUE = -100.0
LOG2E = math.log2(math.e)
SCALE = 1.0 / math.sqrt(HEAD_DIM)
WBLOCK = 18 * DIM
CHUNK = 224
HALF = 16 * CHUNK
PART = 9 * DIM
EXTRA = HALF - 2 * PART
TROWS = 208

F32 = jnp.float32
BF16 = jnp.bfloat16


def token_places():
    t = np.arange(TOKENS)
    w, rest = t // WIN_TOK, t % WIN_TOK
    c, l, r = rest // GROUP, rest % GROUP // ROWS, rest % ROWS
    return r, w * WIN_COLS + c, l


def one_hot(places, size):
    return (places[:, None] == np.arange(size)[None, :]).astype(np.float32)


def grid_picker():
    r, j, _ = token_places()
    return one_hot(r * COLS + j, GRID)


def shifted_picker():
    r, j, _ = token_places()
    half = np.where(r < 3, r, r - 3)
    inner = np.where(r < 3, 0, 144) + half * COLS + j + 6
    edge = np.where(r < 3, 288, 288 + STRIP) + half * 6 + j - 42
    return one_hot(np.where(j < 42, inner, edge), SOURCE)


def returned_picker():
    r, j, _ = token_places()
    half = np.where(r >= 3, r - 3, r)
    inner = np.where(r >= 3, 0, 144) + half * COLS + j
    edge = np.where(r >= 3, 288, 288 + STRIP) + half * 6 + j
    return one_hot(np.where(j >= 6, inner, edge), SOURCE)


def strip_picker():
    picked = np.zeros((2 * STRIP, GRID), np.float32)
    for i in range(3):
        for j in range(6):
            picked[i * 6 + j, (i + 3) * COLS + j] = 1
            picked[STRIP + i * 6 + j, i * COLS + j] = 1
    return picked


def table_rows():
    picked = np.zeros((2, HEADS * 16, 24 * 8), np.float32)
    for h in range(HEADS):
        for lq in range(2):
            for lp in range(2):
                for rq in range(6):
                    picked[lp, h * 16 + lq * 6 + rq, (lq * 12 + lp * 6 + rq) * 8 + h] = 1
    return picked


def table_cols():
    picked = np.zeros((2, 6 * SPAN, WIDE), np.float32)
    for lp in range(2):
        for rp in range(6):
            for d in range(SPAN):
                picked[lp, rp * SPAN + d, d * GROUP + lp * 6 + rp] = 1
    return picked


def nn(a, b):
    return jnp.dot(a, b, preferred_element_type=F32)


def nt(a, b):
    return lax.dot_general(a, b, (((1,), (1,)), ((), ())), preferred_element_type=F32)


def tn(a, b):
    return lax.dot_general(a, b, (((0,), (0,)), ((), ())), preferred_element_type=F32)


def level_mask():
    t = lax.broadcasted_iota(jnp.int32, (TOKENS, DIM), 0)
    return (lax.div(t, 6) & 1) == 1


def gather_tokens(picker, source):
    both = nn(picker, source)
    return jnp.where(level_mask(), both[:, DIM:], both[:, :DIM])


def scatter_tokens(picker, tokens):
    upper = level_mask()
    zero = jnp.zeros_like(tokens)
    both = jnp.concatenate([jnp.where(upper, zero, tokens), jnp.where(upper, tokens, zero)], axis=1)
    return tn(picker, both.astype(BF16))


def normalize(x):
    centre = jnp.mean(x, axis=-1, keepdims=True)
    off = x - centre
    spread = jnp.mean(off * off, axis=-1, keepdims=True)
    inv = lax.rsqrt(spread + NORM_EPS)
    return off * inv, inv


def norm_backward(grad, gain, hat, inv):
    scaled = grad * gain
    mean_one = jnp.mean(scaled, axis=-1, keepdims=True)
    mean_two = jnp.mean(scaled * hat, axis=-1, keepdims=True)
    return inv * (scaled - mean_one - hat * mean_two)


def gelu_parts(x):
    bell = jnp.exp2(x * x * (-0.5 * LOG2E))
    t = 1.0 / (1.0 + (0.3275911 * math.sqrt(0.5)) * jnp.abs(x))
    poly = t * (0.254829592 + t * (-0.284496736 + t * (1.421413741 + t * (-1.453152027 + t * 1.061405429))))
    tail = 0.5 * poly * bell
    below = jnp.where(x >= 0, 1.0 - tail, tail)
    return below, bell * (1.0 / math.sqrt(2.0 * math.pi))


def head_rows():
    lane = lax.div(lax.broadcasted_iota(jnp.int32, (1, DIM), 1), HEAD_DIM)
    return [(lane == h) for h in range(HEADS)]


def stack_heads(x, masks):
    return jnp.concatenate([jnp.where(m, x, jnp.zeros_like(x)) for m in masks], axis=0)


def fold_heads(x, masks):
    folded = x[:WIN_TOK]
    for h in range(1, HEADS):
        folded = jnp.where(masks[h], x[h * WIN_TOK : (h + 1) * WIN_TOK], folded)
    return folded


def expand_table(table_ref, trows_ref, tcols_ref, bias_ref):
    table = jnp.concatenate([table_ref[h] for h in range(HEADS)] + [jnp.zeros((2, TABLE), F32)], axis=0) * LOG2E
    table = jnp.concatenate([table[:, k * CELL : (k + 1) * CELL] for k in range(24)], axis=0)
    high = table.astype(BF16)
    low = (table - high.astype(F32)).astype(BF16)
    wide = jnp.zeros((HEADS * 16, WIDE), F32)
    for lp in range(2):
        for part in (high, low):
            wide += nn(nn(trows_ref[lp], part).astype(BF16), tcols_ref[lp])
    for cq in range(WIN_COLS):
        start = GROUP * (WIN_COLS - 1 - cq)
        row = jnp.concatenate(
            [wide[h * 16 : h * 16 + GROUP, start : start + WIN_TOK] for h in range(HEADS)], axis=1
        )
        bias_ref[cq * GROUP : (cq + 1) * GROUP, :] = row


def add_mask(bias_ref, flag):
    key = lax.broadcasted_iota(jnp.int32, (WIN_TOK, 1), 0)
    query = lax.broadcasted_iota(jnp.int32, (1, QLANES), 1)
    key_up = (lax.div(key, 3) & 1).astype(F32)
    query_up = (lax.div(query, 3) & 1).astype(F32)
    apart = jnp.abs(key_up - query_up)
    bias_ref[...] += apart * (flag * (MASK_VALUE * LOG2E))


def collapse_table(grad_ref, trows_ref, tcols_ref):
    parts = []
    for h in range(HEADS):
        total = None
        for cq in range(WIN_COLS):
            start = GROUP * (WIN_COLS - 1 - cq)
            piece = grad_ref[cq * GROUP : (cq + 1) * GROUP, h * WIN_TOK : (h + 1) * WIN_TOK]
            pads = [jnp.zeros((GROUP, start), F32)] if start else []
            tail = WIDE - start - WIN_TOK
            pads_after = [jnp.zeros((GROUP, tail), F32)] if tail else []
            piece = jnp.concatenate(pads + [piece] + pads_after, axis=1)
            total = piece if total is None else total + piece
        parts.append(jnp.concatenate([total, jnp.zeros((16 - GROUP, WIDE), F32)], axis=0))
    wide = jnp.concatenate(parts, axis=0).astype(BF16)
    result = jnp.zeros((24 * 8, CELL), F32)
    for lp in range(2):
        narrow = nt(wide, tcols_ref[lp]).astype(BF16)
        result += tn(trows_ref[lp], narrow)
    cells = [result[k * 8 : (k + 1) * 8] for k in range(24)] + [jnp.zeros((8, 26 * 128 - TABLE), F32)]
    flat = jnp.concatenate(cells, axis=1)
    return jnp.concatenate([flat[:, j * 128 : (j + 1) * 128] for j in range(26)], axis=0).astype(BF16)


def attention(q_ref, k_ref, v_ref, bias_ref, probs_ref, ctx_ref, masks):
    for w in range(WINDOWS):
        rows = pl.ds(w * WIN_TOK, WIN_TOK)
        stacked = stack_heads(q_ref[rows, :], masks)
        scores = nt(k_ref[rows, :], stacked) * (SCALE * LOG2E) + bias_ref[...]
        weights = jnp.exp2(scores)
        inverse = 1.0 / jnp.sum(weights, axis=0, keepdims=True)
        probs = (weights * inverse).astype(BF16)
        probs_ref[w] = probs
        ctx_ref[rows, :] = fold_heads(tn(probs, v_ref[rows, :]), masks).astype(BF16)


def attention_back(q_ref, k_ref, v_ref, probs_ref, gctx_ref, dq_ref, dk_ref, dv_ref, grad_ref, masks):
    for w in range(WINDOWS):
        rows = pl.ds(w * WIN_TOK, WIN_TOK)
        stacked_g = stack_heads(gctx_ref[rows, :], masks)
        stacked_q = stack_heads(q_ref[rows, :], masks)
        probs_half = probs_ref[w]
        probs = probs_half.astype(F32)
        grad_probs = nt(v_ref[rows, :], stacked_g)
        inner = jnp.sum(grad_probs * probs, axis=0, keepdims=True)
        grad_scores = probs * (grad_probs - inner)
        if w == 0:
            grad_ref[...] = grad_scores
        else:
            grad_ref[...] += grad_scores
        half = grad_scores.astype(BF16)
        dv_ref[rows, :] = nn(probs_half, stacked_g).astype(BF16)
        dk_ref[rows, :] = (nn(half, stacked_q) * SCALE).astype(BF16)
        dq_ref[rows, :] = (fold_heads(tn(half, k_ref[rows, :]), masks) * SCALE).astype(BF16)


def project(normed, qkv_ref, q_ref, k_ref, v_ref):
    for i, ref in enumerate((q_ref, k_ref, v_ref)):
        ref[...] = nn(normed, qkv_ref[:, i * DIM : (i + 1) * DIM]).astype(BF16)


def put_weights(wbuf_ref, offset, value):
    tiles = value.shape[1] // 128
    for j in range(tiles):
        half, place = divmod(offset + j, 9)
        wbuf_ref[half, place * DIM : (place + 1) * DIM, :] = value[:, j * 128 : (j + 1) * 128].astype(BF16)


def weight_grads(wbuf_ref, normed, dq, dk, dv, ctx, gbranch, normed_mlp, gpre_ref, expanded_ref, g):
    for j in range(3):
        cols = slice(j * 256, (j + 1) * 256)
        put_weights(wbuf_ref, 2 * j, tn(normed_mlp, gpre_ref[:, cols]))
        put_weights(wbuf_ref, 6 + 2 * j, tn(g, expanded_ref[:, cols]))
    put_weights(wbuf_ref, 12, tn(normed, jnp.concatenate([dq, dk], axis=1)))
    put_weights(wbuf_ref, 15, jnp.concatenate([tn(normed, dv), tn(ctx, gbranch)], axis=1))


def attention_backward_part(
    x, gain, qkv_ref, out_ref, ghid, q_ref, k_ref, v_ref, probs_ref, ctx_ref, gctx_ref, dq_ref, dk_ref, dv_ref, grad_ref, masks
):
    gbranch = ghid.astype(BF16)
    gctx_ref[...] = nt(gbranch, out_ref[...]).astype(BF16)
    attention_back(q_ref, k_ref, v_ref, probs_ref, gctx_ref, dq_ref, dk_ref, dv_ref, grad_ref, masks)
    gnormed = nt(dq_ref[...], qkv_ref[:, :DIM])
    gnormed += nt(dk_ref[...], qkv_ref[:, DIM : 2 * DIM])
    gnormed += nt(dv_ref[...], qkv_ref[:, 2 * DIM :])
    gnormed = gnormed.astype(BF16).astype(F32)
    hat, inv = normalize(x)
    gain_grad = jnp.sum(gnormed * hat, axis=0, keepdims=True)
    gblock = norm_backward(gnormed, gain, hat, inv) + ghid
    normed = (hat * gain).astype(BF16)
    return gblock, normed, gbranch, gain_grad


def first_attention(
    far_x, far_pick, far_gains, far_qkv, far_table, far_trows, far_tcols, far_out,
    xw_ref, q_ref, k_ref, v_ref, probs_ref, ctx_ref, hidden_ref,
    bias_ref, x_ref, pick_ref, gains_ref, qkv_ref, table_ref, trows_ref, tcols_ref, out_ref, sems,
):
    pairs = [
        (far_table.at[pl.ds(0, HEADS)], table_ref), (far_trows, trows_ref), (far_tcols, tcols_ref),
        (far_x, x_ref), (far_pick, pick_ref), (far_gains.at[0], gains_ref), (far_qkv.at[0], qkv_ref), (far_out.at[0], out_ref),
    ]
    fetches = [pltpu.make_async_copy(far, near, sems.at[i]) for i, (far, near) in enumerate(pairs)]
    for fetch in fetches:
        fetch.start()
    for fetch in fetches[:3]:
        fetch.wait()
    expand_table(table_ref, trows_ref, tcols_ref, bias_ref)
    for fetch in fetches[3:]:
        fetch.wait()
    x = gather_tokens(pick_ref[...], x_ref[...])
    xw_ref[...] = x.astype(BF16)
    hat, _ = normalize(x)
    project((hat * gains_ref[0:1, :]).astype(BF16), qkv_ref, q_ref, k_ref, v_ref)
    attention(q_ref, k_ref, v_ref, bias_ref, probs_ref, ctx_ref, head_rows())
    branch = nn(ctx_ref[...], out_ref[...]).astype(BF16)
    hidden_ref[...] = xw_ref[...].astype(F32) + branch.astype(F32)


def first_mlp(
    hidden_ref, cot_ref, gains_ref, up_ref, down_ref, pick_ref, strips_ref,
    expanded_ref, slope_ref, bottom_ref, row_ref, side_ref, corner_ref,
):
    row_ref[144:, :] = cot_ref[:144, :]
    edges = nn(strips_ref[...], cot_ref[...]).astype(BF16)
    side_ref[STRIP:, :] = edges[:STRIP]
    corner_ref[STRIP:, :] = edges[STRIP:]
    hidden = hidden_ref[...]
    hat, _ = normalize(hidden)
    normed_mlp = (hat * gains_ref[1:2, :]).astype(BF16)
    total = hidden
    for j in range(3):
        cols = slice(j * 256, (j + 1) * 256)
        pre = nn(normed_mlp, up_ref[:, cols])
        below, density = gelu_parts(pre)
        expanded = (pre * below).astype(BF16)
        expanded_ref[:, cols] = expanded
        slope_ref[:, cols] = (below + pre * density).astype(BF16)
        total = total + nt(expanded, down_ref[:, cols])
    grid = scatter_tokens(pick_ref[...], total.astype(BF16)).astype(BF16)
    row_ref[:144, :] = grid[:144]
    bottom_ref[...] = grid[144:]
    edges = nn(strips_ref[...], grid).astype(BF16)
    side_ref[:STRIP, :] = edges[:STRIP]
    corner_ref[:STRIP, :] = edges[STRIP:]


def fill_source(source_ref, own, row_ref, side_ref, corner_ref, part):
    source_ref[0:144, :] = own
    source_ref[144:288, :] = row_ref[part * 144 : (part + 1) * 144, :]
    source_ref[288 : 288 + STRIP, :] = side_ref[part * STRIP : (part + 1) * STRIP, :]
    source_ref[288 + STRIP :, :] = corner_ref[part * STRIP : (part + 1) * STRIP, :]


def put_source(own_ref, row_ref, side_ref, corner_ref, part, value):
    own_ref[...] = value[0:144]
    row_ref[part * 144 : (part + 1) * 144, :] = value[144:288]
    side_ref[part * STRIP : (part + 1) * STRIP, :] = value[288 : 288 + STRIP]
    corner_ref[part * STRIP : (part + 1) * STRIP, :] = value[288 + STRIP :]


def split_halves(wbuf_ref, mine_ref, theirs_ref, sems):
    core = lax.rem(lax.axis_index("lat"), 2)
    send = pltpu.make_async_copy(wbuf_ref.at[1 - core], theirs_ref, sems.at[0])
    keep = pltpu.make_async_copy(wbuf_ref.at[core], mine_ref, sems.at[1])
    send.start()
    keep.start()
    send.wait()
    keep.wait()


def second_bias(table_ref, trows_ref, tcols_ref, bias_ref):
    expand_table(table_ref, trows_ref, tcols_ref, bias_ref)
    add_mask(bias_ref, (lax.axis_index("lat") == lax.axis_size("lat") - 1).astype(F32))


def second_both(
    own_ref, row_ref, side_ref, corner_ref, cot_ref, bias_ref,
    gains_ref, qkv_ref, out_ref, up_ref, down_ref, pick_ref,
    back_own_ref, y_own_ref, sent_row_ref, sent_side_ref, sent_corner_ref,
    g_ref, normed_ref, dq_ref, dk_ref, dv_ref, ctx_ref, gbranch_ref, normed_mlp_ref, gpre_ref, expanded_ref, grad_ref, gain_grad_ref,
    source_ref, x_ref, q_ref, k_ref, v_ref, probs_ref, gctx_ref,
):
    masks = head_rows()
    fill_source(source_ref, own_ref[...], row_ref, side_ref, corner_ref, 0)
    x_ref[...] = gather_tokens(pick_ref[...], source_ref[...])
    fill_source(source_ref, cot_ref[144:288, :], row_ref, side_ref, corner_ref, 1)
    g_ref[...] = gather_tokens(pick_ref[...], source_ref[...]).astype(BF16)
    hat, _ = normalize(x_ref[...])
    project((hat * gains_ref[0:1, :]).astype(BF16), qkv_ref, q_ref, k_ref, v_ref)
    attention(q_ref, k_ref, v_ref, bias_ref, probs_ref, ctx_ref, masks)
    branch = nn(ctx_ref[...], out_ref[...]).astype(BF16)
    hidden = x_ref[...] + branch.astype(F32)
    hat_mlp, inv_mlp = normalize(hidden)
    normed_mlp = (hat_mlp * gains_ref[1:2, :]).astype(BF16)
    normed_mlp_ref[...] = normed_mlp
    total = hidden
    gnormed = jnp.zeros((TOKENS, DIM), F32)
    for j in range(3):
        cols = slice(j * 256, (j + 1) * 256)
        pre = nn(normed_mlp, up_ref[:, cols])
        below, density = gelu_parts(pre)
        expanded = (pre * below).astype(BF16)
        expanded_ref[:, cols] = expanded
        total = total + nt(expanded, down_ref[:, cols])
        gact = nn(g_ref[...], down_ref[:, cols]).astype(BF16).astype(F32)
        gpre = ((below + pre * density) * gact).astype(BF16)
        gpre_ref[:, cols] = gpre
        gnormed = gnormed + nt(gpre, up_ref[:, cols])
    y = scatter_tokens(pick_ref[...], total.astype(BF16)).astype(BF16)
    put_source(y_own_ref, sent_row_ref, sent_side_ref, sent_corner_ref, 1, y)
    gnormed = gnormed.astype(BF16).astype(F32)
    gain_grad_ref[1:2, :] = jnp.sum(gnormed * hat_mlp, axis=0, keepdims=True)
    ghid = g_ref[...].astype(F32) + norm_backward(gnormed, gains_ref[1:2, :], hat_mlp, inv_mlp)
    gblock, normed, gbranch, gain_grad = attention_backward_part(
        x_ref[...], gains_ref[0:1, :], qkv_ref, out_ref, ghid,
        q_ref, k_ref, v_ref, probs_ref, ctx_ref, gctx_ref, dq_ref, dk_ref, dv_ref, grad_ref, masks,
    )
    gain_grad_ref[0:1, :] = gain_grad
    back = scatter_tokens(pick_ref[...], gblock.astype(BF16)).astype(BF16)
    put_source(back_own_ref, sent_row_ref, sent_side_ref, sent_corner_ref, 0, back)
    normed_ref[...] = normed
    gbranch_ref[...] = gbranch


def second_weights(
    normed_ref, dq_ref, dk_ref, dv_ref, ctx_ref, gbranch_ref, normed_mlp_ref, gpre_ref, expanded_ref, grad_ref, g_ref,
    trows_ref, tcols_ref, mine_ref, theirs_ref, table_grad_ref, wbuf_ref, sems,
):
    weight_grads(
        wbuf_ref, normed_ref[...], dq_ref[...], dk_ref[...], dv_ref[...], ctx_ref[...], gbranch_ref[...],
        normed_mlp_ref[...], gpre_ref, expanded_ref, g_ref[...],
    )
    table_grad_ref[...] = collapse_table(grad_ref, trows_ref, tcols_ref)
    split_halves(wbuf_ref, mine_ref, theirs_ref, sems)


def first_mlp_back(
    back_ref, row_ref, side_ref, corner_ref, hidden_ref, slope_ref, gains_ref, up_ref, down_ref, returned_ref,
    g_ref, ghid_ref, normed_mlp_ref, gpre_ref, gain_grad_ref, source_ref,
):
    fill_source(source_ref, back_ref[...], row_ref, side_ref, corner_ref, 0)
    g32 = gather_tokens(returned_ref[...], source_ref[...])
    g = g32.astype(BF16)
    g_ref[...] = g
    hat_mlp, inv_mlp = normalize(hidden_ref[...])
    normed_mlp_ref[...] = (hat_mlp * gains_ref[1:2, :]).astype(BF16)
    gnormed = jnp.zeros((TOKENS, DIM), F32)
    for j in range(3):
        cols = slice(j * 256, (j + 1) * 256)
        gact = nn(g, down_ref[:, cols]).astype(BF16).astype(F32)
        gpre = (slope_ref[:, cols].astype(F32) * gact).astype(BF16)
        gpre_ref[:, cols] = gpre
        gnormed = gnormed + nt(gpre, up_ref[:, cols])
    gnormed = gnormed.astype(BF16).astype(F32)
    gain_grad_ref[...] = jnp.sum(gnormed * hat_mlp, axis=0, keepdims=True)
    ghid_ref[...] = g32 + norm_backward(gnormed, gains_ref[1:2, :], hat_mlp, inv_mlp)


def first_attention_back(
    ghid_ref, g_ref, normed_mlp_ref, gpre_ref, mlp_gain_ref, xw_ref, q_ref, k_ref, v_ref, probs_ref, ctx_ref, expanded_ref,
    gains_ref, qkv_ref, out_ref, last_gain_ref,
    gblock_ref, grad_ref, mine_ref, theirs_ref,
    gctx_ref, dq_ref, dk_ref, dv_ref, wbuf_ref, sems,
):
    masks = head_rows()
    gblock, normed, gbranch, gain_grad = attention_backward_part(
        xw_ref[...].astype(F32), gains_ref[0:1, :], qkv_ref, out_ref, ghid_ref[...],
        q_ref, k_ref, v_ref, probs_ref, ctx_ref, gctx_ref, dq_ref, dk_ref, dv_ref, grad_ref, masks,
    )
    gblock_ref[...] = gblock.astype(BF16)
    weight_grads(
        wbuf_ref, normed, dq_ref[...], dk_ref[...], dv_ref[...], ctx_ref[...], gbranch,
        normed_mlp_ref[...], gpre_ref, expanded_ref, g_ref[...],
    )
    gains = jnp.concatenate([gain_grad, mlp_gain_ref[...], last_gain_ref[0:1, :], last_gain_ref[1:2, :]], axis=1)
    for h in range(2):
        wbuf_ref[h, PART:, :] = jnp.zeros((EXTRA, 128), BF16)
    for j in range(6):
        tile = jnp.concatenate([gains[:, j * 128 : (j + 1) * 128], jnp.zeros((15, 128), F32)], axis=0)
        wbuf_ref[0, PART + j * 16 : PART + (j + 1) * 16, :] = tile.astype(BF16)
    split_halves(wbuf_ref, mine_ref, theirs_ref, sems)


def first_finish(gblock_ref, grad_ref, last_table_ref, trows_ref, tcols_ref, pick_ref, gin_ref, tables_ref):
    tables_ref[0:TROWS, :] = collapse_table(grad_ref, trows_ref, tcols_ref)
    tables_ref[TROWS : 2 * TROWS, :] = last_table_ref[...]
    gin_ref[...] = scatter_tokens(pick_ref[...], gblock_ref[...].astype(F32)).astype(BF16)


def pack(first_ref, first_other_ref, last_ref, last_other_ref, packed_ref):
    first = (first_ref[...].astype(F32) + first_other_ref[...].astype(F32)).astype(BF16)
    packed_ref[:PART, :] = first[:PART]
    packed_ref[PART : 2 * PART, :] = (last_ref[...].astype(F32) + last_other_ref[...].astype(F32)).astype(BF16)
    packed_ref[2 * PART :, :] = first[PART:]


def add_two(mine_ref, other_ref, total_ref):
    total_ref[...] = (mine_ref[...].astype(F32) + other_ref[...].astype(F32)).astype(BF16)


def sum_parts(parts_ref, total_ref):
    total = parts_ref[0].astype(F32)
    for j in range(1, 16):
        total += parts_ref[j].astype(F32)
    total_ref[...] = total.astype(BF16)


def sum_and_spread(*refs):
    total = refs[0][...].astype(F32)
    for ref in refs[1:-1]:
        total += ref[...].astype(F32)
    total = total.astype(BF16)
    for j in range(16):
        refs[-1][j] = total


def unpack(
    mine_ref, other_ref, t0_ref, t1_ref, t2_ref, t3_ref, qkv_ref, out_ref, up_ref, down_ref, gains_ref, table_ref, sum_ref
):
    core = lax.rem(lax.axis_index("lat"), 2)

    def load(half, start, count):
        here = mine_ref[start : start + count, :].astype(F32)
        there = other_ref[start : start + count, :].astype(F32)
        return jnp.where(core == half, here, there)

    total = t0_ref[...].astype(F32)
    for ref in (t1_ref, t2_ref, t3_ref):
        total += ref[...].astype(F32)
    sum_ref[...] = total
    for b in range(2):
        for j in range(18):
            tile = load(j // 9, b * PART + j % 9 * DIM, DIM)
            if j < 6:
                up_ref[b, :, j * 128 : (j + 1) * 128] = tile
            elif j < 12:
                down_ref[b, :, (j - 6) * 128 : (j - 5) * 128] = tile
            elif j < 16:
                qkv_ref[b, :, (j - 12) * 128 : (j - 11) * 128] = tile
            elif j == 16:
                qkv_ref[b, :, 512:576] = tile[:, :64]
                out_ref[b, :, 0:64] = tile[:, 64:]
            else:
                out_ref[b, :, 64:192] = tile
        for j in range(26):
            place = b * TROWS + j * 8
            piece = sum_ref[place : place + HEADS, :]
            width = min(128, TABLE - j * 128)
            for h in range(HEADS):
                table_ref[b * HEADS + h, :, j * 128 : j * 128 + width] = piece[h : h + 1, :width]
    gains = jnp.concatenate([load(0, 2 * PART + j * 16, 16)[0:1] for j in range(6)], axis=1)
    for b in range(2):
        for i in range(2):
            k = b * 2 + i
            gains_ref[b, i : i + 1, :] = gains[:, k * DIM : (k + 1) * DIM]


def whole(array):
    return pl.BlockSpec(array.shape, lambda i: (0,) * array.ndim)


def picked(array, index):
    rest = array.shape[1:]
    return pl.BlockSpec((None,) + rest, lambda i: (index,) + (0,) * len(rest))


def in_place():
    return pl.BlockSpec(memory_space=pl.ANY)


def call(kernel, operands, specs, outs, scratch=(), micros=2, out_specs=None, mebibytes=10):
    shapes = [jax.ShapeDtypeStruct(shape, dtype) for shape, dtype in outs]
    moved = sum(a.size * a.dtype.itemsize for a in (*operands, *shapes))
    return pl.pallas_call(
        kernel,
        grid=(1,),
        out_shape=shapes,
        in_specs=specs,
        out_specs=out_specs or [whole(s) for s in shapes],
        scratch_shapes=list(scratch),
        cost_estimate=pl.CostEstimate(flops=micros * 1_100_000_000, bytes_accessed=moved, transcendentals=0),
        compiler_params=pltpu.CompilerParams(vmem_limit_bytes=mebibytes * 1024 * 1024),
    )(*operands)


def neighbour(sizes, steps):
    pairs = []
    for a in range(sizes[0]):
        for b in range(sizes[1]):
            source = ((a + steps[0]) % sizes[0]) * sizes[1] + (b + steps[1]) % sizes[1]
            pairs.append((source, a * sizes[1] + b))
    return pairs


def exchange(rows, side, corner, sizes, step):
    both = ("lat", "lon")
    rows = lax.ppermute(rows, both, neighbour(sizes, (step, 0)))
    side = lax.ppermute(side, both, neighbour(sizes, (0, step)))
    corner = lax.ppermute(corner, both, neighbour(sizes, (step, step)))
    return rows, side, corner


def vmem(shape, dtype):
    return pltpu.VMEM(shape, dtype)


def device_place(i):
    lat, lon = divmod(i, 8)
    return lat // 8, lat // 2 % 4, lat % 2, lon // 2, lon % 2


def flat_device(z_hi, y, core, x, z_lo):
    return ((z_hi * 4 + y) * 2 + core) * 8 + x * 2 + z_lo


def shifted_pairs(core=0, x=0, z_lo=0):
    pairs = []
    for i in range(128):
        h, y, c, a, b = device_place(i)
        pairs.append((flat_device(h, y, (c + core) % 2, (a + x) % 4, (b + z_lo) % 2), i))
    return pairs


def moved(array, **steps):
    return lax.ppermute(array, ("lat", "lon"), shifted_pairs(**steps))


def sum_over_devices(first, last, finish):
    both = ("lat", "lon")
    planes = {}
    for i in range(128):
        _, _, c, a, _ = device_place(i)
        planes.setdefault((c, a), []).append(i)
    groups = list(planes.values())

    def run(kernel, operands, shape):
        [result] = call(kernel, operands, [whole(a) for a in operands], [(shape, BF16)])
        return result

    sent = run(pack, [first[0], moved(first[1], core=1), *last], (HALF, 128))
    sent, finish = lax.optimization_barrier((sent, finish))
    parts = lax.all_to_all(sent.reshape(16, CHUNK, 128), both, 0, 0, axis_index_groups=groups)
    outs = [((GRID, 2 * DIM), BF16), ((2 * TROWS, 128), BF16)]
    grad_inputs, tables = call(first_finish, finish, [whole(a) for a in finish], outs)
    other = moved(tables, z_lo=1)
    parts, other = lax.optimization_barrier((parts, other))
    tables = run(add_two, [tables, other], tables.shape)
    total = run(sum_parts, [parts], (CHUNK, 128))
    spread = run(sum_and_spread, [total] + [moved(total, x=k) for k in (1, 2, 3)], (16, CHUNK, 128))
    spread, tables = lax.optimization_barrier((spread, tables))
    half = lax.all_to_all(spread, both, 0, 0, axis_index_groups=groups)
    table_terms = [tables] + [moved(tables, x=k) for k in (1, 2, 3)]
    half, table_terms = lax.optimization_barrier((half, table_terms))
    half = half.reshape(HALF, 128)
    operands = [half, moved(half, core=1), *table_terms]
    outs = [((2, DIM, 3 * DIM), F32), ((2, DIM, DIM), F32), ((2, DIM, UNITS), F32), ((2, DIM, UNITS), F32)]
    outs += [((2, 2, DIM), F32), ((2 * HEADS, 1, TABLE), F32)]
    grads = call(unpack, operands, [whole(a) for a in operands], outs, [vmem((2 * TROWS, 128), F32)])
    return grad_inputs, grads


def on_device(sizes, inputs, cotangent, norm_gains, qkv_weight, out_weight, up_weight, down_weight, bias_table):
    x = inputs.reshape(GRID, 2 * DIM)
    cot = cotangent.reshape(GRID, 2 * DIM)
    trows, tcols = jnp.asarray(table_rows(), BF16), jnp.asarray(table_cols(), BF16)
    pick_grid, pick_shift, pick_back = (
        jnp.asarray(m, BF16) for m in (grid_picker(), shifted_picker(), returned_picker())
    )
    strips = jnp.asarray(strip_picker(), BF16)
    weights = (norm_gains, qkv_weight, out_weight, up_weight, jnp.swapaxes(down_weight, 1, 2))
    tok, src, hid = (TOKENS, DIM), (SOURCE, 2 * DIM), (TOKENS, UNITS)
    probs = (WINDOWS, WIN_TOK, QLANES)

    def table_spec(index):
        return pl.BlockSpec((HEADS, 1, TABLE), lambda i: (index, 0, 0))

    bias_table = bias_table.reshape(2 * HEADS, 1, TABLE)
    gains, qkv, out, up, down = weights
    wide_tok, wide_hid = (tok, BF16), (hid, BF16)
    bias = (WIN_TOK, QLANES)

    def specs_for(arrays, index):
        specs = []
        for a in arrays:
            if any(a is w for w in weights):
                specs.append(picked(a, index))
            elif a is bias_table:
                specs.append(table_spec(index))
            else:
                specs.append(whole(a))
        return specs

    operands = [x, pick_grid, gains, qkv, bias_table, trows, tcols, out]
    outs = [wide_tok] * 4 + [(probs, BF16), wide_tok, (tok, F32)]
    scratch = [vmem(bias, F32), vmem(x.shape, BF16), vmem(pick_grid.shape, BF16), vmem((2, DIM), F32), vmem((DIM, 3 * DIM), BF16)]
    scratch += [vmem((HEADS, 1, TABLE), F32), vmem(trows.shape, BF16), vmem(tcols.shape, BF16), vmem((DIM, DIM), BF16)]
    scratch += [pltpu.SemaphoreType.DMA((8,))]
    operands = [pltpu.with_memory_space_constraint(a, pltpu.HBM) for a in operands]
    specs = [in_place()] * 8
    results = call(first_attention, operands, specs, outs, scratch, 7, mebibytes=14)
    xw, q, k, v, probs_first, ctx, hidden = results

    operands = [hidden, cot, gains, up, down, pick_grid, strips]
    strip_outs = [((288, 2 * DIM), BF16), ((2 * STRIP, 2 * DIM), BF16), ((2 * STRIP, 2 * DIM), BF16)]
    outs = [wide_hid, wide_hid, ((144, 2 * DIM), BF16)] + strip_outs
    results = call(first_mlp, operands, specs_for(operands, 0), outs, (), 4, mebibytes=14)
    expanded, slope, bottom, *sent = results
    sent, bias_table = lax.optimization_barrier((sent, bias_table))

    arrived = exchange(*sent, sizes, 1)
    operands = [bias_table, trows, tcols]
    [bias_last] = call(second_bias, operands, specs_for(operands, 1), [(bias, F32)], (), 2, mebibytes=14)

    operands = [bottom, *arrived, cot, bias_last, *weights, pick_shift]
    outs = [((144, 2 * DIM), BF16)] * 2 + strip_outs + [wide_tok] * 8 + [wide_hid] * 2 + [(bias, F32), ((2, DIM), F32)]
    scratch = [vmem(src, BF16), vmem(tok, F32)] + [vmem(tok, BF16)] * 3 + [vmem(probs, BF16), vmem(tok, BF16)]
    results = call(second_both, operands, specs_for(operands, 1), outs, scratch, 12, mebibytes=14)
    back_own, y_own, sent, terms, last_gain = results[0], results[1], results[2:5], results[5:16], results[16]

    arrived = exchange(*sent, sizes, -1)
    g, *terms = terms
    operands = [*terms, g, trows, tcols]
    outs = [((PART, 128), BF16)] * 2 + [((TROWS, 128), BF16)]
    out_specs = [in_place()] * 2 + [whole(jax.ShapeDtypeStruct(*o)) for o in outs[2:]]
    scratch = [vmem((2, PART, 128), BF16), pltpu.SemaphoreType.DMA((2,))]
    results = call(second_weights, operands, specs_for(operands, 1), outs, scratch, 4, out_specs, 14)
    last_mine, last_theirs, last_table = results

    operands = [back_own, *arrived, hidden, slope, gains, up, down, pick_back]
    outs = [wide_tok, (tok, F32), wide_tok, wide_hid, ((1, DIM), F32)]
    results = call(first_mlp_back, operands, specs_for(operands, 0), outs, [vmem(src, BF16)], 3, mebibytes=14)
    g, ghid, normed_mlp, gpre, mlp_gain = results
    ghid, last_theirs = lax.optimization_barrier((ghid, last_theirs))
    last = [last_mine, moved(last_theirs, core=1)]

    operands = [ghid, g, normed_mlp, gpre, mlp_gain, xw, q, k, v, probs_first, ctx, expanded, gains, qkv, out]
    operands += [last_gain]
    first_shape = (PART + EXTRA, 128)
    outs = [wide_tok, (bias, F32), (first_shape, BF16), (first_shape, BF16)]
    out_specs = [whole(jax.ShapeDtypeStruct(*o)) for o in outs[:2]] + [in_place()] * 2
    scratch = [vmem(tok, BF16)] * 4 + [vmem((2, *first_shape), BF16), pltpu.SemaphoreType.DMA((2,))]
    gblock, grad_scores, *first = call(
        first_attention_back, operands, specs_for(operands, 0), outs, scratch, 8, out_specs, 14
    )
    last, first = lax.optimization_barrier((last, first))
    finish = [gblock, grad_scores, last_table, trows, tcols, pick_grid]
    grad_inputs, grads = sum_over_devices(first, last, finish)
    y_rows, y_side, y_corner = arrived
    rows = jnp.concatenate([y_rows[144:], y_own]).reshape(ROWS, COLS, 2 * DIM)
    edge = jnp.concatenate([a[STRIP : STRIP + 18].reshape(3, 6, 2 * DIM) for a in (y_corner, y_side)])
    output = jnp.concatenate([edge, rows[:, 6:]], axis=1)

    grad_qkv, grad_out, grad_up, grad_down, grad_gains, grad_table = grads
    grad_down = jnp.swapaxes(grad_down, 1, 2)
    grad_table = grad_table.reshape(2, 1, HEADS, TABLE)
    return (output, grad_inputs.reshape(ROWS, COLS, 2 * DIM), grad_gains, grad_qkv, grad_out, grad_up, grad_down, grad_table)


def solution(mesh):
    sizes = (mesh.shape["lat"], mesh.shape["lon"])

    def program(*arguments):
        return on_device(sizes, *arguments)

    fields, tables = P("lat", "lon", None), P(None, "lat", None, None)
    return jax.shard_map(
        program,
        mesh=mesh,
        in_specs=(fields, fields, P(), P(), P(), P(), P(), tables),
        out_specs=(fields, fields, P(), P(), P(), P(), P(), tables),
        check_vma=False,
    )
```

```python
import math

import jax
import jax.numpy as jnp
import numpy as np
from jax import lax
from jax.experimental import pallas as pl
from jax.experimental.pallas import tpu as pltpu
from jax.sharding import PartitionSpec as P

DIM = 192
HEADS = 6
HEAD_DIM = 32
UNITS = 768
ROWS = 6
COLS = 48
WIN_COLS = 12
WINDOWS = 4
WIN_TOK = 144
TOKENS = 576
GRID = ROWS * COLS
GROUP = 12
SPAN = 23
WIDE = SPAN * GROUP
CELL = 6 * SPAN
TABLE = 24 * CELL
QLANES = HEADS * WIN_TOK
STRIP = 32
SOURCE = 288 + 2 * STRIP
NORM_EPS = 1e-05
MASK_VALUE = -100.0
LOG2E = math.log2(math.e)
SCALE = 1.0 / math.sqrt(HEAD_DIM)
WBLOCK = 18 * DIM
CHUNK = 224
HALF = 16 * CHUNK
PART = 9 * DIM
EXTRA = HALF - 2 * PART
TROWS = 208

F32 = jnp.float32
BF16 = jnp.bfloat16


def token_places():
    t = np.arange(TOKENS)
    w, rest = t // WIN_TOK, t % WIN_TOK
    c, l, r = rest // GROUP, rest % GROUP // ROWS, rest % ROWS
    return r, w * WIN_COLS + c, l


def one_hot(places, size):
    return (places[:, None] == np.arange(size)[None, :]).astype(np.float32)


def grid_picker():
    r, j, _ = token_places()
    return one_hot(r * COLS + j, GRID)


def shifted_picker():
    r, j, _ = token_places()
    half = np.where(r < 3, r, r - 3)
    inner = np.where(r < 3, 0, 144) + half * COLS + j + 6
    edge = np.where(r < 3, 288, 288 + STRIP) + half * 6 + j - 42
    return one_hot(np.where(j < 42, inner, edge), SOURCE)


def returned_picker():
    r, j, _ = token_places()
    half = np.where(r >= 3, r - 3, r)
    inner = np.where(r >= 3, 0, 144) + half * COLS + j
    edge = np.where(r >= 3, 288, 288 + STRIP) + half * 6 + j
    return one_hot(np.where(j >= 6, inner, edge), SOURCE)


def strip_picker():
    picked = np.zeros((2 * STRIP, GRID), np.float32)
    for i in range(3):
        for j in range(6):
            picked[i * 6 + j, (i + 3) * COLS + j] = 1
            picked[STRIP + i * 6 + j, i * COLS + j] = 1
    return picked


def table_rows():
    picked = np.zeros((2, HEADS * 16, 24 * 8), np.float32)
    for h in range(HEADS):
        for lq in range(2):
            for lp in range(2):
                for rq in range(6):
                    picked[lp, h * 16 + lq * 6 + rq, (lq * 12 + lp * 6 + rq) * 8 + h] = 1
    return picked


def table_cols():
    picked = np.zeros((2, 6 * SPAN, WIDE), np.float32)
    for lp in range(2):
        for rp in range(6):
            for d in range(SPAN):
                picked[lp, rp * SPAN + d, d * GROUP + lp * 6 + rp] = 1
    return picked


def nn(a, b):
    return jnp.dot(a, b, preferred_element_type=F32)


def nt(a, b):
    return lax.dot_general(a, b, (((1,), (1,)), ((), ())), preferred_element_type=F32)


def tn(a, b):
    return lax.dot_general(a, b, (((0,), (0,)), ((), ())), preferred_element_type=F32)


def level_mask():
    t = lax.broadcasted_iota(jnp.int32, (TOKENS, DIM), 0)
    return (lax.div(t, 6) & 1) == 1


def gather_tokens(picker, source):
    both = nn(picker, source)
    return jnp.where(level_mask(), both[:, DIM:], both[:, :DIM])


def scatter_tokens(picker, tokens):
    upper = level_mask()
    zero = jnp.zeros_like(tokens)
    both = jnp.concatenate([jnp.where(upper, zero, tokens), jnp.where(upper, tokens, zero)], axis=1)
    return tn(picker, both.astype(BF16))


def normalize(x):
    centre = jnp.mean(x, axis=-1, keepdims=True)
    off = x - centre
    spread = jnp.mean(off * off, axis=-1, keepdims=True)
    inv = lax.rsqrt(spread + NORM_EPS)
    return off * inv, inv


def norm_backward(grad, gain, hat, inv):
    scaled = grad * gain
    mean_one = jnp.mean(scaled, axis=-1, keepdims=True)
    mean_two = jnp.mean(scaled * hat, axis=-1, keepdims=True)
    return inv * (scaled - mean_one - hat * mean_two)


def gelu_parts(x):
    below = 0.5 + 0.5 * lax.erf(x * math.sqrt(0.5))
    return below, jnp.exp2(x * x * (-0.5 * LOG2E)) * (1.0 / math.sqrt(2.0 * math.pi))


def head_rows():
    lane = lax.div(lax.broadcasted_iota(jnp.int32, (1, DIM), 1), HEAD_DIM)
    return [(lane == h) for h in range(HEADS)]


def stack_heads(x, masks):
    return jnp.concatenate([jnp.where(m, x, jnp.zeros_like(x)) for m in masks], axis=0)


def fold_heads(x, masks):
    folded = x[:WIN_TOK]
    for h in range(1, HEADS):
        folded = jnp.where(masks[h], x[h * WIN_TOK : (h + 1) * WIN_TOK], folded)
    return folded


def expand_table(table_ref, trows_ref, tcols_ref, bias_ref):
    table = jnp.concatenate([table_ref[h] for h in range(HEADS)] + [jnp.zeros((2, TABLE), F32)], axis=0) * LOG2E
    table = jnp.concatenate([table[:, k * CELL : (k + 1) * CELL] for k in range(24)], axis=0)
    high = table.astype(BF16)
    low = (table - high.astype(F32)).astype(BF16)
    wide = jnp.zeros((HEADS * 16, WIDE), F32)
    for lp in range(2):
        for part in (high, low):
            wide += nn(nn(trows_ref[lp], part).astype(BF16), tcols_ref[lp])
    for cq in range(WIN_COLS):
        start = GROUP * (WIN_COLS - 1 - cq)
        row = jnp.concatenate(
            [wide[h * 16 : h * 16 + GROUP, start : start + WIN_TOK] for h in range(HEADS)], axis=1
        )
        bias_ref[cq * GROUP : (cq + 1) * GROUP, :] = row


def add_mask(bias_ref, flag):
    key = lax.broadcasted_iota(jnp.int32, (WIN_TOK, 1), 0)
    query = lax.broadcasted_iota(jnp.int32, (1, QLANES), 1)
    key_up = (lax.div(key, 3) & 1).astype(F32)
    query_up = (lax.div(query, 3) & 1).astype(F32)
    apart = jnp.abs(key_up - query_up)
    bias_ref[...] += apart * (flag * (MASK_VALUE * LOG2E))


def collapse_table(grad_ref, trows_ref, tcols_ref):
    parts = []
    for h in range(HEADS):
        total = None
        for cq in range(WIN_COLS):
            start = GROUP * (WIN_COLS - 1 - cq)
            piece = grad_ref[cq * GROUP : (cq + 1) * GROUP, h * WIN_TOK : (h + 1) * WIN_TOK]
            pads = [jnp.zeros((GROUP, start), F32)] if start else []
            tail = WIDE - start - WIN_TOK
            pads_after = [jnp.zeros((GROUP, tail), F32)] if tail else []
            piece = jnp.concatenate(pads + [piece] + pads_after, axis=1)
            total = piece if total is None else total + piece
        parts.append(jnp.concatenate([total, jnp.zeros((16 - GROUP, WIDE), F32)], axis=0))
    wide = jnp.concatenate(parts, axis=0).astype(BF16)
    result = jnp.zeros((24 * 8, CELL), F32)
    for lp in range(2):
        narrow = nt(wide, tcols_ref[lp]).astype(BF16)
        result += tn(trows_ref[lp], narrow)
    cells = [result[k * 8 : (k + 1) * 8] for k in range(24)] + [jnp.zeros((8, 26 * 128 - TABLE), F32)]
    flat = jnp.concatenate(cells, axis=1)
    return jnp.concatenate([flat[:, j * 128 : (j + 1) * 128] for j in range(26)], axis=0).astype(BF16)


def attention(q_ref, k_ref, v_ref, bias_ref, probs_ref, ctx_ref, masks):
    for w in range(WINDOWS):
        rows = pl.ds(w * WIN_TOK, WIN_TOK)
        stacked = stack_heads(q_ref[rows, :], masks)
        scores = nt(k_ref[rows, :], stacked) * (SCALE * LOG2E) + bias_ref[...]
        weights = jnp.exp2(scores)
        inverse = 1.0 / jnp.sum(weights, axis=0, keepdims=True)
        probs = (weights * inverse).astype(BF16)
        probs_ref[w] = probs
        ctx_ref[rows, :] = fold_heads(tn(probs, v_ref[rows, :]), masks).astype(BF16)


def attention_back(q_ref, k_ref, v_ref, probs_ref, gctx_ref, dq_ref, dk_ref, dv_ref, grad_ref, masks):
    for w in range(WINDOWS):
        rows = pl.ds(w * WIN_TOK, WIN_TOK)
        stacked_g = stack_heads(gctx_ref[rows, :], masks)
        stacked_q = stack_heads(q_ref[rows, :], masks)
        probs_half = probs_ref[w]
        probs = probs_half.astype(F32)
        grad_probs = nt(v_ref[rows, :], stacked_g)
        inner = jnp.sum(grad_probs * probs, axis=0, keepdims=True)
        grad_scores = probs * (grad_probs - inner)
        if w == 0:
            grad_ref[...] = grad_scores
        else:
            grad_ref[...] += grad_scores
        half = grad_scores.astype(BF16)
        dv_ref[rows, :] = nn(probs_half, stacked_g).astype(BF16)
        dk_ref[rows, :] = (nn(half, stacked_q) * SCALE).astype(BF16)
        dq_ref[rows, :] = (fold_heads(tn(half, k_ref[rows, :]), masks) * SCALE).astype(BF16)


def project(normed, qkv_ref, q_ref, k_ref, v_ref):
    for i, ref in enumerate((q_ref, k_ref, v_ref)):
        ref[...] = nn(normed, qkv_ref[:, i * DIM : (i + 1) * DIM]).astype(BF16)


def put_weights(wbuf_ref, offset, value):
    tiles = value.shape[1] // 128
    for j in range(tiles):
        half, place = divmod(offset + j, 9)
        wbuf_ref[half, place * DIM : (place + 1) * DIM, :] = value[:, j * 128 : (j + 1) * 128].astype(BF16)


def weight_grads(wbuf_ref, normed, dq, dk, dv, ctx, gbranch, normed_mlp, gpre_ref, expanded_ref, g):
    for j in range(3):
        cols = slice(j * 256, (j + 1) * 256)
        put_weights(wbuf_ref, 2 * j, tn(normed_mlp, gpre_ref[:, cols]))
        put_weights(wbuf_ref, 6 + 2 * j, tn(g, expanded_ref[:, cols]))
    put_weights(wbuf_ref, 12, tn(normed, jnp.concatenate([dq, dk], axis=1)))
    put_weights(wbuf_ref, 15, jnp.concatenate([tn(normed, dv), tn(ctx, gbranch)], axis=1))


def attention_backward_part(
    hat, inv, gain, qkv_ref, out_ref, ghid, q_ref, k_ref, v_ref, probs_ref, ctx_ref, gctx_ref, dq_ref, dk_ref, dv_ref, grad_ref, masks
):
    gbranch = ghid.astype(BF16)
    gctx_ref[...] = nt(gbranch, out_ref[...]).astype(BF16)
    attention_back(q_ref, k_ref, v_ref, probs_ref, gctx_ref, dq_ref, dk_ref, dv_ref, grad_ref, masks)
    gnormed = nt(dq_ref[...], qkv_ref[:, :DIM])
    gnormed += nt(dk_ref[...], qkv_ref[:, DIM : 2 * DIM])
    gnormed += nt(dv_ref[...], qkv_ref[:, 2 * DIM :])
    gnormed = gnormed.astype(BF16).astype(F32)
    gain_grad = jnp.sum(gnormed * hat, axis=0, keepdims=True)
    gblock = norm_backward(gnormed, gain, hat, inv) + ghid
    return gblock, gbranch, gain_grad


def first_attention(
    far_x, far_pick, far_gains, far_qkv, far_table, far_trows, far_tcols, far_out,
    xw_ref, q_ref, k_ref, v_ref, probs_ref, ctx_ref, hidden_ref,
    bias_ref, x_ref, pick_ref, gains_ref, qkv_ref, table_ref, trows_ref, tcols_ref, out_ref, sems,
):
    pairs = [
        (far_table.at[pl.ds(0, HEADS)], table_ref), (far_trows, trows_ref), (far_tcols, tcols_ref),
        (far_x, x_ref), (far_pick, pick_ref), (far_gains.at[0], gains_ref), (far_qkv.at[0], qkv_ref), (far_out.at[0], out_ref),
    ]
    fetches = [pltpu.make_async_copy(far, near, sems.at[i]) for i, (far, near) in enumerate(pairs)]
    for fetch in fetches:
        fetch.start()
    for fetch in fetches[:3]:
        fetch.wait()
    expand_table(table_ref, trows_ref, tcols_ref, bias_ref)
    for fetch in fetches[3:]:
        fetch.wait()
    x = gather_tokens(pick_ref[...], x_ref[...])
    xw_ref[...] = x.astype(BF16)
    hat, _ = normalize(x)
    project((hat * gains_ref[0:1, :]).astype(BF16), qkv_ref, q_ref, k_ref, v_ref)
    attention(q_ref, k_ref, v_ref, bias_ref, probs_ref, ctx_ref, head_rows())
    branch = nn(ctx_ref[...], out_ref[...]).astype(BF16)
    hidden_ref[...] = xw_ref[...].astype(F32) + branch.astype(F32)


def first_mlp(
    hidden_ref, cot_ref, gains_ref, up_ref, down_ref, pick_ref, strips_ref,
    expanded_ref, slope_ref, bottom_ref, row_ref, side_ref, corner_ref,
):
    row_ref[144:, :] = cot_ref[:144, :]
    edges = nn(strips_ref[...], cot_ref[...]).astype(BF16)
    side_ref[STRIP:, :] = edges[:STRIP]
    corner_ref[STRIP:, :] = edges[STRIP:]
    hidden = hidden_ref[...]
    hat, _ = normalize(hidden)
    normed_mlp = (hat * gains_ref[1:2, :]).astype(BF16)
    total = hidden
    for j in range(3):
        cols = slice(j * 256, (j + 1) * 256)
        pre = nn(normed_mlp, up_ref[:, cols])
        below, density = gelu_parts(pre)
        expanded = (pre * below).astype(BF16)
        expanded_ref[:, cols] = expanded
        slope_ref[:, cols] = (below + pre * density).astype(BF16)
        total = total + nt(expanded, down_ref[:, cols])
    grid = scatter_tokens(pick_ref[...], total.astype(BF16)).astype(BF16)
    row_ref[:144, :] = grid[:144]
    bottom_ref[...] = grid[144:]
    edges = nn(strips_ref[...], grid).astype(BF16)
    side_ref[:STRIP, :] = edges[:STRIP]
    corner_ref[:STRIP, :] = edges[STRIP:]


def fill_source(source_ref, own, row_ref, side_ref, corner_ref, part):
    source_ref[0:144, :] = own
    source_ref[144:288, :] = row_ref[part * 144 : (part + 1) * 144, :]
    source_ref[288 : 288 + STRIP, :] = side_ref[part * STRIP : (part + 1) * STRIP, :]
    source_ref[288 + STRIP :, :] = corner_ref[part * STRIP : (part + 1) * STRIP, :]


def put_source(own_ref, row_ref, side_ref, corner_ref, part, value):
    own_ref[...] = value[0:144]
    row_ref[part * 144 : (part + 1) * 144, :] = value[144:288]
    side_ref[part * STRIP : (part + 1) * STRIP, :] = value[288 : 288 + STRIP]
    corner_ref[part * STRIP : (part + 1) * STRIP, :] = value[288 + STRIP :]


def split_halves(wbuf_ref, mine_ref, theirs_ref, sems):
    core = lax.rem(lax.axis_index("lat"), 2)
    send = pltpu.make_async_copy(wbuf_ref.at[1 - core], theirs_ref, sems.at[0])
    keep = pltpu.make_async_copy(wbuf_ref.at[core], mine_ref, sems.at[1])
    send.start()
    keep.start()
    send.wait()
    keep.wait()


def second_bias(table_ref, trows_ref, tcols_ref, bias_ref):
    expand_table(table_ref, trows_ref, tcols_ref, bias_ref)
    add_mask(bias_ref, (lax.axis_index("lat") == lax.axis_size("lat") - 1).astype(F32))


def second_both(
    own_ref, row_ref, side_ref, corner_ref, cot_ref, bias_ref,
    gains_ref, qkv_ref, out_ref, up_ref, down_ref, pick_ref,
    back_own_ref, y_own_ref, sent_row_ref, sent_side_ref, sent_corner_ref,
    g_ref, normed_ref, dq_ref, dk_ref, dv_ref, ctx_ref, gbranch_ref, normed_mlp_ref, gpre_ref, expanded_ref, grad_ref, gain_grad_ref,
    source_ref, x_ref, hat_ref, q_ref, k_ref, v_ref, probs_ref, gctx_ref,
):
    masks = head_rows()
    fill_source(source_ref, own_ref[...], row_ref, side_ref, corner_ref, 0)
    x_ref[...] = gather_tokens(pick_ref[...], source_ref[...])
    fill_source(source_ref, cot_ref[144:288, :], row_ref, side_ref, corner_ref, 1)
    g_ref[...] = gather_tokens(pick_ref[...], source_ref[...]).astype(BF16)
    hat, inv = normalize(x_ref[...])
    normed_ref[...] = (hat * gains_ref[0:1, :]).astype(BF16)
    hat_ref[...] = hat
    project(normed_ref[...], qkv_ref, q_ref, k_ref, v_ref)
    attention(q_ref, k_ref, v_ref, bias_ref, probs_ref, ctx_ref, masks)
    branch = nn(ctx_ref[...], out_ref[...]).astype(BF16)
    hidden = x_ref[...] + branch.astype(F32)
    hat_mlp, inv_mlp = normalize(hidden)
    normed_mlp = (hat_mlp * gains_ref[1:2, :]).astype(BF16)
    normed_mlp_ref[...] = normed_mlp
    total = hidden
    gnormed = jnp.zeros((TOKENS, DIM), F32)
    for j in range(3):
        cols = slice(j * 256, (j + 1) * 256)
        pre = nn(normed_mlp, up_ref[:, cols])
        below, density = gelu_parts(pre)
        expanded = (pre * below).astype(BF16)
        expanded_ref[:, cols] = expanded
        total = total + nt(expanded, down_ref[:, cols])
        gact = nn(g_ref[...], down_ref[:, cols]).astype(BF16).astype(F32)
        gpre = ((below + pre * density) * gact).astype(BF16)
        gpre_ref[:, cols] = gpre
        gnormed = gnormed + nt(gpre, up_ref[:, cols])
    y = scatter_tokens(pick_ref[...], total.astype(BF16)).astype(BF16)
    put_source(y_own_ref, sent_row_ref, sent_side_ref, sent_corner_ref, 1, y)
    gnormed = gnormed.astype(BF16).astype(F32)
    gain_grad_ref[1:2, :] = jnp.sum(gnormed * hat_mlp, axis=0, keepdims=True)
    ghid = g_ref[...].astype(F32) + norm_backward(gnormed, gains_ref[1:2, :], hat_mlp, inv_mlp)
    gblock, gbranch, gain_grad = attention_backward_part(
        hat_ref[...], inv, gains_ref[0:1, :], qkv_ref, out_ref, ghid,
        q_ref, k_ref, v_ref, probs_ref, ctx_ref, gctx_ref, dq_ref, dk_ref, dv_ref, grad_ref, masks,
    )
    gain_grad_ref[0:1, :] = gain_grad
    back = scatter_tokens(pick_ref[...], gblock.astype(BF16)).astype(BF16)
    put_source(back_own_ref, sent_row_ref, sent_side_ref, sent_corner_ref, 0, back)
    gbranch_ref[...] = gbranch


def second_weights(
    normed_ref, dq_ref, dk_ref, dv_ref, ctx_ref, gbranch_ref, normed_mlp_ref, gpre_ref, expanded_ref, grad_ref, g_ref,
    trows_ref, tcols_ref, mine_ref, theirs_ref, table_grad_ref, wbuf_ref, sems,
):
    weight_grads(
        wbuf_ref, normed_ref[...], dq_ref[...], dk_ref[...], dv_ref[...], ctx_ref[...], gbranch_ref[...],
        normed_mlp_ref[...], gpre_ref, expanded_ref, g_ref[...],
    )
    table_grad_ref[...] = collapse_table(grad_ref, trows_ref, tcols_ref)
    split_halves(wbuf_ref, mine_ref, theirs_ref, sems)


def first_norms(xw_ref, hidden_ref, gains_ref, hat_ref, inv_ref, normed_ref, hat_mlp_ref, inv_mlp_ref, normed_mlp_ref):
    hat, inv = normalize(xw_ref[...].astype(F32))
    hat_ref[...] = hat
    inv_ref[...] = inv
    normed_ref[...] = (hat * gains_ref[0:1, :]).astype(BF16)
    hat, inv = normalize(hidden_ref[...])
    hat_mlp_ref[...] = hat
    inv_mlp_ref[...] = inv
    normed_mlp_ref[...] = (hat * gains_ref[1:2, :]).astype(BF16)


def first_mlp_back(
    back_ref, row_ref, side_ref, corner_ref, hat_mlp_ref, inv_mlp_ref, slope_ref, gains_ref, up_ref, down_ref, returned_ref,
    g_ref, ghid_ref, gpre_ref, gain_grad_ref, source_ref,
):
    fill_source(source_ref, back_ref[...], row_ref, side_ref, corner_ref, 0)
    g32 = gather_tokens(returned_ref[...], source_ref[...])
    g = g32.astype(BF16)
    g_ref[...] = g
    hat_mlp, inv_mlp = hat_mlp_ref[...], inv_mlp_ref[...]
    gnormed = jnp.zeros((TOKENS, DIM), F32)
    for j in range(3):
        cols = slice(j * 256, (j + 1) * 256)
        gact = nn(g, down_ref[:, cols]).astype(BF16).astype(F32)
        gpre = (slope_ref[:, cols].astype(F32) * gact).astype(BF16)
        gpre_ref[:, cols] = gpre
        gnormed = gnormed + nt(gpre, up_ref[:, cols])
    gnormed = gnormed.astype(BF16).astype(F32)
    gain_grad_ref[...] = jnp.sum(gnormed * hat_mlp, axis=0, keepdims=True)
    ghid_ref[...] = g32 + norm_backward(gnormed, gains_ref[1:2, :], hat_mlp, inv_mlp)


def first_attention_back(
    ghid_ref, g_ref, gpre_ref, mlp_gain_ref, hat_ref, inv_ref, normed_ref, normed_mlp_ref, q_ref, k_ref, v_ref, probs_ref, ctx_ref, expanded_ref,
    gains_ref, qkv_ref, out_ref, last_gain_ref,
    gblock_ref, grad_ref, mine_ref, theirs_ref,
    gctx_ref, dq_ref, dk_ref, dv_ref, wbuf_ref, sems,
):
    masks = head_rows()
    gblock, gbranch, gain_grad = attention_backward_part(
        hat_ref[...], inv_ref[...], gains_ref[0:1, :], qkv_ref, out_ref, ghid_ref[...],
        q_ref, k_ref, v_ref, probs_ref, ctx_ref, gctx_ref, dq_ref, dk_ref, dv_ref, grad_ref, masks,
    )
    gblock_ref[...] = gblock.astype(BF16)
    weight_grads(
        wbuf_ref, normed_ref[...], dq_ref[...], dk_ref[...], dv_ref[...], ctx_ref[...], gbranch,
        normed_mlp_ref[...], gpre_ref, expanded_ref, g_ref[...],
    )
    gains = jnp.concatenate([gain_grad, mlp_gain_ref[...], last_gain_ref[0:1, :], last_gain_ref[1:2, :]], axis=1)
    for h in range(2):
        wbuf_ref[h, PART:, :] = jnp.zeros((EXTRA, 128), BF16)
    for j in range(6):
        tile = jnp.concatenate([gains[:, j * 128 : (j + 1) * 128], jnp.zeros((15, 128), F32)], axis=0)
        wbuf_ref[0, PART + j * 16 : PART + (j + 1) * 16, :] = tile.astype(BF16)
    split_halves(wbuf_ref, mine_ref, theirs_ref, sems)


def first_finish(gblock_ref, grad_ref, last_table_ref, trows_ref, tcols_ref, pick_ref, gin_ref, tables_ref):
    tables_ref[0:TROWS, :] = collapse_table(grad_ref, trows_ref, tcols_ref)
    tables_ref[TROWS : 2 * TROWS, :] = last_table_ref[...]
    gin_ref[...] = scatter_tokens(pick_ref[...], gblock_ref[...].astype(F32)).astype(BF16)


def pack(first_ref, first_other_ref, last_ref, last_other_ref, packed_ref):
    first = (first_ref[...].astype(F32) + first_other_ref[...].astype(F32)).astype(BF16)
    packed_ref[:PART, :] = first[:PART]
    packed_ref[PART : 2 * PART, :] = (last_ref[...].astype(F32) + last_other_ref[...].astype(F32)).astype(BF16)
    packed_ref[2 * PART :, :] = first[PART:]


def add_two(mine_ref, other_ref, total_ref):
    total_ref[...] = (mine_ref[...].astype(F32) + other_ref[...].astype(F32)).astype(BF16)


def sum_parts(parts_ref, total_ref):
    total = parts_ref[0].astype(F32)
    for j in range(1, 16):
        total += parts_ref[j].astype(F32)
    total_ref[...] = total.astype(BF16)


def sum_and_spread(*refs):
    total = refs[0][...].astype(F32)
    for ref in refs[1:-1]:
        total += ref[...].astype(F32)
    total = total.astype(BF16)
    for j in range(16):
        refs[-1][j] = total


def unpack(
    mine_ref, other_ref, t0_ref, t1_ref, t2_ref, t3_ref, qkv_ref, out_ref, up_ref, down_ref, gains_ref, table_ref, sum_ref
):
    core = lax.rem(lax.axis_index("lat"), 2)

    def load(half, start, count):
        here = mine_ref[start : start + count, :].astype(F32)
        there = other_ref[start : start + count, :].astype(F32)
        return jnp.where(core == half, here, there)

    total = t0_ref[...].astype(F32)
    for ref in (t1_ref, t2_ref, t3_ref):
        total += ref[...].astype(F32)
    sum_ref[...] = total
    for b in range(2):
        for j in range(18):
            tile = load(j // 9, b * PART + j % 9 * DIM, DIM)
            if j < 6:
                up_ref[b, :, j * 128 : (j + 1) * 128] = tile
            elif j < 12:
                down_ref[b, :, (j - 6) * 128 : (j - 5) * 128] = tile
            elif j < 16:
                qkv_ref[b, :, (j - 12) * 128 : (j - 11) * 128] = tile
            elif j == 16:
                qkv_ref[b, :, 512:576] = tile[:, :64]
                out_ref[b, :, 0:64] = tile[:, 64:]
            else:
                out_ref[b, :, 64:192] = tile
        for j in range(26):
            place = b * TROWS + j * 8
            piece = sum_ref[place : place + HEADS, :]
            width = min(128, TABLE - j * 128)
            for h in range(HEADS):
                table_ref[b * HEADS + h, :, j * 128 : j * 128 + width] = piece[h : h + 1, :width]
    gains = jnp.concatenate([load(0, 2 * PART + j * 16, 16)[0:1] for j in range(6)], axis=1)
    for b in range(2):
        for i in range(2):
            k = b * 2 + i
            gains_ref[b, i : i + 1, :] = gains[:, k * DIM : (k + 1) * DIM]


def whole(array):
    return pl.BlockSpec(array.shape, lambda i: (0,) * array.ndim)


def picked(array, index):
    rest = array.shape[1:]
    return pl.BlockSpec((None,) + rest, lambda i: (index,) + (0,) * len(rest))


def in_place():
    return pl.BlockSpec(memory_space=pl.ANY)


def call(kernel, operands, specs, outs, scratch=(), micros=2, out_specs=None, mebibytes=10):
    shapes = [jax.ShapeDtypeStruct(shape, dtype) for shape, dtype in outs]
    moved = sum(a.size * a.dtype.itemsize for a in (*operands, *shapes))
    return pl.pallas_call(
        kernel,
        grid=(1,),
        out_shape=shapes,
        in_specs=specs,
        out_specs=out_specs or [whole(s) for s in shapes],
        scratch_shapes=list(scratch),
        cost_estimate=pl.CostEstimate(flops=micros * 1_100_000_000, bytes_accessed=moved, transcendentals=0),
        compiler_params=pltpu.CompilerParams(vmem_limit_bytes=mebibytes * 1024 * 1024),
    )(*operands)


def neighbour(sizes, steps):
    pairs = []
    for a in range(sizes[0]):
        for b in range(sizes[1]):
            source = ((a + steps[0]) % sizes[0]) * sizes[1] + (b + steps[1]) % sizes[1]
            pairs.append((source, a * sizes[1] + b))
    return pairs


def exchange(rows, side, corner, sizes, step):
    both = ("lat", "lon")
    rows = lax.ppermute(rows, both, neighbour(sizes, (step, 0)))
    side = lax.ppermute(side, both, neighbour(sizes, (0, step)))
    corner = lax.ppermute(corner, both, neighbour(sizes, (step, step)))
    return rows, side, corner


def vmem(shape, dtype):
    return pltpu.VMEM(shape, dtype)


def device_place(i):
    lat, lon = divmod(i, 8)
    return lat // 8, lat // 2 % 4, lat % 2, lon // 2, lon % 2


def flat_device(z_hi, y, core, x, z_lo):
    return ((z_hi * 4 + y) * 2 + core) * 8 + x * 2 + z_lo


def shifted_pairs(core=0, x=0, z_lo=0):
    pairs = []
    for i in range(128):
        h, y, c, a, b = device_place(i)
        pairs.append((flat_device(h, y, (c + core) % 2, (a + x) % 4, (b + z_lo) % 2), i))
    return pairs


def moved(array, **steps):
    return lax.ppermute(array, ("lat", "lon"), shifted_pairs(**steps))


def sum_over_devices(first, last, finish):
    both = ("lat", "lon")
    planes = {}
    for i in range(128):
        _, _, c, a, _ = device_place(i)
        planes.setdefault((c, a), []).append(i)
    groups = list(planes.values())

    def run(kernel, operands, shape):
        [result] = call(kernel, operands, [whole(a) for a in operands], [(shape, BF16)])
        return result

    sent = run(pack, [first[0], moved(first[1], core=1), *last], (HALF, 128))
    sent, finish = lax.optimization_barrier((sent, finish))
    parts = lax.all_to_all(sent.reshape(16, CHUNK, 128), both, 0, 0, axis_index_groups=groups)
    outs = [((GRID, 2 * DIM), BF16), ((2 * TROWS, 128), BF16)]
    grad_inputs, tables = call(first_finish, finish, [whole(a) for a in finish], outs)
    parts, tables = lax.optimization_barrier((parts, tables))
    total = run(sum_parts, [parts], (CHUNK, 128))
    spread = run(sum_and_spread, [total] + [moved(total, x=k) for k in (1, 2, 3)], (16, CHUNK, 128))
    tables = run(add_two, [tables, moved(tables, z_lo=1)], tables.shape)
    spread, tables = lax.optimization_barrier((spread, tables))
    half = lax.all_to_all(spread, both, 0, 0, axis_index_groups=groups)
    table_terms = [tables] + [moved(tables, x=k) for k in (1, 2, 3)]
    half, table_terms = lax.optimization_barrier((half, table_terms))
    half = half.reshape(HALF, 128)
    operands = [half, moved(half, core=1), *table_terms]
    outs = [((2, DIM, 3 * DIM), F32), ((2, DIM, DIM), F32), ((2, DIM, UNITS), F32), ((2, DIM, UNITS), F32)]
    outs += [((2, 2, DIM), F32), ((2 * HEADS, 1, TABLE), F32)]
    grads = call(unpack, operands, [whole(a) for a in operands], outs, [vmem((2 * TROWS, 128), F32)])
    return grad_inputs, grads


def on_device(sizes, inputs, cotangent, norm_gains, qkv_weight, out_weight, up_weight, down_weight, bias_table):
    x = inputs.reshape(GRID, 2 * DIM)
    cot = cotangent.reshape(GRID, 2 * DIM)
    trows, tcols = jnp.asarray(table_rows(), BF16), jnp.asarray(table_cols(), BF16)
    pick_grid, pick_shift, pick_back = (
        jnp.asarray(m, BF16) for m in (grid_picker(), shifted_picker(), returned_picker())
    )
    strips = jnp.asarray(strip_picker(), BF16)
    weights = (norm_gains, qkv_weight, out_weight, up_weight, jnp.swapaxes(down_weight, 1, 2))
    tok, src, hid = (TOKENS, DIM), (SOURCE, 2 * DIM), (TOKENS, UNITS)
    probs = (WINDOWS, WIN_TOK, QLANES)

    def table_spec(index):
        return pl.BlockSpec((HEADS, 1, TABLE), lambda i: (index, 0, 0))

    bias_table = bias_table.reshape(2 * HEADS, 1, TABLE)
    gains, qkv, out, up, down = weights
    wide_tok, wide_hid = (tok, BF16), (hid, BF16)
    bias = (WIN_TOK, QLANES)

    def specs_for(arrays, index):
        specs = []
        for a in arrays:
            if any(a is w for w in weights):
                specs.append(picked(a, index))
            elif a is bias_table:
                specs.append(table_spec(index))
            else:
                specs.append(whole(a))
        return specs

    operands = [x, pick_grid, gains, qkv, bias_table, trows, tcols, out]
    outs = [wide_tok] * 4 + [(probs, BF16), wide_tok, (tok, F32)]
    scratch = [vmem(bias, F32), vmem(x.shape, BF16), vmem(pick_grid.shape, BF16), vmem((2, DIM), F32), vmem((DIM, 3 * DIM), BF16)]
    scratch += [vmem((HEADS, 1, TABLE), F32), vmem(trows.shape, BF16), vmem(tcols.shape, BF16), vmem((DIM, DIM), BF16)]
    scratch += [pltpu.SemaphoreType.DMA((8,))]
    operands = [pltpu.with_memory_space_constraint(a, pltpu.HBM) for a in operands]
    specs = [in_place()] * 8
    results = call(first_attention, operands, specs, outs, scratch, 7, mebibytes=14)
    xw, q, k, v, probs_first, ctx, hidden = results

    operands = [hidden, cot, gains, up, down, pick_grid, strips]
    strip_outs = [((288, 2 * DIM), BF16), ((2 * STRIP, 2 * DIM), BF16), ((2 * STRIP, 2 * DIM), BF16)]
    outs = [wide_hid, wide_hid, ((144, 2 * DIM), BF16)] + strip_outs
    results = call(first_mlp, operands, specs_for(operands, 0), outs, (), 4, mebibytes=14)
    expanded, slope, bottom, *sent = results
    sent, bias_table, xw = lax.optimization_barrier((sent, bias_table, xw))

    arrived = exchange(*sent, sizes, 1)
    operands = [bias_table, trows, tcols]
    [bias_last] = call(second_bias, operands, specs_for(operands, 1), [(bias, F32)], (), 2, mebibytes=14)

    operands = [xw, hidden, gains]
    norm_outs = [(tok, F32), ((TOKENS, 1), F32), wide_tok]
    norms = call(first_norms, operands, specs_for(operands, 0), norm_outs * 2, (), 1, mebibytes=14)
    hat, inv, normed_first, hat_mlp, inv_mlp, normed_mlp = norms

    operands = [bottom, *arrived, cot, bias_last, *weights, pick_shift]
    outs = [((144, 2 * DIM), BF16)] * 2 + strip_outs + [wide_tok] * 8 + [wide_hid] * 2 + [(bias, F32), ((2, DIM), F32)]
    scratch = [vmem(src, BF16), vmem(tok, F32), vmem(tok, F32)] + [vmem(tok, BF16)] * 3 + [vmem(probs, BF16), vmem(tok, BF16)]
    results = call(second_both, operands, specs_for(operands, 1), outs, scratch, 12, mebibytes=14)
    back_own, y_own, sent, terms, last_gain = results[0], results[1], results[2:5], results[5:16], results[16]

    arrived = exchange(*sent, sizes, -1)
    g, *terms = terms
    operands = [*terms, g, trows, tcols]
    outs = [((PART, 128), BF16)] * 2 + [((TROWS, 128), BF16)]
    out_specs = [in_place()] * 2 + [whole(jax.ShapeDtypeStruct(*o)) for o in outs[2:]]
    scratch = [vmem((2, PART, 128), BF16), pltpu.SemaphoreType.DMA((2,))]
    results = call(second_weights, operands, specs_for(operands, 1), outs, scratch, 4, out_specs, 14)
    last_mine, last_theirs, last_table = results

    operands = [back_own, *arrived, hat_mlp, inv_mlp, slope, gains, up, down, pick_back]
    outs = [wide_tok, (tok, F32), wide_hid, ((1, DIM), F32)]
    results = call(first_mlp_back, operands, specs_for(operands, 0), outs, [vmem(src, BF16)], 3, mebibytes=14)
    g, ghid, gpre, mlp_gain = results
    ghid, last_theirs = lax.optimization_barrier((ghid, last_theirs))
    last = [last_mine, moved(last_theirs, core=1)]

    operands = [ghid, g, gpre, mlp_gain, hat, inv, normed_first, normed_mlp, q, k, v, probs_first, ctx, expanded, gains, qkv, out]
    operands += [last_gain]
    first_shape = (PART + EXTRA, 128)
    outs = [wide_tok, (bias, F32), (first_shape, BF16), (first_shape, BF16)]
    out_specs = [whole(jax.ShapeDtypeStruct(*o)) for o in outs[:2]] + [in_place()] * 2
    scratch = [vmem(tok, BF16)] * 4 + [vmem((2, *first_shape), BF16), pltpu.SemaphoreType.DMA((2,))]
    gblock, grad_scores, *first = call(
        first_attention_back, operands, specs_for(operands, 0), outs, scratch, 8, out_specs, 14
    )
    last, first = lax.optimization_barrier((last, first))
    finish = [gblock, grad_scores, last_table, trows, tcols, pick_grid]
    grad_inputs, grads = sum_over_devices(first, last, finish)
    y_rows, y_side, y_corner = arrived
    rows = jnp.concatenate([y_rows[144:], y_own]).reshape(ROWS, COLS, 2 * DIM)
    edge = jnp.concatenate([a[STRIP : STRIP + 18].reshape(3, 6, 2 * DIM) for a in (y_corner, y_side)])
    output = jnp.concatenate([edge, rows[:, 6:]], axis=1)

    grad_qkv, grad_out, grad_up, grad_down, grad_gains, grad_table = grads
    grad_down = jnp.swapaxes(grad_down, 1, 2)
    grad_table = grad_table.reshape(2, 1, HEADS, TABLE)
    return (output, grad_inputs.reshape(ROWS, COLS, 2 * DIM), grad_gains, grad_qkv, grad_out, grad_up, grad_down, grad_table)


def solution(mesh):
    sizes = (mesh.shape["lat"], mesh.shape["lon"])

    def program(*arguments):
        return on_device(sizes, *arguments)

    fields, tables = P("lat", "lon", None), P(None, "lat", None, None)
    return jax.shard_map(
        program,
        mesh=mesh,
        in_specs=(fields, fields, P(), P(), P(), P(), P(), tables),
        out_specs=(fields, fields, P(), P(), P(), P(), P(), tables),
        check_vma=False,
    )
```

```python
import math

import jax
import jax.numpy as jnp
import numpy as np
from jax import lax
from jax.experimental import pallas as pl
from jax.experimental.pallas import tpu as pltpu
from jax.sharding import PartitionSpec as P

DIM = 192
HEADS = 6
HEAD_DIM = 32
UNITS = 768
ROWS = 6
COLS = 48
WIN_COLS = 12
WINDOWS = 4
WIN_TOK = 144
TOKENS = 576
GRID = ROWS * COLS
GROUP = 12
SPAN = 23
WIDE = SPAN * GROUP
CELL = 6 * SPAN
TABLE = 24 * CELL
QLANES = HEADS * WIN_TOK
STRIP = 32
SOURCE = 288 + 2 * STRIP
NORM_EPS = 1e-05
MASK_VALUE = -100.0
LOG2E = math.log2(math.e)
SCALE = 1.0 / math.sqrt(HEAD_DIM)
WBLOCK = 18 * DIM
CHUNK = 224
HALF = 16 * CHUNK
PART = 9 * DIM
EXTRA = HALF - 2 * PART
TROWS = 208

F32 = jnp.float32
BF16 = jnp.bfloat16


def token_places():
    t = np.arange(TOKENS)
    w, rest = t // WIN_TOK, t % WIN_TOK
    c, l, r = rest // GROUP, rest % GROUP // ROWS, rest % ROWS
    return r, w * WIN_COLS + c, l


def one_hot(places, size):
    return (places[:, None] == np.arange(size)[None, :]).astype(np.float32)


def grid_picker():
    r, j, _ = token_places()
    return one_hot(r * COLS + j, GRID)


def shifted_picker():
    r, j, _ = token_places()
    half = np.where(r < 3, r, r - 3)
    inner = np.where(r < 3, 0, 144) + half * COLS + j + 6
    edge = np.where(r < 3, 288, 288 + STRIP) + half * 6 + j - 42
    return one_hot(np.where(j < 42, inner, edge), SOURCE)


def returned_picker():
    r, j, _ = token_places()
    half = np.where(r >= 3, r - 3, r)
    inner = np.where(r >= 3, 0, 144) + half * COLS + j
    edge = np.where(r >= 3, 288, 288 + STRIP) + half * 6 + j
    return one_hot(np.where(j >= 6, inner, edge), SOURCE)


def strip_picker():
    picked = np.zeros((2 * STRIP, GRID), np.float32)
    for i in range(3):
        for j in range(6):
            picked[i * 6 + j, (i + 3) * COLS + j] = 1
            picked[STRIP + i * 6 + j, i * COLS + j] = 1
    return picked


def table_rows():
    picked = np.zeros((2, HEADS * 16, 24 * 8), np.float32)
    for h in range(HEADS):
        for lq in range(2):
            for lp in range(2):
                for rq in range(6):
                    picked[lp, h * 16 + lq * 6 + rq, (lq * 12 + lp * 6 + rq) * 8 + h] = 1
    return picked


def table_cols():
    picked = np.zeros((2, 6 * SPAN, WIDE), np.float32)
    for lp in range(2):
        for rp in range(6):
            for d in range(SPAN):
                picked[lp, rp * SPAN + d, d * GROUP + lp * 6 + rp] = 1
    return picked


def nn(a, b):
    return jnp.dot(a, b, preferred_element_type=F32)


def nt(a, b):
    return lax.dot_general(a, b, (((1,), (1,)), ((), ())), preferred_element_type=F32)


def tn(a, b):
    return lax.dot_general(a, b, (((0,), (0,)), ((), ())), preferred_element_type=F32)


def level_mask():
    t = lax.broadcasted_iota(jnp.int32, (TOKENS, DIM), 0)
    return (lax.div(t, 6) & 1) == 1


def gather_tokens(picker, source):
    return jnp.where(level_mask(), nn(picker, source[:, DIM:]), nn(picker, source[:, :DIM]))


def scatter_tokens(picker, tokens):
    upper = level_mask()
    zero = jnp.zeros_like(tokens)
    low = tn(picker, jnp.where(upper, zero, tokens).astype(BF16))
    high = tn(picker, jnp.where(upper, tokens, zero).astype(BF16))
    return jnp.concatenate([low, high], axis=1)


def normalize(x):
    centre = jnp.mean(x, axis=-1, keepdims=True)
    off = x - centre
    spread = jnp.mean(off * off, axis=-1, keepdims=True)
    inv = lax.rsqrt(spread + NORM_EPS)
    return off * inv, inv


def norm_backward(grad, gain, hat, inv):
    scaled = grad * gain
    mean_one = jnp.mean(scaled, axis=-1, keepdims=True)
    mean_two = jnp.mean(scaled * hat, axis=-1, keepdims=True)
    return inv * (scaled - mean_one - hat * mean_two)


def gelu_parts(x):
    below = 0.5 + 0.5 * lax.erf(x * math.sqrt(0.5))
    return below, jnp.exp2(x * x * (-0.5 * LOG2E)) * (1.0 / math.sqrt(2.0 * math.pi))


def head_rows():
    lane = lax.div(lax.broadcasted_iota(jnp.int32, (1, DIM), 1), HEAD_DIM)
    return [(lane == h) for h in range(HEADS)]


def stack_heads(x, masks):
    return jnp.concatenate([jnp.where(m, x, jnp.zeros_like(x)) for m in masks], axis=0)


def fold_heads(x, masks):
    folded = x[:WIN_TOK]
    for h in range(1, HEADS):
        folded = jnp.where(masks[h], x[h * WIN_TOK : (h + 1) * WIN_TOK], folded)
    return folded


def expand_table(table_ref, trows_ref, tcols_ref, bias_ref):
    table = jnp.concatenate([table_ref[h] for h in range(HEADS)] + [jnp.zeros((2, TABLE), F32)], axis=0) * LOG2E
    table = jnp.concatenate([table[:, k * CELL : (k + 1) * CELL] for k in range(24)], axis=0)
    high = table.astype(BF16)
    low = (table - high.astype(F32)).astype(BF16)
    wide = jnp.zeros((HEADS * 16, WIDE), F32)
    for lp in range(2):
        for part in (high, low):
            wide += nn(nn(trows_ref[lp], part).astype(BF16), tcols_ref[lp])
    for cq in range(WIN_COLS):
        start = GROUP * (WIN_COLS - 1 - cq)
        row = jnp.concatenate(
            [wide[h * 16 : h * 16 + GROUP, start : start + WIN_TOK] for h in range(HEADS)], axis=1
        )
        bias_ref[cq * GROUP : (cq + 1) * GROUP, :] = row


def add_mask(bias_ref, flag):
    key = lax.broadcasted_iota(jnp.int32, (WIN_TOK, 1), 0)
    query = lax.broadcasted_iota(jnp.int32, (1, QLANES), 1)
    key_up = (lax.div(key, 3) & 1).astype(F32)
    query_up = (lax.div(query, 3) & 1).astype(F32)
    apart = jnp.abs(key_up - query_up)
    bias_ref[...] += apart * (flag * (MASK_VALUE * LOG2E))


def collapse_table(grad_ref, trows_ref, tcols_ref):
    parts = []
    for h in range(HEADS):
        total = None
        for cq in range(WIN_COLS):
            start = GROUP * (WIN_COLS - 1 - cq)
            piece = grad_ref[cq * GROUP : (cq + 1) * GROUP, h * WIN_TOK : (h + 1) * WIN_TOK]
            pads = [jnp.zeros((GROUP, start), F32)] if start else []
            tail = WIDE - start - WIN_TOK
            pads_after = [jnp.zeros((GROUP, tail), F32)] if tail else []
            piece = jnp.concatenate(pads + [piece] + pads_after, axis=1)
            total = piece if total is None else total + piece
        parts.append(jnp.concatenate([total, jnp.zeros((16 - GROUP, WIDE), F32)], axis=0))
    wide = jnp.concatenate(parts, axis=0).astype(BF16)
    result = jnp.zeros((24 * 8, CELL), F32)
    for lp in range(2):
        narrow = nt(wide, tcols_ref[lp]).astype(BF16)
        result += tn(trows_ref[lp], narrow)
    cells = [result[k * 8 : (k + 1) * 8] for k in range(24)] + [jnp.zeros((8, 26 * 128 - TABLE), F32)]
    flat = jnp.concatenate(cells, axis=1)
    return jnp.concatenate([flat[:, j * 128 : (j + 1) * 128] for j in range(26)], axis=0).astype(BF16)


def attention(q_ref, k_ref, v_ref, bias_ref, probs_ref, ctx_ref, masks):
    for w in range(WINDOWS):
        rows = pl.ds(w * WIN_TOK, WIN_TOK)
        stacked = stack_heads(q_ref[rows, :], masks)
        scores = nt(k_ref[rows, :], stacked) * (SCALE * LOG2E) + bias_ref[...]
        weights = jnp.exp2(scores)
        inverse = 1.0 / jnp.sum(weights, axis=0, keepdims=True)
        probs = (weights * inverse).astype(BF16)
        probs_ref[w] = probs
        ctx_ref[rows, :] = fold_heads(tn(probs, v_ref[rows, :]), masks).astype(BF16)


def attention_back(q_ref, k_ref, v_ref, probs_ref, gctx_ref, dq_ref, dk_ref, dv_ref, grad_ref, masks):
    for w in range(WINDOWS):
        rows = pl.ds(w * WIN_TOK, WIN_TOK)
        stacked_g = stack_heads(gctx_ref[rows, :], masks)
        stacked_q = stack_heads(q_ref[rows, :], masks)
        probs_half = probs_ref[w]
        probs = probs_half.astype(F32)
        grad_probs = nt(v_ref[rows, :], stacked_g)
        inner = jnp.sum(grad_probs * probs, axis=0, keepdims=True)
        grad_scores = probs * (grad_probs - inner)
        if w == 0:
            grad_ref[...] = grad_scores
        else:
            grad_ref[...] += grad_scores
        half = grad_scores.astype(BF16)
        dv_ref[rows, :] = nn(probs_half, stacked_g).astype(BF16)
        dk_ref[rows, :] = (nn(half, stacked_q) * SCALE).astype(BF16)
        dq_ref[rows, :] = (fold_heads(tn(half, k_ref[rows, :]), masks) * SCALE).astype(BF16)


def project(normed, qkv_ref, q_ref, k_ref, v_ref):
    for i, ref in enumerate((q_ref, k_ref, v_ref)):
        ref[...] = nn(normed, qkv_ref[:, i * DIM : (i + 1) * DIM]).astype(BF16)


def put_weights(wbuf_ref, offset, value):
    tiles = value.shape[1] // 128
    for j in range(tiles):
        half, place = divmod(offset + j, 9)
        wbuf_ref[half, place * DIM : (place + 1) * DIM, :] = value[:, j * 128 : (j + 1) * 128].astype(BF16)


def weight_grads(wbuf_ref, normed, dq, dk, dv, ctx, gbranch, normed_mlp, gpre_ref, expanded_ref, g):
    for j in range(3):
        cols = slice(j * 256, (j + 1) * 256)
        put_weights(wbuf_ref, 2 * j, tn(normed_mlp, gpre_ref[:, cols]))
        put_weights(wbuf_ref, 6 + 2 * j, tn(g, expanded_ref[:, cols]))
    put_weights(wbuf_ref, 12, tn(normed, jnp.concatenate([dq, dk], axis=1)))
    put_weights(wbuf_ref, 15, jnp.concatenate([tn(normed, dv), tn(ctx, gbranch)], axis=1))


def attention_backward_part(
    hat, inv, gain, qkv_ref, out_ref, ghid, q_ref, k_ref, v_ref, probs_ref, ctx_ref, gctx_ref, dq_ref, dk_ref, dv_ref, grad_ref, masks
):
    gbranch = ghid.astype(BF16)
    gctx_ref[...] = nt(gbranch, out_ref[...]).astype(BF16)
    attention_back(q_ref, k_ref, v_ref, probs_ref, gctx_ref, dq_ref, dk_ref, dv_ref, grad_ref, masks)
    gnormed = nt(dq_ref[...], qkv_ref[:, :DIM])
    gnormed += nt(dk_ref[...], qkv_ref[:, DIM : 2 * DIM])
    gnormed += nt(dv_ref[...], qkv_ref[:, 2 * DIM :])
    gnormed = gnormed.astype(BF16).astype(F32)
    gain_grad = jnp.sum(gnormed * hat, axis=0, keepdims=True)
    gblock = norm_backward(gnormed, gain, hat, inv) + ghid
    return gblock, gbranch, gain_grad


def first_attention(
    far_x, far_pick, far_gains, far_qkv, far_table, far_trows, far_tcols, far_out,
    xw_ref, q_ref, k_ref, v_ref, probs_ref, ctx_ref, hidden_ref,
    bias_ref, x_ref, pick_ref, gains_ref, qkv_ref, table_ref, trows_ref, tcols_ref, out_ref, sems,
):
    pairs = [
        (far_table.at[pl.ds(0, HEADS)], table_ref), (far_trows, trows_ref), (far_tcols, tcols_ref),
        (far_x, x_ref), (far_pick, pick_ref), (far_gains.at[0], gains_ref), (far_qkv.at[0], qkv_ref), (far_out.at[0], out_ref),
    ]
    fetches = [pltpu.make_async_copy(far, near, sems.at[i]) for i, (far, near) in enumerate(pairs)]
    for fetch in fetches:
        fetch.start()
    for fetch in fetches[:3]:
        fetch.wait()
    expand_table(table_ref, trows_ref, tcols_ref, bias_ref)
    for fetch in fetches[3:]:
        fetch.wait()
    x = gather_tokens(pick_ref[...], x_ref[...])
    xw_ref[...] = x.astype(BF16)
    hat, _ = normalize(x)
    project((hat * gains_ref[0:1, :]).astype(BF16), qkv_ref, q_ref, k_ref, v_ref)
    attention(q_ref, k_ref, v_ref, bias_ref, probs_ref, ctx_ref, head_rows())
    branch = nn(ctx_ref[...], out_ref[...]).astype(BF16)
    hidden_ref[...] = xw_ref[...].astype(F32) + branch.astype(F32)


def first_mlp(
    hidden_ref, cot_ref, gains_ref, up_ref, down_ref, pick_ref, strips_ref,
    expanded_ref, slope_ref, bottom_ref, row_ref, side_ref, corner_ref,
):
    row_ref[144:, :] = cot_ref[:144, :]
    edges = nn(strips_ref[...], cot_ref[...]).astype(BF16)
    side_ref[STRIP:, :] = edges[:STRIP]
    corner_ref[STRIP:, :] = edges[STRIP:]
    hidden = hidden_ref[...]
    hat, _ = normalize(hidden)
    normed_mlp = (hat * gains_ref[1:2, :]).astype(BF16)
    total = hidden
    for j in range(3):
        cols = slice(j * 256, (j + 1) * 256)
        pre = nn(normed_mlp, up_ref[:, cols])
        below, density = gelu_parts(pre)
        expanded = (pre * below).astype(BF16)
        expanded_ref[:, cols] = expanded
        slope_ref[:, cols] = (below + pre * density).astype(BF16)
        total = total + nt(expanded, down_ref[:, cols])
    grid = scatter_tokens(pick_ref[...], total.astype(BF16)).astype(BF16)
    row_ref[:144, :] = grid[:144]
    bottom_ref[...] = grid[144:]
    edges = nn(strips_ref[...], grid).astype(BF16)
    side_ref[:STRIP, :] = edges[:STRIP]
    corner_ref[:STRIP, :] = edges[STRIP:]


def fill_source(source_ref, own, row_ref, side_ref, corner_ref, part):
    source_ref[0:144, :] = own
    source_ref[144:288, :] = row_ref[part * 144 : (part + 1) * 144, :]
    source_ref[288 : 288 + STRIP, :] = side_ref[part * STRIP : (part + 1) * STRIP, :]
    source_ref[288 + STRIP :, :] = corner_ref[part * STRIP : (part + 1) * STRIP, :]


def put_source(own_ref, row_ref, side_ref, corner_ref, part, value):
    own_ref[...] = value[0:144]
    row_ref[part * 144 : (part + 1) * 144, :] = value[144:288]
    side_ref[part * STRIP : (part + 1) * STRIP, :] = value[288 : 288 + STRIP]
    corner_ref[part * STRIP : (part + 1) * STRIP, :] = value[288 + STRIP :]


def split_halves(wbuf_ref, mine_ref, theirs_ref, sems):
    core = lax.rem(lax.axis_index("lat"), 2)
    send = pltpu.make_async_copy(wbuf_ref.at[1 - core], theirs_ref, sems.at[0])
    keep = pltpu.make_async_copy(wbuf_ref.at[core], mine_ref, sems.at[1])
    send.start()
    keep.start()
    send.wait()
    keep.wait()


def second_bias(table_ref, trows_ref, tcols_ref, bias_ref):
    expand_table(table_ref, trows_ref, tcols_ref, bias_ref)
    add_mask(bias_ref, (lax.axis_index("lat") == lax.axis_size("lat") - 1).astype(F32))


def second_both(
    own_ref, row_ref, side_ref, corner_ref, cot_ref, bias_ref,
    gains_ref, qkv_ref, out_ref, up_ref, down_ref, pick_ref,
    back_own_ref, y_own_ref, sent_row_ref, sent_side_ref, sent_corner_ref,
    g_ref, normed_ref, dq_ref, dk_ref, dv_ref, ctx_ref, gbranch_ref, normed_mlp_ref, gpre_ref, expanded_ref, grad_ref, gain_grad_ref,
    source_ref, x_ref, hat_ref, q_ref, k_ref, v_ref, probs_ref, gctx_ref,
):
    masks = head_rows()
    fill_source(source_ref, own_ref[...], row_ref, side_ref, corner_ref, 0)
    x_ref[...] = gather_tokens(pick_ref[...], source_ref[...])
    fill_source(source_ref, cot_ref[144:288, :], row_ref, side_ref, corner_ref, 1)
    g_ref[...] = gather_tokens(pick_ref[...], source_ref[...]).astype(BF16)
    hat, inv = normalize(x_ref[...])
    normed_ref[...] = (hat * gains_ref[0:1, :]).astype(BF16)
    hat_ref[...] = hat
    project(normed_ref[...], qkv_ref, q_ref, k_ref, v_ref)
    attention(q_ref, k_ref, v_ref, bias_ref, probs_ref, ctx_ref, masks)
    branch = nn(ctx_ref[...], out_ref[...]).astype(BF16)
    hidden = x_ref[...] + branch.astype(F32)
    hat_mlp, inv_mlp = normalize(hidden)
    normed_mlp = (hat_mlp * gains_ref[1:2, :]).astype(BF16)
    normed_mlp_ref[...] = normed_mlp
    total = hidden
    gnormed = jnp.zeros((TOKENS, DIM), F32)
    for j in range(3):
        cols = slice(j * 256, (j + 1) * 256)
        pre = nn(normed_mlp, up_ref[:, cols])
        below, density = gelu_parts(pre)
        expanded = (pre * below).astype(BF16)
        expanded_ref[:, cols] = expanded
        total = total + nt(expanded, down_ref[:, cols])
        gact = nn(g_ref[...], down_ref[:, cols]).astype(BF16).astype(F32)
        gpre = ((below + pre * density) * gact).astype(BF16)
        gpre_ref[:, cols] = gpre
        gnormed = gnormed + nt(gpre, up_ref[:, cols])
    y = scatter_tokens(pick_ref[...], total.astype(BF16)).astype(BF16)
    put_source(y_own_ref, sent_row_ref, sent_side_ref, sent_corner_ref, 1, y)
    gnormed = gnormed.astype(BF16).astype(F32)
    gain_grad_ref[1:2, :] = jnp.sum(gnormed * hat_mlp, axis=0, keepdims=True)
    ghid = g_ref[...].astype(F32) + norm_backward(gnormed, gains_ref[1:2, :], hat_mlp, inv_mlp)
    gblock, gbranch, gain_grad = attention_backward_part(
        hat_ref[...], inv, gains_ref[0:1, :], qkv_ref, out_ref, ghid,
        q_ref, k_ref, v_ref, probs_ref, ctx_ref, gctx_ref, dq_ref, dk_ref, dv_ref, grad_ref, masks,
    )
    gain_grad_ref[0:1, :] = gain_grad
    back = scatter_tokens(pick_ref[...], gblock.astype(BF16)).astype(BF16)
    put_source(back_own_ref, sent_row_ref, sent_side_ref, sent_corner_ref, 0, back)
    gbranch_ref[...] = gbranch


def second_weights(
    normed_ref, dq_ref, dk_ref, dv_ref, ctx_ref, gbranch_ref, normed_mlp_ref, gpre_ref, expanded_ref, grad_ref, g_ref,
    trows_ref, tcols_ref, mine_ref, theirs_ref, table_grad_ref, wbuf_ref, sems,
):
    weight_grads(
        wbuf_ref, normed_ref[...], dq_ref[...], dk_ref[...], dv_ref[...], ctx_ref[...], gbranch_ref[...],
        normed_mlp_ref[...], gpre_ref, expanded_ref, g_ref[...],
    )
    table_grad_ref[...] = collapse_table(grad_ref, trows_ref, tcols_ref)
    split_halves(wbuf_ref, mine_ref, theirs_ref, sems)


def first_norms(xw_ref, hidden_ref, gains_ref, hat_ref, inv_ref, normed_ref, hat_mlp_ref, inv_mlp_ref, normed_mlp_ref):
    hat, inv = normalize(xw_ref[...].astype(F32))
    hat_ref[...] = hat
    inv_ref[...] = inv
    normed_ref[...] = (hat * gains_ref[0:1, :]).astype(BF16)
    hat, inv = normalize(hidden_ref[...])
    hat_mlp_ref[...] = hat
    inv_mlp_ref[...] = inv
    normed_mlp_ref[...] = (hat * gains_ref[1:2, :]).astype(BF16)


def first_mlp_back(
    back_ref, row_ref, side_ref, corner_ref, hat_mlp_ref, inv_mlp_ref, slope_ref, gains_ref, up_ref, down_ref, returned_ref,
    g_ref, ghid_ref, gpre_ref, gain_grad_ref, source_ref,
):
    fill_source(source_ref, back_ref[...], row_ref, side_ref, corner_ref, 0)
    g32 = gather_tokens(returned_ref[...], source_ref[...])
    g = g32.astype(BF16)
    g_ref[...] = g
    hat_mlp, inv_mlp = hat_mlp_ref[...], inv_mlp_ref[...]
    gnormed = jnp.zeros((TOKENS, DIM), F32)
    for j in range(3):
        cols = slice(j * 256, (j + 1) * 256)
        gact = nn(g, down_ref[:, cols]).astype(BF16).astype(F32)
        gpre = (slope_ref[:, cols].astype(F32) * gact).astype(BF16)
        gpre_ref[:, cols] = gpre
        gnormed = gnormed + nt(gpre, up_ref[:, cols])
    gnormed = gnormed.astype(BF16).astype(F32)
    gain_grad_ref[...] = jnp.sum(gnormed * hat_mlp, axis=0, keepdims=True)
    ghid_ref[...] = g32 + norm_backward(gnormed, gains_ref[1:2, :], hat_mlp, inv_mlp)


def first_attention_back(
    ghid_ref, g_ref, gpre_ref, mlp_gain_ref, hat_ref, inv_ref, normed_ref, normed_mlp_ref, q_ref, k_ref, v_ref, probs_ref, ctx_ref, expanded_ref,
    gains_ref, qkv_ref, out_ref, last_gain_ref,
    gblock_ref, grad_ref, mine_ref, theirs_ref,
    gctx_ref, dq_ref, dk_ref, dv_ref, wbuf_ref, sems,
):
    masks = head_rows()
    gblock, gbranch, gain_grad = attention_backward_part(
        hat_ref[...], inv_ref[...], gains_ref[0:1, :], qkv_ref, out_ref, ghid_ref[...],
        q_ref, k_ref, v_ref, probs_ref, ctx_ref, gctx_ref, dq_ref, dk_ref, dv_ref, grad_ref, masks,
    )
    gblock_ref[...] = gblock.astype(BF16)
    weight_grads(
        wbuf_ref, normed_ref[...], dq_ref[...], dk_ref[...], dv_ref[...], ctx_ref[...], gbranch,
        normed_mlp_ref[...], gpre_ref, expanded_ref, g_ref[...],
    )
    gains = jnp.concatenate([gain_grad, mlp_gain_ref[...], last_gain_ref[0:1, :], last_gain_ref[1:2, :]], axis=1)
    for h in range(2):
        wbuf_ref[h, PART:, :] = jnp.zeros((EXTRA, 128), BF16)
    for j in range(6):
        tile = jnp.concatenate([gains[:, j * 128 : (j + 1) * 128], jnp.zeros((15, 128), F32)], axis=0)
        wbuf_ref[0, PART + j * 16 : PART + (j + 1) * 16, :] = tile.astype(BF16)
    split_halves(wbuf_ref, mine_ref, theirs_ref, sems)


def first_finish(gblock_ref, grad_ref, last_table_ref, trows_ref, tcols_ref, pick_ref, gin_ref, tables_ref):
    tables_ref[0:TROWS, :] = collapse_table(grad_ref, trows_ref, tcols_ref)
    tables_ref[TROWS : 2 * TROWS, :] = last_table_ref[...]
    gin_ref[...] = scatter_tokens(pick_ref[...], gblock_ref[...].astype(F32)).astype(BF16)


def pack(first_ref, first_other_ref, last_ref, last_other_ref, packed_ref):
    first = (first_ref[...].astype(F32) + first_other_ref[...].astype(F32)).astype(BF16)
    packed_ref[:PART, :] = first[:PART]
    packed_ref[PART : 2 * PART, :] = (last_ref[...].astype(F32) + last_other_ref[...].astype(F32)).astype(BF16)
    packed_ref[2 * PART :, :] = first[PART:]


def add_two(mine_ref, other_ref, total_ref):
    total_ref[...] = (mine_ref[...].astype(F32) + other_ref[...].astype(F32)).astype(BF16)


def sum_parts(parts_ref, total_ref):
    total = parts_ref[0].astype(F32)
    for j in range(1, 16):
        total += parts_ref[j].astype(F32)
    total_ref[...] = total.astype(BF16)


def sum_and_spread(*refs):
    total = refs[0][...].astype(F32)
    for ref in refs[1:-1]:
        total += ref[...].astype(F32)
    total = total.astype(BF16)
    for j in range(16):
        refs[-1][j] = total


def unpack(
    mine_ref, other_ref, t0_ref, t1_ref, t2_ref, t3_ref, qkv_ref, out_ref, up_ref, down_ref, gains_ref, table_ref, sum_ref
):
    block = pl.program_id(0)
    core = lax.rem(lax.axis_index("lat"), 2)

    def load(half, start, count):
        rows = pl.ds(pl.multiple_of(start, 16), count)
        return jnp.where(core == half, mine_ref[rows, :].astype(F32), other_ref[rows, :].astype(F32))

    for j in range(18):
        tile = load(j // 9, block * PART + j % 9 * DIM, DIM)
        if j < 6:
            up_ref[:, j * 128 : (j + 1) * 128] = tile
        elif j < 12:
            down_ref[:, (j - 6) * 128 : (j - 5) * 128] = tile
        elif j < 16:
            qkv_ref[:, (j - 12) * 128 : (j - 11) * 128] = tile
        elif j == 16:
            qkv_ref[:, 512:576] = tile[:, :64]
            out_ref[:, 0:64] = tile[:, 64:]
        else:
            out_ref[:, 64:192] = tile
    rows = pl.ds(pl.multiple_of(block * TROWS, 16), TROWS)
    total = t0_ref[rows, :].astype(F32)
    for ref in (t1_ref, t2_ref, t3_ref):
        total += ref[rows, :].astype(F32)
    sum_ref[...] = total
    for j in range(26):
        piece = sum_ref[j * 8 : j * 8 + HEADS, :]
        width = min(128, TABLE - j * 128)
        for h in range(HEADS):
            table_ref[h, :, j * 128 : j * 128 + width] = piece[h : h + 1, :width]
    gains = jnp.concatenate([load(0, 2 * PART + (block * 3 + j) * 16, 16)[0:1] for j in range(3)], axis=1)
    for i in range(2):
        gains_ref[i : i + 1, :] = gains[:, i * DIM : (i + 1) * DIM]


def whole(array):
    return pl.BlockSpec(array.shape, lambda i: (0,) * array.ndim)


def picked(array, index):
    rest = array.shape[1:]
    return pl.BlockSpec((None,) + rest, lambda i: (index,) + (0,) * len(rest))


def in_place():
    return pl.BlockSpec(memory_space=pl.ANY)


def call(kernel, operands, specs, outs, scratch=(), micros=2, out_specs=None, mebibytes=10, steps=1):
    shapes = [jax.ShapeDtypeStruct(shape, dtype) for shape, dtype in outs]
    moved = sum(a.size * a.dtype.itemsize for a in (*operands, *shapes))
    return pl.pallas_call(
        kernel,
        grid=(steps,),
        out_shape=shapes,
        in_specs=specs,
        out_specs=out_specs or [whole(s) for s in shapes],
        scratch_shapes=list(scratch),
        cost_estimate=pl.CostEstimate(flops=micros * 1_100_000_000, bytes_accessed=moved, transcendentals=0),
        compiler_params=pltpu.CompilerParams(vmem_limit_bytes=mebibytes * 1024 * 1024),
    )(*operands)


def neighbour(sizes, steps):
    pairs = []
    for a in range(sizes[0]):
        for b in range(sizes[1]):
            source = ((a + steps[0]) % sizes[0]) * sizes[1] + (b + steps[1]) % sizes[1]
            pairs.append((source, a * sizes[1] + b))
    return pairs


def exchange(rows, side, corner, sizes, step):
    both = ("lat", "lon")
    rows = lax.ppermute(rows, both, neighbour(sizes, (step, 0)))
    side = lax.ppermute(side, both, neighbour(sizes, (0, step)))
    corner = lax.ppermute(corner, both, neighbour(sizes, (step, step)))
    return rows, side, corner


def vmem(shape, dtype):
    return pltpu.VMEM(shape, dtype)


def device_place(i):
    lat, lon = divmod(i, 8)
    return lat // 8, lat // 2 % 4, lat % 2, lon // 2, lon % 2


def flat_device(z_hi, y, core, x, z_lo):
    return ((z_hi * 4 + y) * 2 + core) * 8 + x * 2 + z_lo


def shifted_pairs(core=0, x=0, z_lo=0):
    pairs = []
    for i in range(128):
        h, y, c, a, b = device_place(i)
        pairs.append((flat_device(h, y, (c + core) % 2, (a + x) % 4, (b + z_lo) % 2), i))
    return pairs


def moved(array, **steps):
    return lax.ppermute(array, ("lat", "lon"), shifted_pairs(**steps))


def sum_over_devices(first, last, finish):
    both = ("lat", "lon")
    planes = {}
    for i in range(128):
        _, _, c, a, _ = device_place(i)
        planes.setdefault((c, a), []).append(i)
    groups = list(planes.values())

    def run(kernel, operands, shape):
        [result] = call(kernel, operands, [whole(a) for a in operands], [(shape, BF16)])
        return result

    sent = run(pack, [first[0], moved(first[1], core=1), *last], (HALF, 128))
    sent, finish = lax.optimization_barrier((sent, finish))
    parts = lax.all_to_all(sent.reshape(16, CHUNK, 128), both, 0, 0, axis_index_groups=groups)
    outs = [((GRID, 2 * DIM), BF16), ((2 * TROWS, 128), BF16)]
    grad_inputs, tables = call(first_finish, finish, [whole(a) for a in finish], outs)
    parts, tables = lax.optimization_barrier((parts, tables))
    total = run(sum_parts, [parts], (CHUNK, 128))
    spread = run(sum_and_spread, [total] + [moved(total, x=k) for k in (1, 2, 3)], (16, CHUNK, 128))
    tables = run(add_two, [tables, moved(tables, z_lo=1)], tables.shape)
    spread, tables = lax.optimization_barrier((spread, tables))
    half = lax.all_to_all(spread, both, 0, 0, axis_index_groups=groups)
    table_terms = [tables] + [moved(tables, x=k) for k in (1, 2, 3)]
    half, table_terms = lax.optimization_barrier((half, table_terms))
    half = half.reshape(HALF, 128)
    operands = [half, moved(half, core=1), *table_terms]
    outs = [((2, DIM, 3 * DIM), F32), ((2, DIM, DIM), F32), ((2, DIM, UNITS), F32), ((2, DIM, UNITS), F32)]
    outs += [((2, 2, DIM), F32), ((2 * HEADS, 1, TABLE), F32)]
    out_specs = [pl.BlockSpec((None,) + shape[1:], lambda b: (b, 0, 0)) for shape, _ in outs[:-1]]
    out_specs.append(pl.BlockSpec((HEADS, 1, TABLE), lambda b: (b, 0, 0)))
    grads = call(
        unpack, operands, [whole(a) for a in operands], outs, [vmem((TROWS, 128), F32)], 2, out_specs, steps=2
    )
    return grad_inputs, grads


def on_device(sizes, inputs, cotangent, norm_gains, qkv_weight, out_weight, up_weight, down_weight, bias_table):
    x = inputs.reshape(GRID, 2 * DIM)
    cot = cotangent.reshape(GRID, 2 * DIM)
    trows, tcols = jnp.asarray(table_rows(), BF16), jnp.asarray(table_cols(), BF16)
    pick_grid, pick_shift, pick_back = (
        jnp.asarray(m, BF16) for m in (grid_picker(), shifted_picker(), returned_picker())
    )
    strips = jnp.asarray(strip_picker(), BF16)
    weights = (norm_gains, qkv_weight, out_weight, up_weight, jnp.swapaxes(down_weight, 1, 2))
    tok, src, hid = (TOKENS, DIM), (SOURCE, 2 * DIM), (TOKENS, UNITS)
    probs = (WINDOWS, WIN_TOK, QLANES)

    def table_spec(index):
        return pl.BlockSpec((HEADS, 1, TABLE), lambda i: (index, 0, 0))

    bias_table = bias_table.reshape(2 * HEADS, 1, TABLE)
    gains, qkv, out, up, down = weights
    wide_tok, wide_hid = (tok, BF16), (hid, BF16)
    bias = (WIN_TOK, QLANES)

    def specs_for(arrays, index):
        specs = []
        for a in arrays:
            if any(a is w for w in weights):
                specs.append(picked(a, index))
            elif a is bias_table:
                specs.append(table_spec(index))
            else:
                specs.append(whole(a))
        return specs

    operands = [x, pick_grid, gains, qkv, bias_table, trows, tcols, out]
    outs = [wide_tok] * 4 + [(probs, BF16), wide_tok, (tok, F32)]
    scratch = [vmem(bias, F32), vmem(x.shape, BF16), vmem(pick_grid.shape, BF16), vmem((2, DIM), F32), vmem((DIM, 3 * DIM), BF16)]
    scratch += [vmem((HEADS, 1, TABLE), F32), vmem(trows.shape, BF16), vmem(tcols.shape, BF16), vmem((DIM, DIM), BF16)]
    scratch += [pltpu.SemaphoreType.DMA((8,))]
    operands = [pltpu.with_memory_space_constraint(a, pltpu.HBM) for a in operands]
    specs = [in_place()] * 8
    results = call(first_attention, operands, specs, outs, scratch, 7, mebibytes=14)
    xw, q, k, v, probs_first, ctx, hidden = results

    operands = [hidden, cot, gains, up, down, pick_grid, strips]
    strip_outs = [((288, 2 * DIM), BF16), ((2 * STRIP, 2 * DIM), BF16), ((2 * STRIP, 2 * DIM), BF16)]
    outs = [wide_hid, wide_hid, ((144, 2 * DIM), BF16)] + strip_outs
    results = call(first_mlp, operands, specs_for(operands, 0), outs, (), 4, mebibytes=14)
    expanded, slope, bottom, *sent = results
    sent, bias_table, xw = lax.optimization_barrier((sent, bias_table, xw))

    arrived = exchange(*sent, sizes, 1)
    operands = [bias_table, trows, tcols]
    [bias_last] = call(second_bias, operands, specs_for(operands, 1), [(bias, F32)], (), 2, mebibytes=14)

    operands = [xw, hidden, gains]
    norm_outs = [(tok, F32), ((TOKENS, 1), F32), wide_tok]
    norms = call(first_norms, operands, specs_for(operands, 0), norm_outs * 2, (), 1, mebibytes=14)
    hat, inv, normed_first, hat_mlp, inv_mlp, normed_mlp = norms

    operands = [bottom, *arrived, cot, bias_last, *weights, pick_shift]
    outs = [((144, 2 * DIM), BF16)] * 2 + strip_outs + [wide_tok] * 8 + [wide_hid] * 2 + [(bias, F32), ((2, DIM), F32)]
    scratch = [vmem(src, BF16), vmem(tok, F32), vmem(tok, F32)] + [vmem(tok, BF16)] * 3 + [vmem(probs, BF16), vmem(tok, BF16)]
    results = call(second_both, operands, specs_for(operands, 1), outs, scratch, 12, mebibytes=14)
    back_own, y_own, sent, terms, last_gain = results[0], results[1], results[2:5], results[5:16], results[16]

    arrived = exchange(*sent, sizes, -1)
    g, *terms = terms
    operands = [*terms, g, trows, tcols]
    outs = [((PART, 128), BF16)] * 2 + [((TROWS, 128), BF16)]
    out_specs = [in_place()] * 2 + [whole(jax.ShapeDtypeStruct(*o)) for o in outs[2:]]
    scratch = [vmem((2, PART, 128), BF16), pltpu.SemaphoreType.DMA((2,))]
    results = call(second_weights, operands, specs_for(operands, 1), outs, scratch, 4, out_specs, 14)
    last_mine, last_theirs, last_table = results

    operands = [back_own, *arrived, hat_mlp, inv_mlp, slope, gains, up, down, pick_back]
    outs = [wide_tok, (tok, F32), wide_hid, ((1, DIM), F32)]
    results = call(first_mlp_back, operands, specs_for(operands, 0), outs, [vmem(src, BF16)], 3, mebibytes=14)
    g, ghid, gpre, mlp_gain = results

    operands = [ghid, g, gpre, mlp_gain, hat, inv, normed_first, normed_mlp, q, k, v, probs_first, ctx, expanded, gains, qkv, out]
    operands += [last_gain]
    first_shape = (PART + EXTRA, 128)
    outs = [wide_tok, (bias, F32), (first_shape, BF16), (first_shape, BF16)]
    out_specs = [whole(jax.ShapeDtypeStruct(*o)) for o in outs[:2]] + [in_place()] * 2
    scratch = [vmem(tok, BF16)] * 4 + [vmem((2, *first_shape), BF16), pltpu.SemaphoreType.DMA((2,))]
    gblock, grad_scores, *first = call(
        first_attention_back, operands, specs_for(operands, 0), outs, scratch, 8, out_specs, 14
    )
    last_theirs, first = lax.optimization_barrier((last_theirs, first))
    last = [last_mine, moved(last_theirs, core=1)]
    finish = [gblock, grad_scores, last_table, trows, tcols, pick_grid]
    grad_inputs, grads = sum_over_devices(first, last, finish)
    y_rows, y_side, y_corner = arrived
    rows = jnp.concatenate([y_rows[144:], y_own]).reshape(ROWS, COLS, 2 * DIM)
    edge = jnp.concatenate([a[STRIP : STRIP + 18].reshape(3, 6, 2 * DIM) for a in (y_corner, y_side)])
    output = jnp.concatenate([edge, rows[:, 6:]], axis=1)

    grad_qkv, grad_out, grad_up, grad_down, grad_gains, grad_table = grads
    grad_down = jnp.swapaxes(grad_down, 1, 2)
    grad_table = grad_table.reshape(2, 1, HEADS, TABLE)
    return (output, grad_inputs.reshape(ROWS, COLS, 2 * DIM), grad_gains, grad_qkv, grad_out, grad_up, grad_down, grad_table)


def solution(mesh):
    sizes = (mesh.shape["lat"], mesh.shape["lon"])

    def program(*arguments):
        return on_device(sizes, *arguments)

    fields, tables = P("lat", "lon", None), P(None, "lat", None, None)
    return jax.shard_map(
        program,
        mesh=mesh,
        in_specs=(fields, fields, P(), P(), P(), P(), P(), tables),
        out_specs=(fields, fields, P(), P(), P(), P(), P(), tables),
        check_vma=False,
    )
```
